128 devices in a mesh: sx: 8 (over y, z_hi), sy: 16 (over z_lo, x, core).
Axes of the slice: x: 4, y: 4, z: 4 (z_hi: 2, z_lo: 2; z = z_hi * 2 + z_lo), core: 2. Of those that a mesh axis runs over, the one named last changes fastest.
Arguments:
- tokens: bfloat16 [16384, 5120], P(('sx', 'sy')), may hold values from -5 to 5
- mod_shift: float32 [5120], replicated, may hold values from -3 to 3
- mod_scale: float32 [5120], replicated, may hold values from -2.5 to 2.5
- w_query: bfloat16 [5120, 4096], P(None, 'sy'), may hold values from -2.5 to 2.5
- w_key: bfloat16 [5120, 4096], P(None, 'sy'), may hold values from -2.5 to 2.5
- w_value: bfloat16 [5120, 4096], P(None, 'sy'), may hold values from -0.078125 to 0.078125
- query_gain: float32 [4096], replicated, may hold values from 0.1 to 1.9
- key_gain: float32 [4096], replicated, may hold values from 0.1 to 1.9
Outputs:
- attended: bfloat16 [16384, 4096], P(('sx', 'sy'))
- row_max: float32 [32, 16384], P(None, ('sx', 'sy'))
- row_sum: float32 [32, 16384], P(None, ('sx', 'sy'))
The draws below stay inside these ranges and needn't reach their ends.
All inputs are finite; a program needn't handle non-finite values.
Results may differ from the reference program's by a relative error of at most 0.0061.
Values may be sent and summed in bfloat16 or wider, within the bound.
No kernel may reach another device: no remote copies, remote signals or barrier semaphores. Data moves between devices by JAX's collectives and lax.ppermute only.
A program may use at most 128 MiB of HBM per device.

```python
import jax
import jax.numpy as jnp
from jax import lax

D = 5120
H = 32
HD = 128
ROUNDS = 4
GRID_W = 80
GRID_H = 45
TOK_DEV = 128
TOKENS = 16384
HH = 4096


def column_heads():
    return jnp.arange(H * HD, dtype=jnp.int32) // HD


def rising_scale(head_of):
    return 3.0 ** (0.5 * head_of.astype(jnp.float32) / (H - 1))


def draw_tokens(key, part):
    key = jax.random.fold_in(key, 3)
    base_key = jax.random.fold_in(key, 0)
    base = jnp.clip(jax.random.normal(base_key, (TOKENS, D), jnp.float32), -5.0, 5.0)
    return base.astype(jnp.bfloat16)


def draw_w_query(key, part):
    key = jax.random.fold_in(key, 1)
    own = jnp.clip(jax.random.normal(key, (D, H * HD), jnp.float32), -4.0, 4.0)
    head_of = column_heads()
    factor = rising_scale(head_of)
    return (own * factor[None, :] / 64.0).astype(jnp.bfloat16)


def draw_w_key(key, part):
    key = jax.random.fold_in(key, 2)
    own = jnp.clip(jax.random.normal(key, (D, H * HD), jnp.float32), -4.0, 4.0)
    head_of = column_heads()
    factor = rising_scale(head_of)
    return (own * factor[None, :] / 64.0).astype(jnp.bfloat16)


def levels(key, extent, cuts, low, largest):
    level = 1.0
    for axis_at, shards_of in cuts:
        draws = jax.random.uniform(jax.random.fold_in(jax.random.fold_in(key, 6), axis_at), (shards_of,), jnp.float32, low / len(cuts), largest / len(cuts))
        level = level * jnp.repeat(jnp.exp(draws), extent[axis_at] // shards_of).reshape((-1,) + (1,) * (len(extent) - 1 - axis_at))
    return level


def centred(own_key, extent, scale, bound, cuts=(), held_as=jnp.bfloat16):
    result = scale * jax.random.normal(own_key, extent, jnp.float32)
    if cuts:
        result = result * levels(own_key, extent, cuts, -0.22, 0.18)
    return jnp.clip(result, -bound, bound).astype(held_as)


def setup_inputs(seed: int = 0) -> dict:
    splits = jax.random.split(jax.random.key(seed), 9)
    return {
        "tokens": draw_tokens(jax.random.fold_in(splits[8], 71), 0),
        "mod_shift": centred(splits[1], (D,), 0.5, 3.0, (), jnp.float32),
        "mod_scale": centred(splits[2], (D,), 0.3, 2.5, (), jnp.float32),
        "w_query": draw_w_query(jax.random.fold_in(splits[8], 71), 0),
        "w_key": draw_w_key(jax.random.fold_in(splits[8], 71), 0),
        "w_value": centred(splits[5], (D, HH), D ** -0.5, 0.078125, ((1, 16),)),
        "query_gain": jnp.clip(1.0 + 0.18 * jax.random.normal(splits[6], (HH,), jnp.float32), 0.1, 1.9),
        "key_gain": jnp.clip(1.0 + 0.18 * jax.random.normal(splits[7], (HH,), jnp.float32), 0.1, 1.9),
    }


def layer_norm(values, mod_shift, mod_scale):
    wide = values.astype(jnp.float32)
    center = lax.optimization_barrier(jnp.mean(wide, axis=-1, keepdims=True))
    spread = lax.optimization_barrier(jnp.mean((wide - center) ** 2, axis=-1, keepdims=True))
    scaled = (wide - center) * lax.rsqrt(spread + 1e-06)
    return (scaled * (1.0 + mod_scale) + mod_shift).astype(jnp.bfloat16)

def rope_angles(positions, head_size):
    small_pairs = head_size // 6
    time_pairs = (head_size - 4 * small_pairs) // 2
    frame = (positions // (GRID_H * GRID_W)).astype(jnp.float32)
    row_pos = (positions // GRID_W % GRID_H).astype(jnp.float32)
    col_pos = (positions % GRID_W).astype(jnp.float32)
    time_freq = 10000.0 ** (-jnp.arange(time_pairs, dtype=jnp.float32) / time_pairs)
    space_freq = 10000.0 ** (-jnp.arange(small_pairs, dtype=jnp.float32) / small_pairs)
    angles = jnp.concatenate([frame[:, None] * time_freq[None, :], row_pos[:, None] * space_freq[None, :], col_pos[:, None] * space_freq[None, :]], axis=1)
    return jnp.repeat(angles, 2, axis=1)

def norm_rope(raw, gain, positions, heads, head_size):
    wide = raw.astype(jnp.float32)
    wide = wide * lax.rsqrt(lax.optimization_barrier(jnp.mean(wide * wide, axis=-1, keepdims=True)) + 1e-06) * gain
    wide = wide.reshape(wide.shape[0], heads, head_size)
    angles = rope_angles(positions, head_size)[:, None, :]
    cosine = jnp.cos(angles)
    sine = jnp.sin(angles)
    channel = jnp.arange(head_size, dtype=jnp.int32)
    is_even = (channel % 2 == 0)[None, None, :]
    partner = jnp.where(is_even, -jnp.roll(wide, -1, axis=-1), jnp.roll(wide, 1, axis=-1))
    return (wide * cosine + partner * sine).astype(jnp.bfloat16)

def window_half(q_blocks, k_blocks, v_blocks, sign, head_size):
    scale = 1.0 / jnp.sqrt(jnp.float32(head_size))
    q_wide = q_blocks.astype(jnp.float32)
    best = None
    for offset in range(ROUNDS + 1):
        k_near = jnp.roll(k_blocks, sign * offset, axis=0).astype(jnp.float32)
        v_near = jnp.roll(v_blocks, sign * offset, axis=0).astype(jnp.float32)
        scores = jnp.einsum('nqhd,nkhd->nhqk', q_wide, k_near) * scale
        block_max = lax.optimization_barrier(jnp.max(scores, axis=-1))
        weights = jnp.exp(scores - block_max[..., None])
        block_sum = lax.optimization_barrier(jnp.sum(weights, axis=-1))
        rounded = lax.optimization_barrier(weights.astype(jnp.bfloat16))
        block_out = jnp.einsum('nhqk,nkhd->nqhd', rounded.astype(jnp.float32), v_near)
        if best is None:
            best, total, numer = (block_max, block_sum, block_out)
        else:
            newer = jnp.maximum(best, block_max)
            old_fac = jnp.exp(best - newer)
            new_fac = jnp.exp(block_max - newer)
            total = total * old_fac + block_sum * new_fac
            numer = numer * jnp.transpose(old_fac, (0, 2, 1))[..., None] + block_out * jnp.transpose(new_fac, (0, 2, 1))[..., None]
            best = newer
    return (best, total, numer)

def reference(tokens, mod_shift, mod_scale, w_query, w_key, w_value, query_gain, key_gain):
    heads = H
    head_size = HD
    count = TOKENS // TOK_DEV
    normed = layer_norm(tokens, mod_shift, mod_scale)
    q_raw = jnp.dot(normed, w_query, preferred_element_type=jnp.float32).astype(jnp.bfloat16)
    k_raw = jnp.dot(normed, w_key, preferred_element_type=jnp.float32).astype(jnp.bfloat16)
    v_all = jnp.dot(normed, w_value, preferred_element_type=jnp.float32).astype(jnp.bfloat16)
    positions = jnp.arange(TOKENS, dtype=jnp.int32)
    q_all = norm_rope(q_raw, query_gain, positions, heads, head_size)
    k_all = norm_rope(k_raw, key_gain, positions, heads, head_size)
    q_blocks = q_all.reshape(count, TOK_DEV, heads, head_size)
    k_blocks = k_all.reshape(count, TOK_DEV, heads, head_size)
    v_blocks = v_all.reshape(count, TOK_DEV, heads, head_size)
    best_even, total_even, numer_even = window_half(q_blocks[:, :, 0::2], k_blocks[:, :, 0::2], v_blocks[:, :, 0::2], 1, head_size)
    best_odd, total_odd, numer_odd = window_half(q_blocks[:, :, 1::2], k_blocks[:, :, 1::2], v_blocks[:, :, 1::2], -1, head_size)
    best = jnp.stack([best_even, best_odd], axis=2).reshape(count, heads, TOK_DEV)
    total = jnp.stack([total_even, total_odd], axis=2).reshape(count, heads, TOK_DEV)
    numer = jnp.stack([numer_even, numer_odd], axis=3).reshape(count, TOK_DEV, heads, head_size)
    attended = numer / jnp.transpose(total, (0, 2, 1))[..., None]
    attended = attended.reshape(TOKENS, heads * head_size).astype(jnp.bfloat16)
    row_max = jnp.transpose(best, (1, 0, 2)).reshape(heads, TOKENS)
    row_sum = jnp.transpose(total, (1, 0, 2)).reshape(heads, TOKENS)
    return (attended, row_max, row_sum)
```

```python
import jax
import jax.numpy as jnp
import numpy as np
from jax import lax
from jax.experimental import pallas as pl
from jax.experimental.pallas import tpu as pltpu
from jax.sharding import PartitionSpec as P

H = 32
HD = 128
ROUNDS = 4
GRID_W = 80
GRID_H = 45
BLK = 128
HALO = ROUNDS * BLK
EXTRA = 16
NSY = 16
SCALE = np.float32(1.0) / np.sqrt(np.float32(HD))
LOG2E = np.float32(1.4426950408889634)


def layer_norm(values, mod_shift, mod_scale):
    wide = values.astype(jnp.float32)
    center = jnp.mean(wide, axis=-1, keepdims=True)
    spread = jnp.mean((wide - center) ** 2, axis=-1, keepdims=True)
    scaled = (wide - center) * lax.rsqrt(spread + 1e-06)
    return (scaled * (1.0 + mod_scale) + mod_shift).astype(jnp.bfloat16)


def rope_tables(positions):
    small_pairs = HD // 6
    time_pairs = (HD - 4 * small_pairs) // 2
    frame = (positions // (GRID_H * GRID_W)).astype(jnp.float32)
    row_pos = (positions // GRID_W % GRID_H).astype(jnp.float32)
    col_pos = (positions % GRID_W).astype(jnp.float32)
    time_freq = 10000.0 ** (-jnp.arange(time_pairs, dtype=jnp.float32) / time_pairs)
    space_freq = 10000.0 ** (-jnp.arange(small_pairs, dtype=jnp.float32) / small_pairs)
    freq = jnp.repeat(jnp.concatenate([time_freq, space_freq, space_freq]), 2)
    pair = jnp.arange(HD, dtype=jnp.int32) // 2
    where = jnp.where(
        pair < time_pairs,
        frame[:, None],
        jnp.where(pair < time_pairs + small_pairs, row_pos[:, None], col_pos[:, None]),
    )
    angles = where * freq
    sign = jnp.where(jnp.arange(HD) % 2 == 0, -1.0, 1.0).astype(jnp.float32)
    return jnp.cos(angles), jnp.sin(angles) * sign


def as_column(row):
    return jnp.broadcast_to(row, (BLK, BLK)).T


def as_row(column):
    return jnp.broadcast_to(column, (BLK, BLK)).T[0:1, :]


def norm_rope(raw, ssq_row, gain, cosine, sine):
    inv = lax.rsqrt(as_column(ssq_row) * (1.0 / (H * HD)) + 1e-06)
    wide = raw.astype(jnp.float32) * inv * gain
    lane = lax.broadcasted_iota(jnp.int32, wide.shape, 1)
    partner = jnp.where(
        lane % 2 == 0, pltpu.roll(wide, HD - 1, 1), pltpu.roll(wide, 1, 1)
    )
    return (wide * cosine + partner * sine).astype(jnp.bfloat16)


def split3(row):
    hi = row.astype(jnp.bfloat16).astype(jnp.float32)
    rest = row - hi
    mid = rest.astype(jnp.bfloat16).astype(jnp.float32)
    return [hi, mid, rest - mid]


PER_STEP = 2


def attention_kernel(
    q_ref, k_ref, v_ref, before_ref, after_ref, sq_ref, sk_ref, sb_ref, sa_ref,
    gq_ref, gk_ref, cos_ref, sin_ref, out_ref, kbuf, vbuf,
):
    step = pl.program_id(0)
    blocks = k_ref.shape[0] // BLK

    @pl.when(step == 0)
    def _():
        def put(head, dest, raw, values, ssq, table):
            rows = pl.ds(pl.multiple_of(table, BLK), BLK)
            to = pl.ds(pl.multiple_of(dest, BLK), BLK)
            kbuf[head, to, :] = norm_rope(
                raw, ssq, gk_ref[:, head * HD : (head + 1) * HD], cos_ref[rows, :], sin_ref[rows, :]
            )
            vbuf[head, to, :] = values

        for i in range(ROUNDS):
            r = pl.ds(i * BLK, BLK)
            put(0, i * BLK, before_ref[r, 0:HD], before_ref[r, HD:], sb_ref[pl.ds(i, 1), :], i * BLK)
            put(
                1, (blocks + i) * BLK, after_ref[r, 0:HD], after_ref[r, HD:], sa_ref[pl.ds(i, 1), :],
                (blocks + ROUNDS + i) * BLK,
            )

        def own(i, carry):
            r = pl.ds(pl.multiple_of(i * BLK, BLK), BLK)
            ssq = sk_ref[pl.ds(i, 1), :]
            table = (i + ROUNDS) * BLK
            put(0, (i + ROUNDS) * BLK, k_ref[r, 0:HD], v_ref[r, 0:HD], ssq, table)
            put(1, i * BLK, k_ref[r, HD:], v_ref[r, HD:], ssq, table)
            return carry

        lax.fori_loop(0, blocks, own, 0, unroll=2)

    for j in range(PER_STEP):
        b = step * PER_STEP + j
        table = pl.ds(pl.multiple_of((b + ROUNDS) * BLK, BLK), BLK)
        window = pl.ds(pl.multiple_of(b * BLK, BLK), (ROUNDS + 1) * BLK)
        stats = []
        for head in range(2):
            cols = slice(head * HD, (head + 1) * HD)
            q = norm_rope(
                q_ref[j * BLK : (j + 1) * BLK, cols], sq_ref[pl.ds(b, 1), :], gq_ref[:, cols],
                cos_ref[table, :], sin_ref[table, :],
            )
            raw = lax.dot_general(
                q, kbuf[head, window, :], (((1,), (1,)), ((), ())), preferred_element_type=jnp.float32
            )
            top = jnp.max(raw, axis=-1, keepdims=True)
            weights = jnp.exp2((raw - top) * (SCALE * LOG2E))
            total = jnp.sum(weights, axis=-1, keepdims=True)
            mixed = jnp.dot(
                weights.astype(jnp.bfloat16), vbuf[head, window, :], preferred_element_type=jnp.float32
            )
            out_ref[j, 0:BLK, cols] = (mixed / total).astype(jnp.bfloat16)
            stats.append(split3(as_row(top * SCALE)) + split3(as_row(total)))
        pad = jnp.zeros((EXTRA - 6, HD), jnp.float32)
        for head in range(2):
            cols = slice(head * HD, (head + 1) * HD)
            out_ref[j, BLK : BLK + EXTRA, cols] = jnp.concatenate(stats[head] + [pad], axis=0).astype(
                jnp.bfloat16
            )


def attention(q, k, v, before, after, sq, sk, sb, sa, gq, gk, cosine, sine):
    rows = q.shape[0]
    blocks = rows // BLK
    whole = lambda a: pl.BlockSpec(a.shape, lambda i, n=a.ndim: (0,) * n)
    return pl.pallas_call(
        attention_kernel,
        grid=(blocks // PER_STEP,),
        in_specs=[pl.BlockSpec((PER_STEP * BLK, 2 * HD), lambda i: (i, 0))]
        + [whole(a) for a in (k, v, before, after, sq, sk, sb, sa, gq, gk, cosine, sine)],
        out_specs=pl.BlockSpec((PER_STEP, BLK + EXTRA, 2 * HD), lambda i: (i, 0, 0)),
        out_shape=jax.ShapeDtypeStruct((blocks, BLK + EXTRA, 2 * HD), jnp.bfloat16),
        scratch_shapes=[
            pltpu.VMEM((2, rows + HALO, HD), jnp.bfloat16),
            pltpu.VMEM((2, rows + HALO, HD), jnp.bfloat16),
        ],
        compiler_params=pltpu.CompilerParams(
            dimension_semantics=("arbitrary",), vmem_limit_bytes=40 * 1024 * 1024
        ),
        cost_estimate=pl.CostEstimate(flops=2 * 10**9, bytes_accessed=10**7, transcendentals=3 * 10**6),
        name="window_attention",
    )(q, k, v, before, after, sq, sk, sb, sa, gq, gk, cosine, sine)


def square_sum(raw):
    wide = raw.astype(jnp.float32)
    return jnp.sum(wide * wide, axis=-1).reshape(-1, BLK)


def along_sx(block, distance):
    n = lax.axis_size("sx")
    return lax.ppermute(block, "sx", [((i - distance) % n, i) for i in range(n)])


def unpack(arrived):
    attended = arrived[:, :BLK].transpose(1, 0, 2).reshape(BLK, H * HD)
    stats = arrived[:, BLK : BLK + 6].astype(jnp.float32)
    best = (stats[:, 0] + stats[:, 1]) + stats[:, 2]
    total = (stats[:, 3] + stats[:, 4]) + stats[:, 5]
    return attended, best.reshape(H, BLK), total.reshape(H, BLK)


def body(tokens, mod_shift, mod_scale, w_query, w_key, w_value, query_gain, key_gain):
    group = lax.axis_index("sx")
    mine = lax.axis_index("sy")
    normed = layer_norm(tokens, mod_shift, mod_scale)
    piece = lax.all_gather(normed, "sy", axis=0, tiled=True)
    rows = piece.shape[0]
    count = rows * lax.axis_size("sx")
    positions = (group * rows - HALO + jnp.arange(rows + 2 * HALO, dtype=jnp.int32) + count) % count
    cosine, sine = rope_tables(positions)
    gq = lax.dynamic_slice(query_gain, (mine * 2 * HD,), (2 * HD,)).reshape(1, 2 * HD)
    gk = lax.dynamic_slice(key_gain, (mine * 2 * HD,), (2 * HD,)).reshape(1, 2 * HD)
    q, k, v = [
        jnp.dot(piece, weight, preferred_element_type=jnp.float32).astype(jnp.bfloat16)
        for weight in (w_query, w_key, w_value)
    ]
    partial = jnp.stack([square_sum(q), square_sum(k)])
    ssq = jnp.sum(lax.all_gather(partial, "sy", axis=0), axis=0)
    before = along_sx(jnp.concatenate([k[-HALO:, :HD], v[-HALO:, :HD]], axis=1), 1)
    after = along_sx(jnp.concatenate([k[:HALO, HD:], v[:HALO, HD:]], axis=1), -1)
    sb = along_sx(ssq[1, -ROUNDS:], 1)
    sa = along_sx(ssq[1, :ROUNDS], -1)
    out = attention(q, k, v, before, after, ssq[0], ssq[1], sb, sa, gq, gk, cosine, sine)
    arrived = lax.all_to_all(out, "sy", split_axis=0, concat_axis=0, tiled=True)
    return unpack(arrived)


def solution(mesh):
    placed = (
        P(("sx", "sy"), None),
        P(),
        P(),
        P(None, "sy"),
        P(None, "sy"),
        P(None, "sy"),
        P(),
        P(),
    )
    return jax.shard_map(
        body,
        mesh=mesh,
        in_specs=placed,
        out_specs=(P(("sx", "sy"), None), P(None, ("sx", "sy")), P(None, ("sx", "sy"))),
        check_vma=False,
    )
```

```python
import jax
import jax.numpy as jnp
import numpy as np
from jax import lax
from jax.experimental import pallas as pl
from jax.experimental.pallas import tpu as pltpu
from jax.sharding import PartitionSpec as P

H = 32
HD = 128
ROUNDS = 4
GRID_W = 80
GRID_H = 45
BLK = 128
HALO = ROUNDS * BLK
EXTRA = 16
NSY = 16
SCALE = np.float32(1.0) / np.sqrt(np.float32(HD))
LOG2E = np.float32(1.4426950408889634)


def layer_norm(values, mod_shift, mod_scale):
    wide = values.astype(jnp.float32)
    center = jnp.mean(wide, axis=-1, keepdims=True)
    spread = jnp.mean((wide - center) ** 2, axis=-1, keepdims=True)
    scaled = (wide - center) * lax.rsqrt(spread + 1e-06)
    return (scaled * (1.0 + mod_scale) + mod_shift).astype(jnp.bfloat16)


def rope_tables(positions):
    small_pairs = HD // 6
    time_pairs = (HD - 4 * small_pairs) // 2
    frame = (positions // (GRID_H * GRID_W)).astype(jnp.float32)
    row_pos = (positions // GRID_W % GRID_H).astype(jnp.float32)
    col_pos = (positions % GRID_W).astype(jnp.float32)
    time_freq = 10000.0 ** (-jnp.arange(time_pairs, dtype=jnp.float32) / time_pairs)
    space_freq = 10000.0 ** (-jnp.arange(small_pairs, dtype=jnp.float32) / small_pairs)
    freq = jnp.repeat(jnp.concatenate([time_freq, space_freq, space_freq]), 2)
    pair = jnp.arange(HD, dtype=jnp.int32) // 2
    where = jnp.where(
        pair < time_pairs,
        frame[:, None],
        jnp.where(pair < time_pairs + small_pairs, row_pos[:, None], col_pos[:, None]),
    )
    angles = where * freq
    sign = jnp.where(jnp.arange(HD) % 2 == 0, -1.0, 1.0).astype(jnp.float32)
    return jnp.cos(angles), jnp.sin(angles) * sign


def as_column(row):
    return jnp.broadcast_to(row, (BLK, BLK)).T


def as_row(column):
    return jnp.broadcast_to(column, (BLK, BLK)).T[0:1, :]


def norm_rope(raw, ssq_row, gain, cosine, sine):
    inv = lax.rsqrt(as_column(ssq_row) * (1.0 / (H * HD)) + 1e-06)
    wide = raw.astype(jnp.float32) * inv * gain
    lane = lax.broadcasted_iota(jnp.int32, wide.shape, 1)
    partner = jnp.where(
        lane % 2 == 0, pltpu.roll(wide, HD - 1, 1), pltpu.roll(wide, 1, 1)
    )
    return (wide * cosine + partner * sine).astype(jnp.bfloat16)


def split3(row):
    hi = row.astype(jnp.bfloat16).astype(jnp.float32)
    rest = row - hi
    mid = rest.astype(jnp.bfloat16).astype(jnp.float32)
    return [hi, mid, rest - mid]


PER_STEP = 2
SLOTS = ((0, 0), (0, -1), (0, 1), (1, 0), (0, 2), (1, -1), (1, 1), (1, 2))
CHUNKS = (4, 3, 1)


def chip_move(dz, dx, dc):
    return [
        (z * 8 + x * 2 + c, (z + dz) % 2 * 8 + (x + dx) % 4 * 2 + (c + dc) % 2)
        for z in range(2)
        for x in range(4)
        for c in range(2)
    ]


def from_left(block):
    return lax.ppermute(block, "sy", chip_move(0, 1, 0))


def from_right(block):
    return lax.ppermute(block, "sy", chip_move(0, -1, 0))


def from_z(block):
    return lax.ppermute(block, "sy", chip_move(1, 0, 0))


def from_core(block):
    return lax.ppermute(block, "sy", chip_move(0, 0, 1))


def project_kernel(*refs):
    n = len(refs) - 7
    pieces, (own_w, other_w, own_ref, other_ref, ssq_ref, x_ref, sems) = refs[:n], refs[n:]

    @pl.when(pl.program_id(0) == 0)
    def _():
        copies, at = [], 0
        for i, piece in enumerate(pieces):
            rows = piece.shape[0]
            copies.append(pltpu.make_async_copy(piece, x_ref.at[pl.ds(at, rows)], sems.at[i]))
            copies[-1].start()
            at += rows
        for copy in copies:
            copy.wait()

    total = None
    for weight, out in ((own_w, own_ref), (other_w, other_ref)):
        made = jnp.dot(x_ref[...], weight[0], preferred_element_type=jnp.float32).astype(jnp.bfloat16)
        out[0] = made
        wide = made.astype(jnp.float32)
        part = jnp.sum(wide * wide, axis=-1, keepdims=True)
        total = part if total is None else total + part
    for i in range(x_ref.shape[0] // BLK):
        ssq_ref[0, i : i + 1, :] = as_row(total[i * BLK : (i + 1) * BLK])


def project(pieces, own_w, other_w):
    rows = sum(p.shape[0] for p in pieces)
    depth, wide = own_w.shape[1:]
    w_spec = pl.BlockSpec((1, depth, wide), lambda i: (i, 0, 0))
    o_spec = pl.BlockSpec((1, rows, wide), lambda i: (i, 0, 0))
    out = jax.ShapeDtypeStruct((3, rows, wide), jnp.bfloat16)
    return pl.pallas_call(
        project_kernel,
        grid=(3,),
        in_specs=[pl.BlockSpec(memory_space=pl.ANY)] * len(pieces) + [w_spec, w_spec],
        out_specs=[o_spec, o_spec, pl.BlockSpec((1, rows // BLK, BLK), lambda i: (i, 0, 0))],
        out_shape=[out, out, jax.ShapeDtypeStruct((3, rows // BLK, BLK), jnp.float32)],
        scratch_shapes=[pltpu.VMEM((rows, depth), jnp.bfloat16), pltpu.SemaphoreType.DMA((len(pieces),))],
        compiler_params=pltpu.CompilerParams(
            dimension_semantics=("arbitrary",), vmem_limit_bytes=48 * 1024 * 1024
        ),
        cost_estimate=pl.CostEstimate(
            flops=12 * rows * depth * wide, bytes_accessed=12 * depth * wide, transcendentals=0
        ),
        name="project",
    )(*pieces, own_w, other_w)


def sources(refs):
    at = 0
    for chunk, slots in enumerate(CHUNKS):
        for i in range(slots):
            for core in range(2):
                yield (at + i) * 2 + core, refs[chunk * 2 + core], pl.ds(i * BLK, BLK)
        at += slots


def halo_kernel(
    place_ref, fa, ga, fb, gb, fc, gc, ssq_ref, gk_ref, cos_lo, sin_lo, cos_hi, sin_hi,
    before_ref, after_ref, raw, sems,
):
    blocks = 2 * sum(CHUNKS)
    ends = ((lambda n: n >= blocks - ROUNDS, blocks - ROUNDS, 0), (lambda n: n < ROUNDS, 0, 1))

    def each(act):
        for at, ref, rows in sources((fa, ga, fb, gb, fc, gc)):
            n = place_ref[at]
            for inside, first, head in ends:

                @pl.when(inside(n))
                def _(n=n, first=first, head=head, ref=ref, rows=rows, at=at):
                    to = pl.ds(pl.multiple_of((n - first) * BLK, BLK), BLK)
                    cols = pl.ds(head * HD, HD)
                    out = (before_ref, after_ref)[head]
                    act(pltpu.make_async_copy(ref.at[0, rows, cols], raw.at[head, to], sems.at[at, 0]))
                    act(pltpu.make_async_copy(ref.at[2, rows, cols], out.at[to, pl.ds(HD, HD)], sems.at[at, 1]))

    each(lambda copy: copy.start())
    each(lambda copy: copy.wait())
    for head, out, first, cosine, sine in (
        (0, before_ref, blocks - ROUNDS, cos_hi, sin_hi),
        (1, after_ref, 0, cos_lo, sin_lo),
    ):
        for i in range(ROUNDS):
            rows = pl.ds(i * BLK, BLK)
            out[rows, 0:HD] = norm_rope(
                raw[head, rows, :], ssq_ref[pl.ds(first + i, 1), :], gk_ref[:, head * HD : (head + 1) * HD],
                cosine[rows, :], sine[rows, :],
            )


VMEM = pl.BlockSpec(memory_space=pltpu.VMEM)
SMEM = pl.BlockSpec(memory_space=pltpu.SMEM)
ANYWHERE = pl.BlockSpec(memory_space=pl.ANY)


def halo(place, features, ssq_k, gk, cosine, sine):
    rows = cosine.shape[0]
    low = pl.BlockSpec((HALO, HD), lambda i: (0, 0))
    high = pl.BlockSpec((HALO, HD), lambda i: (rows // HALO - 1, 0))
    one = lambda a: pl.BlockSpec(a.shape, lambda i: (0, 0))
    out = jax.ShapeDtypeStruct((HALO, 2 * HD), jnp.bfloat16)
    return pl.pallas_call(
        halo_kernel,
        grid=(1,),
        in_specs=[SMEM] + [ANYWHERE] * 6 + [one(ssq_k), one(gk), low, low, high, high],
        out_specs=[pl.BlockSpec((HALO, 2 * HD), lambda i: (0, 0))] * 2,
        out_shape=[out, out],
        scratch_shapes=[
            pltpu.VMEM((2, HALO, HD), jnp.bfloat16),
            pltpu.SemaphoreType.DMA((2 * sum(CHUNKS), 2)),
        ],
        compiler_params=pltpu.CompilerParams(vmem_limit_bytes=48 * 1024 * 1024),
        cost_estimate=pl.CostEstimate(flops=10**7, bytes_accessed=3 * 10**6, transcendentals=0),
        name="halo_keys",
    )(place, *features, ssq_k, gk, cosine, sine, cosine, sine)


def attention_kernel(
    place_ref, fa, ga, fb, gb, fc, gc, before_ref, after_ref, sk_ref, sq_ref,
    gk_ref, gq_ref, cos_ref, sin_ref, out_ref, raw, kbuf, vbuf, sems,
):
    step = pl.program_id(0)
    blocks = 2 * sum(CHUNKS)
    own_first = (ROUNDS, 0)
    halo_first = (0, blocks)
    columns = [slice(head * HD, (head + 1) * HD) for head in range(2)]

    @pl.when(step == 0)
    def _():
        copies = []
        for at, ref, rows in sources((fa, ga, fb, gb, fc, gc)):
            n = place_ref[at]
            to = pl.ds(pl.multiple_of(n * BLK, BLK), BLK)
            for i in range(2):
                copies.append(pltpu.make_async_copy(ref.at[i, rows], raw.at[i, to], sems.at[at, i]))
            for head in range(2):
                to = pl.ds(pl.multiple_of((n + own_first[head]) * BLK, BLK), BLK)
                copies.append(
                    pltpu.make_async_copy(
                        ref.at[2, rows, pl.ds(head * HD, HD)], vbuf.at[head, to], sems.at[at, 2 + head]
                    )
                )
        for copy in copies:
            copy.start()
        for head, ref in enumerate((before_ref, after_ref)):
            to = pl.ds(halo_first[head] * BLK, HALO)
            kbuf[head, to, :] = ref[:, 0:HD]
            vbuf[head, to, :] = ref[:, HD:]
        for copy in copies:
            copy.wait()

        def own(i, carry):
            rows = pl.ds(pl.multiple_of(i * BLK, BLK), BLK)
            for head in range(2):
                to = pl.ds(pl.multiple_of((i + own_first[head]) * BLK, BLK), BLK)
                kbuf[head, to, :] = norm_rope(
                    raw[0, rows, columns[head]], sk_ref[pl.ds(i, 1), :], gk_ref[:, columns[head]],
                    cos_ref[rows, :], sin_ref[rows, :],
                )
            return carry

        lax.fori_loop(0, blocks, own, 0, unroll=2)

    for j in range(PER_STEP):
        b = step * PER_STEP + j
        rows = pl.ds(pl.multiple_of(b * BLK, BLK), BLK)
        window = pl.ds(pl.multiple_of(b * BLK, BLK), (ROUNDS + 1) * BLK)
        stats = []
        for head in range(2):
            q = norm_rope(
                raw[1, rows, columns[head]], sq_ref[pl.ds(b, 1), :], gq_ref[:, columns[head]],
                cos_ref[rows, :], sin_ref[rows, :],
            )
            scores = lax.dot_general(
                q, kbuf[head, window, :], (((1,), (1,)), ((), ())), preferred_element_type=jnp.float32
            )
            top = jnp.max(scores, axis=-1, keepdims=True)
            weights = jnp.exp2((scores - top) * (SCALE * LOG2E))
            total = jnp.sum(weights, axis=-1, keepdims=True)
            mixed = jnp.dot(
                weights.astype(jnp.bfloat16), vbuf[head, window, :], preferred_element_type=jnp.float32
            )
            out_ref[j, 0:BLK, columns[head]] = (mixed / total).astype(jnp.bfloat16)
            stats.append(split3(as_row(top * SCALE)) + split3(as_row(total)))
        pad = jnp.zeros((EXTRA - 6, HD), jnp.float32)
        for head in range(2):
            out_ref[j, BLK : BLK + EXTRA, columns[head]] = jnp.concatenate(
                stats[head] + [pad], axis=0
            ).astype(jnp.bfloat16)


def attention(place, features, before, after, sk, sq, gk, gq, cosine, sine):
    rows = cosine.shape[0]
    blocks = rows // BLK
    whole = lambda a: pl.BlockSpec(a.shape, lambda i, n=a.ndim: (0,) * n)
    return pl.pallas_call(
        attention_kernel,
        grid=(blocks // PER_STEP,),
        in_specs=[SMEM] + [ANYWHERE] * 6 + [whole(a) for a in (before, after, sk, sq, gk, gq, cosine, sine)],
        out_specs=pl.BlockSpec((PER_STEP, BLK + EXTRA, 2 * HD), lambda i: (i, 0, 0)),
        out_shape=jax.ShapeDtypeStruct((blocks, BLK + EXTRA, 2 * HD), jnp.bfloat16),
        scratch_shapes=[
            pltpu.VMEM((2, rows, 2 * HD), jnp.bfloat16),
            pltpu.VMEM((2, rows + HALO, HD), jnp.bfloat16),
            pltpu.VMEM((2, rows + HALO, HD), jnp.bfloat16),
            pltpu.SemaphoreType.DMA((blocks, 4)),
        ],
        compiler_params=pltpu.CompilerParams(
            dimension_semantics=("arbitrary",), vmem_limit_bytes=48 * 1024 * 1024
        ),
        cost_estimate=pl.CostEstimate(flops=2 * 10**9, bytes_accessed=10**7, transcendentals=3 * 10**6),
        name="window_attention",
    )(place, *features, before, after, sk, sq, gk, gq, cosine, sine)


def along_sx(block, distance):
    n = lax.axis_size("sx")
    return lax.ppermute(block, "sx", [((i - distance) % n, i) for i in range(n)])


def unpack(arrived):
    attended = arrived[:, :BLK].transpose(1, 0, 2).reshape(BLK, H * HD)
    stats = arrived[:, BLK : BLK + 6].astype(jnp.float32)
    best = (stats[:, 0] + stats[:, 1]) + stats[:, 2]
    total = (stats[:, 3] + stats[:, 4]) + stats[:, 5]
    return attended, best.reshape(H, BLK), total.reshape(H, BLK)


def body(tokens, mod_shift, mod_scale, w_query, w_key, w_value, query_gain, key_gain):
    group = lax.axis_index("sx")
    mine = lax.axis_index("sy")
    z, x, core = mine // 8, mine // 2 % 4, mine % 2
    chips = jnp.stack([(z + dz) % 2 * 4 + (x + dx) % 4 for dz, dx in SLOTS])
    place = jnp.stack([chips * 2 + core, chips * 2 + 1 - core], axis=1).reshape(-1).astype(jnp.int32)
    half = BLK // 2

    own = layer_norm(tokens, mod_shift, mod_scale)
    left, right, far_z = from_left(own), from_right(own), from_z(own)
    own_w = jnp.stack([w_key, w_query, w_value])
    other_w = from_core(own_w)
    left_lo, right_hi = left[:half], right[half:]
    far_lo, far_hi = from_left(left_lo), from_right(right_hi)
    z_left_lo, z_right_hi = from_z(left_lo), from_z(right_hi)
    z_left_hi, z_right_lo = from_left(far_z[half:]), from_right(far_z[:half])
    z_far_lo, z_far_hi = from_left(z_left_lo), from_right(z_right_hi)

    rows = BLK * lax.axis_size("sy")
    cosine, sine = rope_tables(group * rows + jnp.arange(rows, dtype=jnp.int32))
    gq = lax.dynamic_slice(query_gain, (mine * 2 * HD,), (2 * HD,)).reshape(1, 2 * HD)
    gk = lax.dynamic_slice(key_gain, (mine * 2 * HD,), (2 * HD,)).reshape(1, 2 * HD)

    features, parts = [], []
    for pieces in (
        (own, left, right, far_z),
        (far_lo, far_hi, z_left_lo, z_left_hi, z_right_lo, z_right_hi),
        (z_far_lo, z_far_hi),
    ):
        made, given, part = project(pieces, own_w, other_w)
        features += [made, from_core(given)]
        parts.append(part[:2])
    part = jnp.concatenate(parts, axis=1)
    here = chips[:, None] == jnp.arange(8)[None, :]
    part = jnp.sum(jnp.where(here[None, :, :, None], part[:, :, None, :], 0.0), axis=1)
    sent = jnp.broadcast_to(part.reshape(1, 16, BLK), (NSY, 16, BLK))
    seen = lax.all_to_all(sent, "sy", split_axis=0, concat_axis=0, tiled=True)
    ssq = jnp.sum(seen.reshape(8, 2, 2, 8, BLK), axis=0).transpose(1, 2, 0, 3).reshape(2, 16, BLK)
    before, after = halo(place, features, ssq[0], gk, cosine, sine)
    before, after = along_sx(before, 1), along_sx(after, -1)
    out = attention(place, features, before, after, ssq[0], ssq[1], gk, gq, cosine, sine)
    arrived = lax.all_to_all(out, "sy", split_axis=0, concat_axis=0, tiled=True)
    return unpack(arrived)


def solution(mesh):
    placed = (
        P(("sx", "sy"), None),
        P(),
        P(),
        P(None, "sy"),
        P(None, "sy"),
        P(None, "sy"),
        P(),
        P(),
    )
    return jax.shard_map(
        body,
        mesh=mesh,
        in_specs=placed,
        out_specs=(P(("sx", "sy"), None), P(None, ("sx", "sy")), P(None, ("sx", "sy"))),
        check_vma=False,
    )
```

```python
import functools

import jax
import jax.numpy as jnp
import numpy as np
from jax import lax
from jax.experimental import pallas as pl
from jax.experimental.pallas import tpu as pltpu
from jax.sharding import PartitionSpec as P

H = 32
HD = 128
ROUNDS = 4
GRID_W = 80
GRID_H = 45
BLK = 128
HALO = ROUNDS * BLK
EXTRA = 16
NSY = 16
SCALE = np.float32(1.0) / np.sqrt(np.float32(HD))
LOG2E = np.float32(1.4426950408889634)


def layer_norm(values, mod_shift, mod_scale):
    wide = values.astype(jnp.float32)
    center = jnp.mean(wide, axis=-1, keepdims=True)
    spread = jnp.mean((wide - center) ** 2, axis=-1, keepdims=True)
    scaled = (wide - center) * lax.rsqrt(spread + 1e-06)
    return (scaled * (1.0 + mod_scale) + mod_shift).astype(jnp.bfloat16)


def rope_tables(positions):
    small_pairs = HD // 6
    time_pairs = (HD - 4 * small_pairs) // 2
    frame = (positions // (GRID_H * GRID_W)).astype(jnp.float32)
    row_pos = (positions // GRID_W % GRID_H).astype(jnp.float32)
    col_pos = (positions % GRID_W).astype(jnp.float32)
    time_freq = 10000.0 ** (-jnp.arange(time_pairs, dtype=jnp.float32) / time_pairs)
    space_freq = 10000.0 ** (-jnp.arange(small_pairs, dtype=jnp.float32) / small_pairs)
    freq = jnp.repeat(jnp.concatenate([time_freq, space_freq, space_freq]), 2)
    pair = jnp.arange(HD, dtype=jnp.int32) // 2
    where = jnp.where(
        pair < time_pairs,
        frame[:, None],
        jnp.where(pair < time_pairs + small_pairs, row_pos[:, None], col_pos[:, None]),
    )
    angles = where * freq
    sign = jnp.where(jnp.arange(HD) % 2 == 0, -1.0, 1.0).astype(jnp.float32)
    return jnp.cos(angles), jnp.sin(angles) * sign


def as_column(row):
    return jnp.broadcast_to(row, (BLK, BLK)).T


def as_row(column):
    return jnp.broadcast_to(column, (BLK, BLK)).T[0:1, :]


def norm_rope(raw, ssq_row, gain, cosine, sine):
    inv = lax.rsqrt(as_column(ssq_row) * (1.0 / (H * HD)) + 1e-06)
    wide = raw.astype(jnp.float32) * inv * gain
    lane = lax.broadcasted_iota(jnp.int32, wide.shape, 1)
    partner = jnp.where(
        lane % 2 == 0, pltpu.roll(wide, HD - 1, 1), pltpu.roll(wide, 1, 1)
    )
    return (wide * cosine + partner * sine).astype(jnp.bfloat16)


def split3(row):
    hi = row.astype(jnp.bfloat16).astype(jnp.float32)
    rest = row - hi
    mid = rest.astype(jnp.bfloat16).astype(jnp.float32)
    return [hi, mid, rest - mid]


PER_STEP = 4
SLOTS = ((0, 0), (0, -1), (0, 1), (1, 0), (0, 2), (1, -1), (1, 1), (1, 2))
CHUNKS = (4, 3, 1)


def chip_move(dz, dx, dc):
    return [
        (z * 8 + x * 2 + c, (z + dz) % 2 * 8 + (x + dx) % 4 * 2 + (c + dc) % 2)
        for z in range(2)
        for x in range(4)
        for c in range(2)
    ]


def from_left(block):
    return lax.ppermute(block, "sy", chip_move(0, 1, 0))


def from_right(block):
    return lax.ppermute(block, "sy", chip_move(0, -1, 0))


def from_z(block):
    return lax.ppermute(block, "sy", chip_move(1, 0, 0))


def from_core(block):
    return lax.ppermute(block, "sy", chip_move(0, 0, 1))


def project_kernel(*refs):
    n = len(refs) - 7
    pieces, (own_w, other_w, own_ref, other_ref, ssq_ref, x_ref, sems) = refs[:n], refs[n:]

    @pl.when(pl.program_id(0) == 0)
    def _():
        copies, at = [], 0
        for i, piece in enumerate(pieces):
            rows = piece.shape[0]
            copies.append(pltpu.make_async_copy(piece, x_ref.at[pl.ds(at, rows)], sems.at[i]))
            copies[-1].start()
            at += rows
        for copy in copies:
            copy.wait()

    total = None
    for weight, out in ((own_w, own_ref), (other_w, other_ref)):
        made = jnp.dot(x_ref[...], weight[0], preferred_element_type=jnp.float32).astype(jnp.bfloat16)
        out[0] = made
        wide = made.astype(jnp.float32)
        part = jnp.sum(wide * wide, axis=-1, keepdims=True)
        total = part if total is None else total + part
    for i in range(x_ref.shape[0] // BLK):
        ssq_ref[0, i : i + 1, :] = as_row(total[i * BLK : (i + 1) * BLK])


def project(pieces, own_w, other_w):
    rows = sum(p.shape[0] for p in pieces)
    depth, wide = own_w.shape[1:]
    w_spec = pl.BlockSpec((1, depth, wide), lambda i: (i, 0, 0))
    o_spec = pl.BlockSpec((1, rows, wide), lambda i: (i, 0, 0))
    out = jax.ShapeDtypeStruct((3, rows, wide), jnp.bfloat16)
    return pl.pallas_call(
        project_kernel,
        grid=(3,),
        in_specs=[pl.BlockSpec(memory_space=pl.ANY)] * len(pieces) + [w_spec, w_spec],
        out_specs=[o_spec, o_spec, pl.BlockSpec((1, rows // BLK, BLK), lambda i: (i, 0, 0))],
        out_shape=[out, out, jax.ShapeDtypeStruct((3, rows // BLK, BLK), jnp.float32)],
        scratch_shapes=[pltpu.VMEM((rows, depth), jnp.bfloat16), pltpu.SemaphoreType.DMA((len(pieces),))],
        compiler_params=pltpu.CompilerParams(
            dimension_semantics=("arbitrary",), vmem_limit_bytes=30 * 1024 * 1024
        ),
        cost_estimate=pl.CostEstimate(
            flops=12 * rows * depth * wide, bytes_accessed=12 * depth * wide, transcendentals=0
        ),
        name="project",
    )(*pieces, own_w, other_w)


def sources(refs):
    at = 0
    for chunk, slots in enumerate(CHUNKS):
        for i in range(slots):
            for core in range(2):
                yield (at + i) * 2 + core, refs[chunk * 2 + core], pl.ds(i * BLK, BLK)
        at += slots


def halo_kernel(
    place_ref, fa, ga, fb, gb, fc, gc, ssq_ref, gk_ref, cos_lo, sin_lo, cos_hi, sin_hi,
    before_ref, after_ref, raw, sems,
):
    blocks = 2 * sum(CHUNKS)
    ends = ((lambda n: n >= blocks - ROUNDS, blocks - ROUNDS, 0), (lambda n: n < ROUNDS, 0, 1))

    def each(act):
        for at, ref, rows in sources((fa, ga, fb, gb, fc, gc)):
            n = place_ref[at]
            for inside, first, head in ends:

                @pl.when(inside(n))
                def _(n=n, first=first, head=head, ref=ref, rows=rows, at=at):
                    to = pl.ds(pl.multiple_of((n - first) * BLK, BLK), BLK)
                    cols = pl.ds(head * HD, HD)
                    out = (before_ref, after_ref)[head]
                    act(pltpu.make_async_copy(ref.at[0, rows, cols], raw.at[head, to], sems.at[at, 0]))
                    act(pltpu.make_async_copy(ref.at[2, rows, cols], out.at[to, pl.ds(HD, HD)], sems.at[at, 1]))

    each(lambda copy: copy.start())
    each(lambda copy: copy.wait())
    for head, out, first, cosine, sine in (
        (0, before_ref, blocks - ROUNDS, cos_hi, sin_hi),
        (1, after_ref, 0, cos_lo, sin_lo),
    ):
        for i in range(ROUNDS):
            rows = pl.ds(i * BLK, BLK)
            out[rows, 0:HD] = norm_rope(
                raw[head, rows, :], ssq_ref[pl.ds(first + i, 1), :], gk_ref[:, head * HD : (head + 1) * HD],
                cosine[rows, :], sine[rows, :],
            )


VMEM = pl.BlockSpec(memory_space=pltpu.VMEM)
SMEM = pl.BlockSpec(memory_space=pltpu.SMEM)
ANYWHERE = pl.BlockSpec(memory_space=pl.ANY)


def halo(place, features, ssq_k, gk, cosine, sine):
    rows = cosine.shape[0]
    low = pl.BlockSpec((HALO, HD), lambda i: (0, 0))
    high = pl.BlockSpec((HALO, HD), lambda i: (rows // HALO - 1, 0))
    one = lambda a: pl.BlockSpec(a.shape, lambda i: (0, 0))
    out = jax.ShapeDtypeStruct((HALO, 2 * HD), jnp.bfloat16)
    return pl.pallas_call(
        halo_kernel,
        grid=(1,),
        in_specs=[SMEM] + [ANYWHERE] * 6 + [one(ssq_k), one(gk), low, low, high, high],
        out_specs=[pl.BlockSpec((HALO, 2 * HD), lambda i: (0, 0))] * 2,
        out_shape=[out, out],
        scratch_shapes=[
            pltpu.VMEM((2, HALO, HD), jnp.bfloat16),
            pltpu.SemaphoreType.DMA((2 * sum(CHUNKS), 2)),
        ],
        compiler_params=pltpu.CompilerParams(vmem_limit_bytes=48 * 1024 * 1024),
        cost_estimate=pl.CostEstimate(flops=10**7, bytes_accessed=3 * 10**6, transcendentals=0),
        name="halo_keys",
    )(place, *features, ssq_k, gk, cosine, sine, cosine, sine)


def attention_kernel(
    part, place_ref, fa, ga, fb, gb, fc, gc, before_ref, after_ref, sk_ref, sq_ref,
    gk_ref, gq_ref, cos_ref, sin_ref, *rest,
):
    out_ref, raw, kbuf, vbuf, sems = rest[-5:]
    step, head = pl.program_id(0), pl.program_id(1)
    blocks = 2 * sum(CHUNKS)
    columns = [slice(head * HD, (head + 1) * HD) for head in range(2)]
    own_first = (ROUNDS, 0)

    def wanted(n, head):
        if part == 0:
            return None
        return n < ROUNDS if head == 0 else n >= blocks - ROUNDS

    def guarded(condition, act):
        if condition is None:
            act()
        else:
            pl.when(condition)(act)

    @pl.when((step == 0) & (head == 0))
    def _():
        copies = []
        for at, ref, rows in sources((fa, ga, fb, gb, fc, gc)):
            n = place_ref[at]
            to = pl.ds(pl.multiple_of(n * BLK, BLK), BLK)
            needed = None if part == 0 else (n < ROUNDS) | (n >= blocks - ROUNDS)
            copies.append((n, needed, pltpu.make_async_copy(ref.at[:, rows], raw.at[:, to], sems.at[at])))
        for _, needed, copy in copies:
            guarded(needed, copy.start)
        if part == 1:
            for head, ref in enumerate((before_ref, after_ref)):
                to = pl.ds((0, blocks)[head] * BLK, HALO)
                kbuf[head, to, :] = ref[:, 0:HD]
                vbuf[head, :, to] = ref[:, HD:].T
        for n, needed, copy in copies:
            guarded(needed, copy.wait)

        def prepare(n, head):
            def act():
                rows = pl.ds(pl.multiple_of(n * BLK, BLK), BLK)
                to = pl.ds(pl.multiple_of((n + own_first[head]) * BLK, BLK), BLK)
                kbuf[head, to, :] = norm_rope(
                    raw[0, rows, columns[head]], sk_ref[pl.ds(n, 1), :], gk_ref[:, columns[head]],
                    cos_ref[rows, :], sin_ref[rows, :],
                )
                vbuf[head, :, to] = raw[2, rows, columns[head]].T

            return act

        for n in range(blocks):
            for head in range(2):
                if wanted(n, head) is not False:
                    prepare(n, head)()

    def attend(first, head):
        for j in range(PER_STEP):
            b = first + j
            rows = pl.ds(pl.multiple_of(b * BLK, BLK), BLK)
            window = pl.ds(pl.multiple_of(b * BLK, BLK), (ROUNDS + 1) * BLK)
            q = norm_rope(
                raw[1, rows, columns[head]], sq_ref[pl.ds(b, 1), :], gq_ref[:, columns[head]],
                cos_ref[rows, :], sin_ref[rows, :],
            )
            scores = lax.dot_general(
                kbuf[head, window, :], q, (((1,), (1,)), ((), ())), preferred_element_type=jnp.float32
            )
            top = jnp.max(scores, axis=0, keepdims=True)
            weight = jnp.exp2((scores - top) * (SCALE * LOG2E))
            total = jnp.sum(weight, axis=0, keepdims=True)
            mixed = jnp.dot(
                vbuf[head, :, window], weight.astype(jnp.bfloat16), preferred_element_type=jnp.float32
            )
            out_ref[j, 0, 0:BLK, :] = (mixed / total).T.astype(jnp.bfloat16)
            stats = split3(top * SCALE) + split3(total) + [jnp.zeros((EXTRA - 6, HD), jnp.float32)]
            out_ref[j, 0, BLK : BLK + EXTRA, :] = jnp.concatenate(stats, axis=0).astype(jnp.bfloat16)

    for which in range(2):
        first = (step + 1 - which) * PER_STEP if part == 0 else (0, blocks - ROUNDS)[which]
        pl.when(head == which)(functools.partial(attend, first, which))


def attention(part, place, features, before, after, sk, sq, gk, gq, cosine, sine, held=None):
    rows = cosine.shape[0]
    blocks = rows // BLK
    whole = lambda a: pl.BlockSpec(a.shape, lambda i, h, n=a.ndim: (0,) * n)
    steps = blocks // PER_STEP - 1 if part == 0 else 1
    which = (lambda i, h: (i + 1 - h, h, 0, 0)) if part == 0 else (lambda i, h: (h * (blocks // PER_STEP - 1), h, 0, 0))
    small = (before, after, sk, sq, gk, gq, cosine, sine)
    more = () if held is None else (held,)
    return pl.pallas_call(
        functools.partial(attention_kernel, part),
        grid=(steps, 2),
        in_specs=[SMEM] + [ANYWHERE] * 6 + [whole(a) for a in small] + [ANYWHERE] * len(more),
        out_specs=pl.BlockSpec((PER_STEP, 1, BLK + EXTRA, HD), which),
        out_shape=jax.ShapeDtypeStruct((blocks, 2, BLK + EXTRA, HD), jnp.bfloat16),
        scratch_shapes=[
            pltpu.VMEM((3, rows, 2 * HD), jnp.bfloat16),
            pltpu.VMEM((2, rows + HALO, HD), jnp.bfloat16),
            pltpu.VMEM((2, HD, rows + HALO), jnp.bfloat16),
            pltpu.SemaphoreType.DMA((blocks,)),
        ],
        input_output_aliases={15: 0} if more else {},
        compiler_params=pltpu.CompilerParams(
            dimension_semantics=("arbitrary", "arbitrary"), vmem_limit_bytes=56 * 1024 * 1024
        ),
        cost_estimate=pl.CostEstimate(
            flops=(1 + 2 * (1 - part)) * 5 * 10**8, bytes_accessed=10**7, transcendentals=10**6
        ),
        name=("window_attention", "window_attention_halo")[part],
    )(place, *features, *small, *more)


def along_sx(block, distance):
    n = lax.axis_size("sx")
    return lax.ppermute(block, "sx", [((i - distance) % n, i) for i in range(n)])


def unpack(arrived):
    attended = arrived[:, :, :BLK].transpose(2, 0, 1, 3).reshape(BLK, H * HD)
    stats = arrived[:, :, BLK : BLK + 6].astype(jnp.float32)
    best = (stats[:, :, 0] + stats[:, :, 1]) + stats[:, :, 2]
    total = (stats[:, :, 3] + stats[:, :, 4]) + stats[:, :, 5]
    return attended, best.reshape(H, BLK), total.reshape(H, BLK)


def body(tokens, mod_shift, mod_scale, w_query, w_key, w_value, query_gain, key_gain):
    group = lax.axis_index("sx")
    mine = lax.axis_index("sy")
    z, x, core = mine // 8, mine // 2 % 4, mine % 2
    chips = jnp.stack([(z + dz) % 2 * 4 + (x + dx) % 4 for dz, dx in SLOTS])
    place = jnp.stack([chips * 2 + core, chips * 2 + 1 - core], axis=1).reshape(-1).astype(jnp.int32)
    half = BLK // 2
    rows = BLK * lax.axis_size("sy")

    own_lo = layer_norm(tokens[:half], mod_shift, mod_scale)
    own_hi = layer_norm(tokens[half:], mod_shift, mod_scale)
    left_lo, right_hi, z_lo = from_left(own_lo), from_right(own_hi), from_z(own_lo)
    left_hi, right_lo, z_hi = from_left(own_hi), from_right(own_lo), from_z(own_hi)
    weights = lax.optimization_barrier((w_key, w_query, w_value, own_lo, own_hi))[:3]
    swapped = [from_core(w) for w in weights]
    weights, swapped, left_lo = lax.optimization_barrier((weights, swapped, left_lo))
    own_w, other_w = jnp.stack(weights), jnp.stack(swapped)
    far_lo, z_left_lo = from_left(left_lo), from_z(left_lo)
    far_hi, z_right_hi = from_right(right_hi), from_z(right_hi)
    z_left_hi, z_right_lo = from_left(z_hi), from_right(z_lo)

    cosine, sine = rope_tables(group * rows + jnp.arange(rows, dtype=jnp.int32))
    gq = lax.dynamic_slice(query_gain, (mine * 2 * HD,), (2 * HD,)).reshape(1, 2 * HD)
    gk = lax.dynamic_slice(key_gain, (mine * 2 * HD,), (2 * HD,)).reshape(1, 2 * HD)
    own_lo, cosine, sine, gq, gk, place = lax.optimization_barrier((own_lo, cosine, sine, gq, gk, place))

    near = project((own_lo, own_hi, left_lo, left_hi, right_lo, right_hi, z_lo, z_hi), own_w, other_w)
    near, z_left_lo, z_right_hi = lax.optimization_barrier((near, z_left_lo, z_right_hi))
    z_far_lo, z_far_hi = from_left(z_left_lo), from_right(z_right_hi)
    middle = project((far_lo, far_hi, z_left_lo, z_left_hi, z_right_lo, z_right_hi), own_w, other_w)
    z_far_lo, z_far_hi, middle = lax.optimization_barrier((z_far_lo, z_far_hi, middle))
    last = project((z_far_lo, z_far_hi), own_w, other_w)

    features, parts = [], []
    for made, given, part in (near, middle, last):
        features += [made, from_core(given)]
        parts.append(part[:2])
    part = jnp.concatenate(parts, axis=1)
    here = chips[:, None] == jnp.arange(8)[None, :]
    part = jnp.sum(jnp.where(here[None, :, :, None], part[:, :, None, :], 0.0), axis=1)
    sent = jnp.broadcast_to(part.reshape(1, 16, BLK), (NSY, 16, BLK))
    seen = lax.all_to_all(sent, "sy", split_axis=0, concat_axis=0, tiled=True)
    ssq = jnp.sum(seen.reshape(8, 2, 2, 8, BLK), axis=0).transpose(1, 2, 0, 3).reshape(2, 16, BLK)
    before, after = halo(place, features, ssq[0], gk, cosine, sine)
    common = (ssq[0], ssq[1], gk, gq, cosine, sine)
    out = attention(0, place, features, before, after, *common)
    before, after = along_sx(before, 1), along_sx(after, -1)
    out = attention(1, place, features, before, after, *common, held=out)
    arrived = lax.all_to_all(out, "sy", split_axis=0, concat_axis=0, tiled=True)
    return unpack(arrived)


def solution(mesh):
    placed = (
        P(("sx", "sy"), None),
        P(),
        P(),
        P(None, "sy"),
        P(None, "sy"),
        P(None, "sy"),
        P(),
        P(),
    )
    return jax.shard_map(
        body,
        mesh=mesh,
        in_specs=placed,
        out_specs=(P(("sx", "sy"), None), P(None, ("sx", "sy")), P(None, ("sx", "sy"))),
        check_vma=False,
    )
```

```python
import functools

import jax
import jax.numpy as jnp
import numpy as np
from jax import lax
from jax.experimental import pallas as pl
from jax.experimental.pallas import tpu as pltpu
from jax.sharding import PartitionSpec as P

H = 32
HD = 128
ROUNDS = 4
GRID_W = 80
GRID_H = 45
BLK = 128
HALO = ROUNDS * BLK
EXTRA = 16
NSY = 16
SCALE = np.float32(1.0) / np.sqrt(np.float32(HD))
LOG2E = np.float32(1.4426950408889634)


def layer_norm(values, mod_shift, mod_scale):
    wide = values.astype(jnp.float32)
    center = jnp.mean(wide, axis=-1, keepdims=True)
    spread = jnp.mean((wide - center) ** 2, axis=-1, keepdims=True)
    scaled = (wide - center) * lax.rsqrt(spread + 1e-06)
    return (scaled * (1.0 + mod_scale) + mod_shift).astype(jnp.bfloat16)


def rope_tables(positions):
    small_pairs = HD // 6
    time_pairs = (HD - 4 * small_pairs) // 2
    frame = (positions // (GRID_H * GRID_W)).astype(jnp.float32)
    row_pos = (positions // GRID_W % GRID_H).astype(jnp.float32)
    col_pos = (positions % GRID_W).astype(jnp.float32)
    time_freq = 10000.0 ** (-jnp.arange(time_pairs, dtype=jnp.float32) / time_pairs)
    space_freq = 10000.0 ** (-jnp.arange(small_pairs, dtype=jnp.float32) / small_pairs)
    freq = jnp.repeat(jnp.concatenate([time_freq, space_freq, space_freq]), 2)
    pair = jnp.arange(HD, dtype=jnp.int32) // 2
    where = jnp.where(
        pair < time_pairs,
        frame[:, None],
        jnp.where(pair < time_pairs + small_pairs, row_pos[:, None], col_pos[:, None]),
    )
    angles = where * freq
    sign = jnp.where(jnp.arange(HD) % 2 == 0, -1.0, 1.0).astype(jnp.float32)
    return jnp.cos(angles), jnp.sin(angles) * sign


def as_column(row):
    return jnp.broadcast_to(row, (BLK, BLK)).T


def as_row(column):
    return jnp.broadcast_to(column, (BLK, BLK)).T[0:1, :]


def inverse_norm(ssq_row):
    return as_column(lax.rsqrt(ssq_row * (1.0 / (H * HD)) + 1e-06))


def norm_rope(raw, inv, gain, cosine, sine):
    wide = raw.astype(jnp.float32) * inv * gain
    lane = lax.broadcasted_iota(jnp.int32, wide.shape, 1)
    partner = jnp.where(
        lane % 2 == 0, pltpu.roll(wide, HD - 1, 1), pltpu.roll(wide, 1, 1)
    )
    return (wide * cosine + partner * sine).astype(jnp.bfloat16)


def split3(row):
    hi = row.astype(jnp.bfloat16).astype(jnp.float32)
    rest = row - hi
    mid = rest.astype(jnp.bfloat16).astype(jnp.float32)
    return [hi, mid, rest - mid]


PER_STEP = 4
SLOTS = ((0, 0), (0, -1), (0, 1), (1, 0), (0, 2), (1, -1), (1, 1), (1, 2))
CHUNKS = (4, 3, 1)


def chip_move(dz, dx, dc):
    return [
        (z * 8 + x * 2 + c, (z + dz) % 2 * 8 + (x + dx) % 4 * 2 + (c + dc) % 2)
        for z in range(2)
        for x in range(4)
        for c in range(2)
    ]


def from_left(block):
    return lax.ppermute(block, "sy", chip_move(0, 1, 0))


def from_right(block):
    return lax.ppermute(block, "sy", chip_move(0, -1, 0))


def from_z(block):
    return lax.ppermute(block, "sy", chip_move(1, 0, 0))


def from_core(block):
    return lax.ppermute(block, "sy", chip_move(0, 0, 1))


ANYWHERE = pl.BlockSpec(memory_space=pl.ANY)
SMEM = pl.BlockSpec(memory_space=pltpu.SMEM)


def project_kernel(cuts, *refs):
    n = len(refs) - 7
    arrays, (own_w, other_w, own_ref, other_ref, ssq_ref, x_ref, sems) = refs[:n], refs[n:]

    @pl.when(pl.program_id(0) == 0)
    def _():
        copies, at = [], 0
        for i, (which, first, count) in enumerate(cuts):
            source = arrays[which].at[pl.ds(first, count)]
            copies.append(pltpu.make_async_copy(source, x_ref.at[pl.ds(at, count)], sems.at[i]))
            copies[-1].start()
            at += count
        for copy in copies:
            copy.wait()

    total = None
    for weight, out in ((own_w, own_ref), (other_w, other_ref)):
        made = jnp.dot(x_ref[...], weight[0], preferred_element_type=jnp.float32).astype(jnp.bfloat16)
        out[0] = made
        wide = made.astype(jnp.float32)
        part = jnp.sum(wide * wide, axis=-1, keepdims=True)
        total = part if total is None else total + part
    for i in range(x_ref.shape[0] // BLK):
        ssq_ref[0, i : i + 1, :] = as_row(total[i * BLK : (i + 1) * BLK])


def project(arrays, cuts, own_w, other_w):
    rows = sum(count for _, _, count in cuts)
    depth, wide = own_w.shape[1:]
    w_spec = pl.BlockSpec((1, depth, wide), lambda i: (i, 0, 0))
    o_spec = pl.BlockSpec((1, rows, wide), lambda i: (i, 0, 0))
    out = jax.ShapeDtypeStruct((3, rows, wide), jnp.bfloat16)
    return pl.pallas_call(
        functools.partial(project_kernel, cuts),
        grid=(3,),
        in_specs=[ANYWHERE] * len(arrays) + [w_spec, w_spec],
        out_specs=[o_spec, o_spec, pl.BlockSpec((1, rows // BLK, BLK), lambda i: (i, 0, 0))],
        out_shape=[out, out, jax.ShapeDtypeStruct((3, rows // BLK, BLK), jnp.float32)],
        scratch_shapes=[pltpu.VMEM((rows, depth), jnp.bfloat16), pltpu.SemaphoreType.DMA((len(cuts),))],
        compiler_params=pltpu.CompilerParams(
            dimension_semantics=("arbitrary",), vmem_limit_bytes=30 * 1024 * 1024
        ),
        cost_estimate=pl.CostEstimate(
            flops=12 * rows * depth * wide, bytes_accessed=12 * depth * wide, transcendentals=0
        ),
        name="project",
    )(*arrays, own_w, other_w)


def sources(refs):
    at = 0
    for chunk, slots in enumerate(CHUNKS):
        for i in range(slots):
            for core in range(2):
                yield (at + i) * 2 + core, refs[chunk * 2 + core], pl.ds(i * BLK, BLK)
        at += slots


def halo_kernel(place_ref, fa, ga, fb, gb, fc, gc, before_ref, after_ref, sems):
    blocks = 2 * sum(CHUNKS)
    ends = ((lambda n: n >= blocks - ROUNDS, blocks - ROUNDS, 0), (lambda n: n < ROUNDS, 0, 1))

    def each(act):
        for at, ref, rows in sources((fa, ga, fb, gb, fc, gc)):
            n = place_ref[at]
            for inside, first, head in ends:

                @pl.when(inside(n))
                def _(n=n, first=first, head=head, ref=ref, rows=rows, at=at):
                    to = pl.ds(pl.multiple_of((n - first) * BLK, BLK), BLK)
                    out = (before_ref, after_ref)[head]
                    for i, kind in enumerate((0, 2)):
                        source = ref.at[kind, rows, pl.ds(head * HD, HD)]
                        act(pltpu.make_async_copy(source, out.at[i, to], sems.at[at, i]))

    each(lambda copy: copy.start())
    each(lambda copy: copy.wait())


def halo(place, features):
    out = jax.ShapeDtypeStruct((2, HALO, HD), jnp.bfloat16)
    return pl.pallas_call(
        halo_kernel,
        in_specs=[SMEM] + [ANYWHERE] * 6,
        out_specs=[ANYWHERE] * 2,
        out_shape=[out, out],
        scratch_shapes=[pltpu.SemaphoreType.DMA((2 * sum(CHUNKS), 2))],
        compiler_params=pltpu.CompilerParams(vmem_limit_bytes=16 * 1024 * 1024),
        cost_estimate=pl.CostEstimate(flops=10**6, bytes_accessed=10**6, transcendentals=0),
        name="halo_rows",
    )(place, *features)


def attention_kernel(
    place_ref, fa, ga, fb, gb, fc, gc, before_ref, after_ref, sk_ref, sq_ref, sb_ref, sa_ref,
    gk_ref, gq_ref, cos_ref, sin_ref, out_ref, raw, kbuf, vbuf, sems,
):
    step = pl.program_id(0)
    blocks = 2 * sum(CHUNKS)
    columns = [slice(head * HD, (head + 1) * HD) for head in range(2)]

    @pl.when(step == 0)
    def _():
        copies = []
        for at, ref, rows in sources((fa, ga, fb, gb, fc, gc)):
            to = pl.ds(pl.multiple_of(place_ref[at] * BLK, BLK), BLK)
            copies.append(pltpu.make_async_copy(ref.at[:, rows], raw.at[:, to], sems.at[at]))
        for copy in copies:
            copy.start()

        def put(head, n, keys, values, inv):
            to = slice(n * BLK, (n + 1) * BLK)
            table = slice((n + head * ROUNDS) * BLK, (n + head * ROUNDS + 1) * BLK)
            kbuf[head, to, :] = norm_rope(keys, inv, gk_ref[:, columns[head]], cos_ref[table, :], sin_ref[table, :])
            vbuf[head, :, to] = values.T

        for head, ref, ssq in ((0, before_ref, sb_ref), (1, after_ref, sa_ref)):
            for i in range(ROUNDS):
                rows = slice(i * BLK, (i + 1) * BLK)
                put(head, head * blocks + i, ref[0, rows, :], ref[1, rows, :], inverse_norm(ssq[i : i + 1, :]))
        for copy in copies:
            copy.wait()
        for n in range(blocks):
            rows = slice(n * BLK, (n + 1) * BLK)
            inv = inverse_norm(sk_ref[n : n + 1, :])
            for head in range(2):
                put(head, n + (1 - head) * ROUNDS, raw[0, rows, columns[head]], raw[2, rows, columns[head]], inv)

    for j in range(PER_STEP):
        b = step * PER_STEP + j
        rows = pl.ds(pl.multiple_of(b * BLK, BLK), BLK)
        table = pl.ds(pl.multiple_of((b + ROUNDS) * BLK, BLK), BLK)
        window = pl.ds(pl.multiple_of(b * BLK, BLK), (ROUNDS + 1) * BLK)
        inv = inverse_norm(sq_ref[pl.ds(b, 1), :])
        for head in range(2):
            q = norm_rope(
                raw[1, rows, columns[head]], inv, gq_ref[:, columns[head]], cos_ref[table, :], sin_ref[table, :]
            )
            scores = lax.dot_general(
                kbuf[head, window, :], q, (((1,), (1,)), ((), ())), preferred_element_type=jnp.float32
            )
            top = jnp.max(scores, axis=0, keepdims=True)
            weight = jnp.exp2((scores - top) * (SCALE * LOG2E))
            total = jnp.sum(weight, axis=0, keepdims=True)
            mixed = jnp.dot(
                vbuf[head, :, window], weight.astype(jnp.bfloat16), preferred_element_type=jnp.float32
            )
            out_ref[j, 0:BLK, columns[head]] = (mixed / total).T.astype(jnp.bfloat16)
            stats = split3(top * SCALE) + split3(total) + [jnp.zeros((EXTRA - 6, HD), jnp.float32)]
            out_ref[j, BLK : BLK + EXTRA, columns[head]] = jnp.concatenate(stats, axis=0).astype(jnp.bfloat16)


def attention(place, features, before, after, sk, sq, sb, sa, gk, gq, cosine, sine):
    rows = sk.shape[0] * BLK
    blocks = rows // BLK
    whole = lambda a: pl.BlockSpec(a.shape, lambda i, n=a.ndim: (0,) * n)
    small = (before, after, sk, sq, sb, sa, gk, gq, cosine, sine)
    return pl.pallas_call(
        attention_kernel,
        grid=(blocks // PER_STEP,),
        in_specs=[SMEM] + [ANYWHERE] * 6 + [whole(a) for a in small],
        out_specs=pl.BlockSpec((PER_STEP, BLK + EXTRA, 2 * HD), lambda i: (i, 0, 0)),
        out_shape=jax.ShapeDtypeStruct((blocks, BLK + EXTRA, 2 * HD), jnp.bfloat16),
        scratch_shapes=[
            pltpu.VMEM((3, rows, 2 * HD), jnp.bfloat16),
            pltpu.VMEM((2, rows + HALO, HD), jnp.bfloat16),
            pltpu.VMEM((2, HD, rows + HALO), jnp.bfloat16),
            pltpu.SemaphoreType.DMA((blocks,)),
        ],
        compiler_params=pltpu.CompilerParams(
            dimension_semantics=("arbitrary",), vmem_limit_bytes=56 * 1024 * 1024
        ),
        cost_estimate=pl.CostEstimate(flops=2 * 10**9, bytes_accessed=10**7, transcendentals=10**6),
        name="window_attention",
    )(place, *features, *small)


def along_sx(block, distance):
    n = lax.axis_size("sx")
    return lax.ppermute(block, "sx", [((i - distance) % n, i) for i in range(n)])


def unpack(arrived):
    attended = arrived[:, :BLK].transpose(1, 0, 2).reshape(BLK, H * HD)
    stats = arrived[:, BLK : BLK + 6].astype(jnp.float32)
    best = (stats[:, 0] + stats[:, 1]) + stats[:, 2]
    total = (stats[:, 3] + stats[:, 4]) + stats[:, 5]
    return attended, best.reshape(H, BLK), total.reshape(H, BLK)


def body(tokens, mod_shift, mod_scale, w_query, w_key, w_value, query_gain, key_gain):
    group = lax.axis_index("sx")
    mine = lax.axis_index("sy")
    z, x, core = mine // 8, mine // 2 % 4, mine % 2
    chips = jnp.stack([(z + dz) % 2 * 4 + (x + dx) % 4 for dz, dx in SLOTS])
    place = jnp.stack([chips * 2 + core, chips * 2 + 1 - core], axis=1).reshape(-1).astype(jnp.int32)
    half = BLK // 2
    rows = BLK * lax.axis_size("sy")
    count = rows * lax.axis_size("sx")
    barrier = lax.optimization_barrier

    own = layer_norm(tokens, mod_shift, mod_scale)
    left, right, beside = from_left(own), from_right(own), from_z(own)
    weights = barrier((w_key, w_query, w_value, own))[:3]
    own_w, other_w = jnp.stack(weights), jnp.stack([from_core(w) for w in weights])
    positions = (group * rows - HALO + jnp.arange(rows + 2 * HALO, dtype=jnp.int32) + count) % count
    cosine, sine = rope_tables(positions)
    gq = lax.dynamic_slice(query_gain, (mine * 2 * HD,), (2 * HD,)).reshape(1, 2 * HD)
    gk = lax.dynamic_slice(key_gain, (mine * 2 * HD,), (2 * HD,)).reshape(1, 2 * HD)
    (left, right, beside), (own_w, other_w), (cosine, sine, gq, gk, place) = barrier(
        ((left, right, beside), (own_w, other_w), (cosine, sine, gq, gk, place))
    )

    by_z = from_z(jnp.concatenate([left[:half], right[half:]]))
    by_left = from_left(jnp.concatenate([left[:half], beside[half:]]))
    by_right = from_right(jnp.concatenate([right[half:], beside[:half]]))
    near = project((own, left, right, beside), tuple((i, 0, BLK) for i in range(4)), own_w, other_w)

    near, by_z = barrier((near, by_z))
    far_lo, far_hi = from_left(by_z[:half]), from_right(by_z[half:])
    middle = project(
        (by_left, by_right, by_z),
        ((0, 0, half), (1, 0, half), (2, 0, half), (0, half, half), (1, half, half), (2, half, half)),
        own_w, other_w,
    )
    far_lo, far_hi, middle = barrier((far_lo, far_hi, middle))
    last = project((far_lo, far_hi), ((0, 0, half), (1, 0, half)), own_w, other_w)

    features, parts = [], []
    for made, given, part in (near, middle, last):
        features += [made, from_core(given)]
        parts.append(part[:2])
    part = jnp.concatenate(parts, axis=1)
    here = chips[:, None] == jnp.arange(8)[None, :]
    part = jnp.sum(jnp.where(here[None, :, :, None], part[:, :, None, :], 0.0), axis=1)
    sent = jnp.broadcast_to(part.reshape(1, 16, BLK), (NSY, 16, BLK))
    seen = lax.all_to_all(sent, "sy", split_axis=0, concat_axis=0, tiled=True)
    ssq = jnp.sum(seen.reshape(8, 2, 2, 8, BLK), axis=0).transpose(1, 2, 0, 3).reshape(2, 16, BLK)
    before, after = halo(place, features)
    before, after = along_sx(before, 1), along_sx(after, -1)
    sb, sa = along_sx(ssq[0, -ROUNDS:], 1), along_sx(ssq[0, :ROUNDS], -1)
    out = attention(place, features, before, after, ssq[0], ssq[1], sb, sa, gk, gq, cosine, sine)
    arrived = lax.all_to_all(out, "sy", split_axis=0, concat_axis=0, tiled=True)
    return unpack(arrived)


def solution(mesh):
    placed = (
        P(("sx", "sy"), None),
        P(),
        P(),
        P(None, "sy"),
        P(None, "sy"),
        P(None, "sy"),
        P(),
        P(),
    )
    return jax.shard_map(
        body,
        mesh=mesh,
        in_specs=placed,
        out_specs=(P(("sx", "sy"), None), P(None, ("sx", "sy")), P(None, ("sx", "sy"))),
        check_vma=False,
    )
```

```python
import functools

import jax
import jax.numpy as jnp
import numpy as np
from jax import lax
from jax.experimental import pallas as pl
from jax.experimental.pallas import tpu as pltpu
from jax.sharding import PartitionSpec as P

H = 32
HD = 128
ROUNDS = 4
GRID_W = 80
GRID_H = 45
BLK = 128
HALO = ROUNDS * BLK
EXTRA = 16
NSY = 16
SCALE = np.float32(1.0) / np.sqrt(np.float32(HD))
LOG2E = np.float32(1.4426950408889634)


def layer_norm_kernel(tokens_ref, shift_ref, scale_ref, out_ref):
    wide = tokens_ref[...].astype(jnp.float32)
    center = jnp.mean(wide, axis=-1, keepdims=True)
    apart = wide - center
    spread = jnp.mean(apart * apart, axis=-1, keepdims=True)
    scaled = apart * lax.rsqrt(spread + 1e-06)
    out_ref[...] = (scaled * (1.0 + scale_ref[...]) + shift_ref[...]).astype(jnp.bfloat16)


def layer_norm(values, mod_shift, mod_scale):
    rows, wide = values.shape
    block = pl.BlockSpec((32, wide), lambda i: (i, 0))
    vector = pl.BlockSpec((1, wide), lambda i: (0, 0))
    return pl.pallas_call(
        layer_norm_kernel,
        grid=(rows // 32,),
        in_specs=[block, vector, vector],
        out_specs=block,
        out_shape=jax.ShapeDtypeStruct((rows, wide), jnp.bfloat16),
        compiler_params=pltpu.CompilerParams(vmem_limit_bytes=16 * 1024 * 1024),
        cost_estimate=pl.CostEstimate(flops=10 * rows * wide, bytes_accessed=4 * rows * wide, transcendentals=rows),
        name="layer_norm",
    )(values, mod_shift.reshape(1, wide), mod_scale.reshape(1, wide))


def rope_tables(positions):
    small_pairs = HD // 6
    time_pairs = (HD - 4 * small_pairs) // 2
    frame = (positions // (GRID_H * GRID_W)).astype(jnp.float32)
    row_pos = (positions // GRID_W % GRID_H).astype(jnp.float32)
    col_pos = (positions % GRID_W).astype(jnp.float32)
    time_freq = 10000.0 ** (-jnp.arange(time_pairs, dtype=jnp.float32) / time_pairs)
    space_freq = 10000.0 ** (-jnp.arange(small_pairs, dtype=jnp.float32) / small_pairs)
    freq = jnp.repeat(jnp.concatenate([time_freq, space_freq, space_freq]), 2)
    pair = jnp.arange(HD, dtype=jnp.int32) // 2
    where = jnp.where(
        pair < time_pairs,
        frame[:, None],
        jnp.where(pair < time_pairs + small_pairs, row_pos[:, None], col_pos[:, None]),
    )
    angles = where * freq
    sign = jnp.where(jnp.arange(HD) % 2 == 0, -1.0, 1.0).astype(jnp.float32)
    return jnp.cos(angles), jnp.sin(angles) * sign


def as_column(row):
    return jnp.broadcast_to(row, (BLK, BLK)).T


def as_row(column):
    return jnp.broadcast_to(column, (BLK, BLK)).T[0:1, :]


def inverse_norm(ssq_row):
    return as_column(lax.rsqrt(ssq_row * (1.0 / (H * HD)) + 1e-06))


def norm_rope(raw, inv, gain, cosine, sine):
    wide = raw.astype(jnp.float32) * inv * gain
    lane = lax.broadcasted_iota(jnp.int32, wide.shape, 1)
    partner = jnp.where(
        lane % 2 == 0, pltpu.roll(wide, HD - 1, 1), pltpu.roll(wide, 1, 1)
    )
    return (wide * cosine + partner * sine).astype(jnp.bfloat16)


def split3(row):
    hi = row.astype(jnp.bfloat16).astype(jnp.float32)
    rest = row - hi
    mid = rest.astype(jnp.bfloat16).astype(jnp.float32)
    return [hi, mid, rest - mid]


PER_STEP = 4
SLOTS = ((0, 0), (0, -1), (0, 1), (1, 0), (0, 2), (1, -1), (1, 1), (1, 2))
CHUNKS = (4, 3, 1)


def chip_move(dz, dx, dc):
    return [
        (z * 8 + x * 2 + c, (z + dz) % 2 * 8 + (x + dx) % 4 * 2 + (c + dc) % 2)
        for z in range(2)
        for x in range(4)
        for c in range(2)
    ]


def from_left(block):
    return lax.ppermute(block, "sy", chip_move(0, 1, 0))


def from_right(block):
    return lax.ppermute(block, "sy", chip_move(0, -1, 0))


def from_z(block):
    return lax.ppermute(block, "sy", chip_move(1, 0, 0))


def from_core(block):
    return lax.ppermute(block, "sy", chip_move(0, 0, 1))


ANYWHERE = pl.BlockSpec(memory_space=pltpu.HBM)
SMEM = pl.BlockSpec(memory_space=pltpu.SMEM)


def project_kernel(cuts, *refs):
    n = len(refs) - 7
    arrays, (own_w, other_w, own_ref, other_ref, ssq_ref, x_ref, sems) = refs[:n], refs[n:]

    @pl.when(pl.program_id(0) == 0)
    def _():
        copies, at = [], 0
        for i, (which, first, count) in enumerate(cuts):
            source = arrays[which].at[pl.ds(first, count)]
            copies.append(pltpu.make_async_copy(source, x_ref.at[pl.ds(at, count)], sems.at[i]))
            copies[-1].start()
            at += count
        for copy in copies:
            copy.wait()

    total = None
    for weight, out in ((own_w, own_ref), (other_w, other_ref)):
        made = jnp.dot(x_ref[...], weight[0], preferred_element_type=jnp.float32).astype(jnp.bfloat16)
        out[0] = made
        wide = made.astype(jnp.float32)
        part = jnp.sum(wide * wide, axis=-1, keepdims=True)
        total = part if total is None else total + part
    for i in range(x_ref.shape[0] // BLK):
        ssq_ref[0, i : i + 1, :] = as_row(total[i * BLK : (i + 1) * BLK])


def project(arrays, cuts, own_w, other_w):
    rows = sum(count for _, _, count in cuts)
    depth, wide = own_w.shape[1:]
    w_spec = pl.BlockSpec((1, depth, wide), lambda i: (i, 0, 0))
    o_spec = pl.BlockSpec((1, rows, wide), lambda i: (i, 0, 0))
    out = jax.ShapeDtypeStruct((3, rows, wide), jnp.bfloat16)
    return pl.pallas_call(
        functools.partial(project_kernel, cuts),
        grid=(3,),
        in_specs=[ANYWHERE] * len(arrays) + [w_spec, w_spec],
        out_specs=[o_spec, o_spec, pl.BlockSpec((1, rows // BLK, BLK), lambda i: (i, 0, 0))],
        out_shape=[out, out, jax.ShapeDtypeStruct((3, rows // BLK, BLK), jnp.float32)],
        scratch_shapes=[pltpu.VMEM((rows, depth), jnp.bfloat16), pltpu.SemaphoreType.DMA((len(cuts),))],
        compiler_params=pltpu.CompilerParams(
            dimension_semantics=("arbitrary",), vmem_limit_bytes=26 * 1024 * 1024
        ),
        cost_estimate=pl.CostEstimate(
            flops=12 * rows * depth * wide, bytes_accessed=12 * depth * wide, transcendentals=0
        ),
        name="project",
    )(*arrays, own_w, other_w)


def sources(refs):
    at = 0
    for chunk, slots in enumerate(CHUNKS):
        for i in range(slots):
            for core in range(2):
                yield (at + i) * 2 + core, refs[chunk * 2 + core], pl.ds(i * BLK, BLK)
        at += slots


def halo_kernel(
    place_ref, fa, ga, fb, gb, fc, gc, ssq_ref, gk_ref, cos_lo, sin_lo, cos_hi, sin_hi,
    before_ref, after_ref, raw, sems,
):
    blocks = 2 * sum(CHUNKS)
    ends = ((lambda n: n >= blocks - ROUNDS, blocks - ROUNDS, 0), (lambda n: n < ROUNDS, 0, 1))

    def each(act):
        for at, ref, rows in sources((fa, ga, fb, gb, fc, gc)):
            n = place_ref[at]
            for inside, first, head in ends:

                @pl.when(inside(n))
                def _(n=n, first=first, head=head, ref=ref, rows=rows, at=at):
                    to = pl.ds(pl.multiple_of((n - first) * BLK, BLK), BLK)
                    cols = pl.ds(head * HD, HD)
                    out = (before_ref, after_ref)[head]
                    act(pltpu.make_async_copy(ref.at[0, rows, cols], raw.at[head, to], sems.at[at, 0]))
                    act(pltpu.make_async_copy(ref.at[2, rows, cols], out.at[to, pl.ds(HD, HD)], sems.at[at, 1]))

    each(lambda copy: copy.start())
    each(lambda copy: copy.wait())
    for head, out, first, cosine, sine in (
        (0, before_ref, blocks - ROUNDS, cos_hi, sin_hi),
        (1, after_ref, 0, cos_lo, sin_lo),
    ):
        for i in range(ROUNDS):
            rows = pl.ds(i * BLK, BLK)
            out[rows, 0:HD] = norm_rope(
                raw[head, rows, :], inverse_norm(ssq_ref[pl.ds(first + i, 1), :]),
                gk_ref[:, head * HD : (head + 1) * HD],
                cosine[rows, :], sine[rows, :],
            )


def halo(place, features, ssq_k, gk, cosine, sine):
    rows = cosine.shape[0]
    low = pl.BlockSpec((HALO, HD), lambda i: (0, 0))
    high = pl.BlockSpec((HALO, HD), lambda i: (rows // HALO - 1, 0))
    one = lambda a: pl.BlockSpec(a.shape, lambda i: (0, 0))
    out = jax.ShapeDtypeStruct((HALO, 2 * HD), jnp.bfloat16)
    return pl.pallas_call(
        halo_kernel,
        grid=(1,),
        in_specs=[SMEM] + [ANYWHERE] * 6 + [one(ssq_k), one(gk), low, low, high, high],
        out_specs=[pl.BlockSpec((HALO, 2 * HD), lambda i: (0, 0))] * 2,
        out_shape=[out, out],
        scratch_shapes=[
            pltpu.VMEM((2, HALO, HD), jnp.bfloat16),
            pltpu.SemaphoreType.DMA((2 * sum(CHUNKS), 2)),
        ],
        compiler_params=pltpu.CompilerParams(vmem_limit_bytes=16 * 1024 * 1024),
        cost_estimate=pl.CostEstimate(flops=10**7, bytes_accessed=3 * 10**6, transcendentals=0),
        name="halo_keys",
    )(place, *features, ssq_k, gk, cosine, sine, cosine, sine)


def attention_kernel(
    part, place_ref, fa, ga, fb, gb, fc, gc, before_ref, after_ref, sk_ref, sq_ref,
    gk_ref, gq_ref, cos_ref, sin_ref, *rest,
):
    out_ref, raw, kbuf, vbuf, sems = rest[-5:]
    step, head = pl.program_id(0), pl.program_id(1)
    blocks = 2 * sum(CHUNKS)
    columns = [slice(head * HD, (head + 1) * HD) for head in range(2)]
    own_first = (ROUNDS, 0)

    def guarded(condition, act):
        if condition is None:
            act()
        else:
            pl.when(condition)(act)

    @pl.when((step == 0) & (head == 0))
    def _():
        copies = []
        for at, ref, rows in sources((fa, ga, fb, gb, fc, gc)):
            n = place_ref[at]
            to = pl.ds(pl.multiple_of(n * BLK, BLK), BLK)
            needed = None if part == 0 else (n < ROUNDS) | (n >= blocks - ROUNDS)
            copies.append((n, needed, pltpu.make_async_copy(ref.at[:, rows], raw.at[:, to], sems.at[at])))
        for _, needed, copy in copies:
            guarded(needed, copy.start)
        if part == 1:
            for head, ref in enumerate((before_ref, after_ref)):
                to = pl.ds((0, blocks)[head] * BLK, HALO)
                kbuf[head, to, :] = ref[:, 0:HD]
                vbuf[head, :, to] = ref[:, HD:].T
        for n, needed, copy in copies:
            guarded(needed, copy.wait)

        for n in range(blocks):
            heads = [head for head in range(2) if part == 0 or (n < ROUNDS, n >= blocks - ROUNDS)[head]]
            rows = slice(n * BLK, (n + 1) * BLK)
            inv = inverse_norm(sk_ref[n : n + 1, :]) if heads else None
            for head in heads:
                to = slice((n + own_first[head]) * BLK, (n + own_first[head] + 1) * BLK)
                kbuf[head, to, :] = norm_rope(
                    raw[0, rows, columns[head]], inv, gk_ref[:, columns[head]], cos_ref[rows, :], sin_ref[rows, :]
                )
                vbuf[head, :, to] = raw[2, rows, columns[head]].T

    def attend(first, head):
        for j in range(PER_STEP):
            b = first + j
            rows = pl.ds(pl.multiple_of(b * BLK, BLK), BLK)
            window = pl.ds(pl.multiple_of(b * BLK, BLK), (ROUNDS + 1) * BLK)
            q = norm_rope(
                raw[1, rows, columns[head]], inverse_norm(sq_ref[pl.ds(b, 1), :]), gq_ref[:, columns[head]],
                cos_ref[rows, :], sin_ref[rows, :],
            )
            scores = lax.dot_general(
                kbuf[head, window, :], q, (((1,), (1,)), ((), ())), preferred_element_type=jnp.float32
            )
            top = jnp.max(scores, axis=0, keepdims=True)
            weight = jnp.exp2((scores - top) * (SCALE * LOG2E))
            total = jnp.sum(weight, axis=0, keepdims=True)
            mixed = jnp.dot(
                vbuf[head, :, window], weight.astype(jnp.bfloat16), preferred_element_type=jnp.float32
            )
            out_ref[j, 0, 0:BLK, :] = (mixed / total).T.astype(jnp.bfloat16)
            stats = split3(top * SCALE) + split3(total) + [jnp.zeros((EXTRA - 6, HD), jnp.float32)]
            out_ref[j, 0, BLK : BLK + EXTRA, :] = jnp.concatenate(stats, axis=0).astype(jnp.bfloat16)

    for which in range(2):
        first = (step + 1 - which) * PER_STEP if part == 0 else (0, blocks - ROUNDS)[which]
        pl.when(head == which)(functools.partial(attend, first, which))


def attention(part, place, features, before, after, sk, sq, gk, gq, cosine, sine, held=None):
    rows = cosine.shape[0]
    blocks = rows // BLK
    whole = lambda a: pl.BlockSpec(a.shape, lambda i, h, n=a.ndim: (0,) * n)
    steps = blocks // PER_STEP - 1 if part == 0 else 1
    which = (lambda i, h: (i + 1 - h, h, 0, 0)) if part == 0 else (lambda i, h: (h * (blocks // PER_STEP - 1), h, 0, 0))
    small = (before, after, sk, sq, gk, gq, cosine, sine)
    more = () if held is None else (held,)
    return pl.pallas_call(
        functools.partial(attention_kernel, part),
        grid=(steps, 2),
        in_specs=[SMEM] + [ANYWHERE] * 6 + [whole(a) for a in small] + [ANYWHERE] * len(more),
        out_specs=pl.BlockSpec((PER_STEP, 1, BLK + EXTRA, HD), which),
        out_shape=jax.ShapeDtypeStruct((blocks, 2, BLK + EXTRA, HD), jnp.bfloat16),
        scratch_shapes=[
            pltpu.VMEM((3, rows, 2 * HD), jnp.bfloat16),
            pltpu.VMEM((2, rows + HALO, HD), jnp.bfloat16),
            pltpu.VMEM((2, HD, rows + HALO), jnp.bfloat16),
            pltpu.SemaphoreType.DMA((blocks,)),
        ],
        input_output_aliases={15: 0} if more else {},
        compiler_params=pltpu.CompilerParams(
            dimension_semantics=("arbitrary", "arbitrary"), vmem_limit_bytes=24 * 1024 * 1024
        ),
        cost_estimate=pl.CostEstimate(
            flops=(1 + 2 * (1 - part)) * 5 * 10**8, bytes_accessed=10**7, transcendentals=10**6
        ),
        name=("window_attention", "window_attention_halo")[part],
    )(place, *features, *small, *more)


def along_sx(block, distance):
    n = lax.axis_size("sx")
    return lax.ppermute(block, "sx", [((i - distance) % n, i) for i in range(n)])


def unpack(arrived):
    attended = arrived[:, :, :BLK].transpose(2, 0, 1, 3).reshape(BLK, H * HD)
    stats = arrived[:, :, BLK : BLK + 6].astype(jnp.float32)
    best = (stats[:, :, 0] + stats[:, :, 1]) + stats[:, :, 2]
    total = (stats[:, :, 3] + stats[:, :, 4]) + stats[:, :, 5]
    return attended, best.reshape(H, BLK), total.reshape(H, BLK)


def body(tokens, mod_shift, mod_scale, w_query, w_key, w_value, query_gain, key_gain):
    group = lax.axis_index("sx")
    mine = lax.axis_index("sy")
    z, x, core = mine // 8, mine // 2 % 4, mine % 2
    chips = jnp.stack([(z + dz) % 2 * 4 + (x + dx) % 4 for dz, dx in SLOTS])
    place = jnp.stack([chips * 2 + core, chips * 2 + 1 - core], axis=1).reshape(-1).astype(jnp.int32)
    rows = BLK * lax.axis_size("sy")
    barrier = lax.optimization_barrier

    own = layer_norm(tokens, mod_shift, mod_scale)
    left, right, beside = from_left(own), from_right(own), from_z(own)
    own_w = jnp.stack(barrier((w_key, w_query, w_value, own))[:3])
    cosine, sine = rope_tables(group * rows + jnp.arange(rows, dtype=jnp.int32))
    gq = lax.dynamic_slice(query_gain, (mine * 2 * HD,), (2 * HD,)).reshape(1, 2 * HD)
    gk = lax.dynamic_slice(key_gain, (mine * 2 * HD,), (2 * HD,)).reshape(1, 2 * HD)
    (left, right, beside), own_w, (cosine, sine, gq, gk, place) = barrier(
        ((left, right, beside), own_w, (cosine, sine, gq, gk, place))
    )

    far, z_right, z_left = from_left(left), from_right(beside), from_z(left)
    other_w = from_core(own_w)
    near = project((own, left, right, beside), tuple((i, 0, BLK) for i in range(4)), own_w, other_w)
    near, far, z_right, z_left = barrier((near, far, z_right, z_left))

    cuts = (48, 96)
    z_far = (from_left(z_left[: cuts[0]]), from_right(z_right[cuts[0] : cuts[1]]), from_z(far[cuts[1] :]))
    middle = project((far, z_left, z_right), tuple((i, 0, BLK) for i in range(3)), own_w, other_w)
    z_far, middle = barrier((z_far, middle))
    last = project(z_far, tuple((i, 0, p.shape[0]) for i, p in enumerate(z_far)), own_w, other_w)

    features, parts = [], []
    for made, given, part in (near, middle, last):
        features += [made, from_core(given)]
        parts.append(part[:2])
    part = jnp.concatenate(parts, axis=1)
    here = chips[:, None] == jnp.arange(8)[None, :]
    part = jnp.sum(jnp.where(here[None, :, :, None], part[:, :, None, :], 0.0), axis=1)
    sent = jnp.broadcast_to(part.reshape(1, 16, BLK), (NSY, 16, BLK))
    seen = lax.all_to_all(sent, "sy", split_axis=0, concat_axis=0, tiled=True)
    ssq = jnp.sum(seen.reshape(8, 2, 2, 8, BLK), axis=0).transpose(1, 2, 0, 3).reshape(2, 16, BLK)
    before, after = halo(place, features, ssq[0], gk, cosine, sine)
    common = (ssq[0], ssq[1], gk, gq, cosine, sine)
    out = attention(0, place, features, before, after, *common)
    before, after = along_sx(before, 1), along_sx(after, -1)
    out = attention(1, place, features, before, after, *common, held=out)
    arrived = lax.all_to_all(out, "sy", split_axis=0, concat_axis=0, tiled=True)
    return unpack(arrived)


def solution(mesh):
    placed = (
        P(("sx", "sy"), None),
        P(),
        P(),
        P(None, "sy"),
        P(None, "sy"),
        P(None, "sy"),
        P(),
        P(),
    )
    return jax.shard_map(
        body,
        mesh=mesh,
        in_specs=placed,
        out_specs=(P(("sx", "sy"), None), P(None, ("sx", "sy")), P(None, ("sx", "sy"))),
        check_vma=False,
    )
```

```python
import functools

import jax
import jax.numpy as jnp
import numpy as np
from jax import lax
from jax.experimental import pallas as pl
from jax.experimental.pallas import tpu as pltpu
from jax.sharding import PartitionSpec as P

H = 32
HD = 128
ROUNDS = 4
GRID_W = 80
GRID_H = 45
BLK = 128
HALO = ROUNDS * BLK
EXTRA = 16
NSY = 16
SCALE = np.float32(1.0) / np.sqrt(np.float32(HD))
LOG2E = np.float32(1.4426950408889634)


def layer_norm_kernel(tokens_ref, shift_ref, scale_ref, out_ref):
    wide = tokens_ref[...].astype(jnp.float32)
    center = jnp.mean(wide, axis=-1, keepdims=True)
    apart = wide - center
    spread = jnp.mean(apart * apart, axis=-1, keepdims=True)
    scaled = apart * lax.rsqrt(spread + 1e-06)
    out_ref[...] = (scaled * (1.0 + scale_ref[...]) + shift_ref[...]).astype(jnp.bfloat16)


def layer_norm(values, mod_shift, mod_scale):
    rows, wide = values.shape
    block = pl.BlockSpec((32, wide), lambda i: (i, 0))
    vector = pl.BlockSpec((1, wide), lambda i: (0, 0))
    return pl.pallas_call(
        layer_norm_kernel,
        grid=(rows // 32,),
        in_specs=[block, vector, vector],
        out_specs=block,
        out_shape=jax.ShapeDtypeStruct((rows, wide), jnp.bfloat16),
        compiler_params=pltpu.CompilerParams(vmem_limit_bytes=60 * 1024 * 1024),
        cost_estimate=pl.CostEstimate(flops=10 * rows * wide, bytes_accessed=4 * rows * wide, transcendentals=rows),
        name="layer_norm",
    )(values, mod_shift.reshape(1, wide), mod_scale.reshape(1, wide))


def rope_tables(positions):
    small_pairs = HD // 6
    time_pairs = (HD - 4 * small_pairs) // 2
    frame = (positions // (GRID_H * GRID_W)).astype(jnp.float32)
    row_pos = (positions // GRID_W % GRID_H).astype(jnp.float32)
    col_pos = (positions % GRID_W).astype(jnp.float32)
    time_freq = 10000.0 ** (-jnp.arange(time_pairs, dtype=jnp.float32) / time_pairs)
    space_freq = 10000.0 ** (-jnp.arange(small_pairs, dtype=jnp.float32) / small_pairs)
    freq = jnp.repeat(jnp.concatenate([time_freq, space_freq, space_freq]), 2)
    pair = jnp.arange(HD, dtype=jnp.int32) // 2
    where = jnp.where(
        pair < time_pairs,
        frame[:, None],
        jnp.where(pair < time_pairs + small_pairs, row_pos[:, None], col_pos[:, None]),
    )
    angles = where * freq
    sign = jnp.where(jnp.arange(HD) % 2 == 0, -1.0, 1.0).astype(jnp.float32)
    return jnp.cos(angles), jnp.sin(angles) * sign


def as_column(row):
    return jnp.broadcast_to(row, (BLK, BLK)).T


def as_row(column):
    return jnp.broadcast_to(column, (BLK, BLK)).T[0:1, :]


def inverse_norm(ssq_row):
    return as_column(lax.rsqrt(ssq_row * (1.0 / (H * HD)) + 1e-06))


def norm_rope(raw, inv, gain, cosine, sine):
    wide = raw.astype(jnp.float32) * inv * gain
    lane = lax.broadcasted_iota(jnp.int32, wide.shape, 1)
    partner = jnp.where(
        lane % 2 == 0, pltpu.roll(wide, HD - 1, 1), pltpu.roll(wide, 1, 1)
    )
    return (wide * cosine + partner * sine).astype(jnp.bfloat16)


def split3(row):
    hi = row.astype(jnp.bfloat16).astype(jnp.float32)
    rest = row - hi
    mid = rest.astype(jnp.bfloat16).astype(jnp.float32)
    return [hi, mid, rest - mid]


PER_STEP = 4
SLOTS = ((0, 0), (0, -1), (0, 1), (1, 0), (0, 2), (1, -1), (1, 1), (1, 2))
CHUNKS = (4, 3, 1)


def chip_move(dz, dx, dc):
    return [
        (z * 8 + x * 2 + c, (z + dz) % 2 * 8 + (x + dx) % 4 * 2 + (c + dc) % 2)
        for z in range(2)
        for x in range(4)
        for c in range(2)
    ]


def from_left(block):
    return lax.ppermute(block, "sy", chip_move(0, 1, 0))


def from_right(block):
    return lax.ppermute(block, "sy", chip_move(0, -1, 0))


def from_z(block):
    return lax.ppermute(block, "sy", chip_move(1, 0, 0))


def from_core(block):
    return lax.ppermute(block, "sy", chip_move(0, 0, 1))


ANYWHERE = pl.BlockSpec(memory_space=pltpu.HBM)
SMEM = pl.BlockSpec(memory_space=pltpu.SMEM)


def project_kernel(cuts, *refs):
    n = len(refs) - 7
    arrays, (own_w, other_w, own_ref, other_ref, ssq_ref, x_ref, sems) = refs[:n], refs[n:]

    @pl.when(pl.program_id(0) == 0)
    def _():
        copies, at = [], 0
        for i, (which, first, count) in enumerate(cuts):
            source = arrays[which].at[pl.ds(first, count)]
            copies.append(pltpu.make_async_copy(source, x_ref.at[pl.ds(at, count)], sems.at[i]))
            copies[-1].start()
            at += count
        for copy in copies:
            copy.wait()

    total = None
    for weight, out in ((own_w, own_ref), (other_w, other_ref)):
        made = jnp.dot(x_ref[...], weight[0], preferred_element_type=jnp.float32).astype(jnp.bfloat16)
        out[0] = made
        wide = made.astype(jnp.float32)
        part = jnp.sum(wide * wide, axis=-1, keepdims=True)
        total = part if total is None else total + part
    for i in range(x_ref.shape[0] // BLK):
        ssq_ref[0, i : i + 1, :] = as_row(total[i * BLK : (i + 1) * BLK])


def project(arrays, cuts, own_w, other_w):
    rows = sum(count for _, _, count in cuts)
    depth, wide = own_w.shape[1:]
    w_spec = pl.BlockSpec((1, depth, wide), lambda i: (i, 0, 0))
    o_spec = pl.BlockSpec((1, rows, wide), lambda i: (i, 0, 0))
    out = jax.ShapeDtypeStruct((3, rows, wide), jnp.bfloat16)
    return pl.pallas_call(
        functools.partial(project_kernel, cuts),
        grid=(3,),
        in_specs=[ANYWHERE] * len(arrays) + [w_spec, w_spec],
        out_specs=[o_spec, o_spec, pl.BlockSpec((1, rows // BLK, BLK), lambda i: (i, 0, 0))],
        out_shape=[out, out, jax.ShapeDtypeStruct((3, rows // BLK, BLK), jnp.float32)],
        scratch_shapes=[pltpu.VMEM((rows, depth), jnp.bfloat16), pltpu.SemaphoreType.DMA((len(cuts),))],
        compiler_params=pltpu.CompilerParams(
            dimension_semantics=("arbitrary",), vmem_limit_bytes=26 * 1024 * 1024
        ),
        cost_estimate=pl.CostEstimate(
            flops=12 * rows * depth * wide, bytes_accessed=12 * depth * wide, transcendentals=0
        ),
        name="project",
    )(*arrays, own_w, other_w)


def cut_kernel(cuts, *refs):
    n = len(cuts)
    copies = [
        pltpu.make_async_copy(refs[i].at[pl.ds(first, count)], refs[n + i], refs[2 * n].at[i])
        for i, (first, count) in enumerate(cuts)
    ]
    for copy in copies:
        copy.start()
    for copy in copies:
        copy.wait()


def cut(arrays, cuts):
    return pl.pallas_call(
        functools.partial(cut_kernel, cuts),
        in_specs=[ANYWHERE] * len(cuts),
        out_specs=[ANYWHERE] * len(cuts),
        out_shape=[jax.ShapeDtypeStruct((count, a.shape[1]), a.dtype) for a, (_, count) in zip(arrays, cuts)],
        scratch_shapes=[pltpu.SemaphoreType.DMA((len(cuts),))],
        cost_estimate=pl.CostEstimate(flops=10**5, bytes_accessed=3 * 10**6, transcendentals=0),
        name="cut_rows",
    )(*arrays)


def sources(refs):
    at = 0
    for chunk, slots in enumerate(CHUNKS):
        for i in range(slots):
            for core in range(2):
                yield (at + i) * 2 + core, refs[chunk * 2 + core], pl.ds(i * BLK, BLK)
        at += slots


def halo_kernel(
    place_ref, fa, ga, fb, gb, fc, gc, ssq_ref, gk_ref, cos_lo, sin_lo, cos_hi, sin_hi,
    before_ref, after_ref, raw, sems,
):
    blocks = 2 * sum(CHUNKS)
    ends = ((lambda n: n >= blocks - ROUNDS, blocks - ROUNDS, 0), (lambda n: n < ROUNDS, 0, 1))

    def each(act):
        for at, ref, rows in sources((fa, ga, fb, gb, fc, gc)):
            n = place_ref[at]
            for inside, first, head in ends:

                @pl.when(inside(n))
                def _(n=n, first=first, head=head, ref=ref, rows=rows, at=at):
                    to = pl.ds(pl.multiple_of((n - first) * BLK, BLK), BLK)
                    cols = pl.ds(head * HD, HD)
                    out = (before_ref, after_ref)[head]
                    act(pltpu.make_async_copy(ref.at[0, rows, cols], raw.at[head, to], sems.at[at, 0]))
                    act(pltpu.make_async_copy(ref.at[2, rows, cols], out.at[to, pl.ds(HD, HD)], sems.at[at, 1]))

    each(lambda copy: copy.start())
    each(lambda copy: copy.wait())
    for head, out, first, cosine, sine in (
        (0, before_ref, blocks - ROUNDS, cos_hi, sin_hi),
        (1, after_ref, 0, cos_lo, sin_lo),
    ):
        for i in range(ROUNDS):
            rows = pl.ds(i * BLK, BLK)
            out[rows, 0:HD] = norm_rope(
                raw[head, rows, :], inverse_norm(ssq_ref[pl.ds(first + i, 1), :]),
                gk_ref[:, head * HD : (head + 1) * HD],
                cosine[rows, :], sine[rows, :],
            )


def halo(place, features, ssq_k, gk, cosine, sine):
    rows = cosine.shape[0]
    low = pl.BlockSpec((HALO, HD), lambda i: (0, 0))
    high = pl.BlockSpec((HALO, HD), lambda i: (rows // HALO - 1, 0))
    one = lambda a: pl.BlockSpec(a.shape, lambda i: (0, 0))
    out = jax.ShapeDtypeStruct((HALO, 2 * HD), jnp.bfloat16)
    return pl.pallas_call(
        halo_kernel,
        grid=(1,),
        in_specs=[SMEM] + [ANYWHERE] * 6 + [one(ssq_k), one(gk), low, low, high, high],
        out_specs=[pl.BlockSpec((HALO, 2 * HD), lambda i: (0, 0))] * 2,
        out_shape=[out, out],
        scratch_shapes=[
            pltpu.VMEM((2, HALO, HD), jnp.bfloat16),
            pltpu.SemaphoreType.DMA((2 * sum(CHUNKS), 2)),
        ],
        compiler_params=pltpu.CompilerParams(vmem_limit_bytes=16 * 1024 * 1024),
        cost_estimate=pl.CostEstimate(flops=10**7, bytes_accessed=3 * 10**6, transcendentals=0),
        name="halo_keys",
    )(place, *features, ssq_k, gk, cosine, sine, cosine, sine)


def attention_kernel(
    part, place_ref, fa, ga, fb, gb, fc, gc, before_ref, after_ref, sk_ref, sq_ref,
    gk_ref, gq_ref, cos_ref, sin_ref, *rest,
):
    out_ref, raw, kbuf, vbuf, sems = rest[-5:]
    step, head = pl.program_id(0), pl.program_id(1)
    blocks = 2 * sum(CHUNKS)
    columns = [slice(head * HD, (head + 1) * HD) for head in range(2)]
    own_first = (ROUNDS, 0)

    def guarded(condition, act):
        if condition is None:
            act()
        else:
            pl.when(condition)(act)

    @pl.when((step == 0) & (head == 0))
    def _():
        copies = []
        for at, ref, rows in sources((fa, ga, fb, gb, fc, gc)):
            n = place_ref[at]
            to = pl.ds(pl.multiple_of(n * BLK, BLK), BLK)
            needed = None if part == 0 else (n < ROUNDS) | (n >= blocks - ROUNDS)
            copies.append((n, needed, pltpu.make_async_copy(ref.at[:, rows], raw.at[:, to], sems.at[at])))
        for _, needed, copy in copies:
            guarded(needed, copy.start)
        if part == 1:
            for head, ref in enumerate((before_ref, after_ref)):
                to = pl.ds((0, blocks)[head] * BLK, HALO)
                kbuf[head, to, :] = ref[:, 0:HD]
                vbuf[head, :, to] = ref[:, HD:].T
        for n, needed, copy in copies:
            guarded(needed, copy.wait)

        for n in range(blocks):
            heads = [head for head in range(2) if part == 0 or (n < ROUNDS, n >= blocks - ROUNDS)[head]]
            rows = slice(n * BLK, (n + 1) * BLK)
            inv = inverse_norm(sk_ref[n : n + 1, :]) if heads else None
            for head in heads:
                to = slice((n + own_first[head]) * BLK, (n + own_first[head] + 1) * BLK)
                kbuf[head, to, :] = norm_rope(
                    raw[0, rows, columns[head]], inv, gk_ref[:, columns[head]], cos_ref[rows, :], sin_ref[rows, :]
                )
                vbuf[head, :, to] = raw[2, rows, columns[head]].T

    def attend(first, head):
        for j in range(PER_STEP):
            b = first + j
            rows = pl.ds(pl.multiple_of(b * BLK, BLK), BLK)
            window = pl.ds(pl.multiple_of(b * BLK, BLK), (ROUNDS + 1) * BLK)
            q = norm_rope(
                raw[1, rows, columns[head]], inverse_norm(sq_ref[pl.ds(b, 1), :]), gq_ref[:, columns[head]],
                cos_ref[rows, :], sin_ref[rows, :],
            )
            scores = lax.dot_general(
                kbuf[head, window, :], q, (((1,), (1,)), ((), ())), preferred_element_type=jnp.float32
            )
            top = jnp.max(scores, axis=0, keepdims=True)
            weight = jnp.exp2((scores - top) * (SCALE * LOG2E))
            total = jnp.sum(weight, axis=0, keepdims=True)
            mixed = jnp.dot(
                vbuf[head, :, window], weight.astype(jnp.bfloat16), preferred_element_type=jnp.float32
            )
            out_ref[j, 0, 0:BLK, :] = (mixed / total).T.astype(jnp.bfloat16)
            stats = split3(top * SCALE) + split3(total) + [jnp.zeros((EXTRA - 6, HD), jnp.float32)]
            out_ref[j, 0, BLK : BLK + EXTRA, :] = jnp.concatenate(stats, axis=0).astype(jnp.bfloat16)

    for which in range(2):
        first = (step + 1 - which) * PER_STEP if part == 0 else (0, blocks - ROUNDS)[which]
        pl.when(head == which)(functools.partial(attend, first, which))


def attention(part, place, features, before, after, sk, sq, gk, gq, cosine, sine, held=None):
    rows = cosine.shape[0]
    blocks = rows // BLK
    whole = lambda a: pl.BlockSpec(a.shape, lambda i, h, n=a.ndim: (0,) * n)
    steps = blocks // PER_STEP - 1 if part == 0 else 1
    which = (lambda i, h: (i + 1 - h, h, 0, 0)) if part == 0 else (lambda i, h: (h * (blocks // PER_STEP - 1), h, 0, 0))
    small = (before, after, sk, sq, gk, gq, cosine, sine)
    more = () if held is None else (held,)
    return pl.pallas_call(
        functools.partial(attention_kernel, part),
        grid=(steps, 2),
        in_specs=[SMEM] + [ANYWHERE] * 6 + [whole(a) for a in small] + [ANYWHERE] * len(more),
        out_specs=pl.BlockSpec((PER_STEP, 1, BLK + EXTRA, HD), which),
        out_shape=jax.ShapeDtypeStruct((blocks, 2, BLK + EXTRA, HD), jnp.bfloat16),
        scratch_shapes=[
            pltpu.VMEM((3, rows, 2 * HD), jnp.bfloat16),
            pltpu.VMEM((2, rows + HALO, HD), jnp.bfloat16),
            pltpu.VMEM((2, HD, rows + HALO), jnp.bfloat16),
            pltpu.SemaphoreType.DMA((blocks,)),
        ],
        input_output_aliases={15: 0} if more else {},
        compiler_params=pltpu.CompilerParams(
            dimension_semantics=("arbitrary", "arbitrary"), vmem_limit_bytes=24 * 1024 * 1024
        ),
        cost_estimate=pl.CostEstimate(
            flops=(1 + 2 * (1 - part)) * 5 * 10**8, bytes_accessed=10**7, transcendentals=10**6
        ),
        name=("window_attention", "window_attention_halo")[part],
    )(place, *features, *small, *more)


def along_sx(block, distance):
    n = lax.axis_size("sx")
    return lax.ppermute(block, "sx", [((i - distance) % n, i) for i in range(n)])


def unpack(arrived):
    attended = arrived[:, :, :BLK].transpose(2, 0, 1, 3).reshape(BLK, H * HD)
    stats = arrived[:, :, BLK : BLK + 6].astype(jnp.float32)
    best = (stats[:, :, 0] + stats[:, :, 1]) + stats[:, :, 2]
    total = (stats[:, :, 3] + stats[:, :, 4]) + stats[:, :, 5]
    return attended, best.reshape(H, BLK), total.reshape(H, BLK)


def body(tokens, mod_shift, mod_scale, w_query, w_key, w_value, query_gain, key_gain):
    group = lax.axis_index("sx")
    mine = lax.axis_index("sy")
    z, x, core = mine // 8, mine // 2 % 4, mine % 2
    chips = jnp.stack([(z + dz) % 2 * 4 + (x + dx) % 4 for dz, dx in SLOTS])
    place = jnp.stack([chips * 2 + core, chips * 2 + 1 - core], axis=1).reshape(-1).astype(jnp.int32)
    rows = BLK * lax.axis_size("sy")
    barrier = lax.optimization_barrier

    own = layer_norm(tokens, mod_shift, mod_scale)
    left, right, beside = from_left(own), from_right(own), from_z(own)
    key_w, query_w, value_w = barrier((w_key, w_query, w_value, own))[:3]
    own_w, sent_w = jnp.stack([key_w, query_w, value_w]), jnp.stack([value_w, query_w, key_w])
    cosine, sine = rope_tables(group * rows + jnp.arange(rows, dtype=jnp.int32))
    gq = lax.dynamic_slice(query_gain, (mine * 2 * HD,), (2 * HD,)).reshape(1, 2 * HD)
    gk = lax.dynamic_slice(key_gain, (mine * 2 * HD,), (2 * HD,)).reshape(1, 2 * HD)
    (left, right, beside), own_w, sent_w, (cosine, sine, gq, gk, place) = barrier(
        ((left, right, beside), own_w, sent_w, (cosine, sine, gq, gk, place))
    )

    far, z_right, z_left = from_left(left), from_right(beside), from_z(left)
    other_w = lax.rev(from_core(sent_w), (0,))
    near = project((own, left, right, beside), tuple((i, 0, BLK) for i in range(4)), own_w, other_w)
    near, far, z_right, z_left = barrier((near, far, z_right, z_left))

    part_left, part_right, part_z = cut((z_left, z_right, far), ((0, 48), (48, 48), (96, 32)))
    z_far = (from_left(part_left), from_right(part_right), from_z(part_z))
    middle = project((far, z_left, z_right), tuple((i, 0, BLK) for i in range(3)), own_w, other_w)
    z_far, middle = barrier((z_far, middle))
    last = project(z_far, tuple((i, 0, p.shape[0]) for i, p in enumerate(z_far)), own_w, other_w)

    features, parts = [], []
    for made, given, part in (near, middle, last):
        features += [made, from_core(given)]
        parts.append(part[:2])
    part = jnp.concatenate(parts, axis=1)
    here = chips[:, None] == jnp.arange(8)[None, :]
    part = jnp.sum(jnp.where(here[None, :, :, None], part[:, :, None, :], 0.0), axis=1)
    sent = jnp.broadcast_to(part.reshape(1, 16, BLK), (NSY, 16, BLK))
    seen = lax.all_to_all(sent, "sy", split_axis=0, concat_axis=0, tiled=True)
    ssq = jnp.sum(seen.reshape(8, 2, 2, 8, BLK), axis=0).transpose(1, 2, 0, 3).reshape(2, 16, BLK)
    before, after = halo(place, features, ssq[0], gk, cosine, sine)
    common = (ssq[0], ssq[1], gk, gq, cosine, sine)
    out = attention(0, place, features, before, after, *common)
    before, after = along_sx(before, 1), along_sx(after, -1)
    out = attention(1, place, features, before, after, *common, held=out)
    arrived = lax.all_to_all(out, "sy", split_axis=0, concat_axis=0, tiled=True)
    return unpack(arrived)


def solution(mesh):
    placed = (
        P(("sx", "sy"), None),
        P(),
        P(),
        P(None, "sy"),
        P(None, "sy"),
        P(None, "sy"),
        P(),
        P(),
    )
    return jax.shard_map(
        body,
        mesh=mesh,
        in_specs=placed,
        out_specs=(P(("sx", "sy"), None), P(None, ("sx", "sy")), P(None, ("sx", "sy"))),
        check_vma=False,
    )
```

```python
import functools

import jax
import jax.numpy as jnp
import numpy as np
from jax import lax
from jax.experimental import pallas as pl
from jax.experimental.pallas import tpu as pltpu
from jax.sharding import PartitionSpec as P

H = 32
HD = 128
ROUNDS = 4
GRID_W = 80
GRID_H = 45
BLK = 128
HALO = ROUNDS * BLK
EXTRA = 16
NSY = 16
SCALE = np.float32(1.0) / np.sqrt(np.float32(HD))
LOG2E = np.float32(1.4426950408889634)


def layer_norm_kernel(tokens_ref, shift_ref, scale_ref, out_ref):
    wide = tokens_ref[...].astype(jnp.float32)
    center = jnp.mean(wide, axis=-1, keepdims=True)
    apart = wide - center
    spread = jnp.mean(apart * apart, axis=-1, keepdims=True)
    scaled = apart * lax.rsqrt(spread + 1e-06)
    out_ref[...] = (scaled * (1.0 + scale_ref[...]) + shift_ref[...]).astype(jnp.bfloat16)


def layer_norm(values, mod_shift, mod_scale):
    rows, wide = values.shape
    block = pl.BlockSpec((64, wide), lambda i: (i, 0))
    vector = pl.BlockSpec((1, wide), lambda i: (0, 0))
    return pl.pallas_call(
        layer_norm_kernel,
        grid=(rows // 64,),
        in_specs=[block, vector, vector],
        out_specs=block,
        out_shape=jax.ShapeDtypeStruct((rows, wide), jnp.bfloat16),
        compiler_params=pltpu.CompilerParams(vmem_limit_bytes=60 * 1024 * 1024),
        cost_estimate=pl.CostEstimate(flops=10 * rows * wide, bytes_accessed=4 * rows * wide, transcendentals=rows),
        name="layer_norm",
    )(values, mod_shift.reshape(1, wide), mod_scale.reshape(1, wide))


def rope_tables(positions):
    small_pairs = HD // 6
    time_pairs = (HD - 4 * small_pairs) // 2
    frame = (positions // (GRID_H * GRID_W)).astype(jnp.float32)
    row_pos = (positions // GRID_W % GRID_H).astype(jnp.float32)
    col_pos = (positions % GRID_W).astype(jnp.float32)
    time_freq = 10000.0 ** (-jnp.arange(time_pairs, dtype=jnp.float32) / time_pairs)
    space_freq = 10000.0 ** (-jnp.arange(small_pairs, dtype=jnp.float32) / small_pairs)
    freq = jnp.repeat(jnp.concatenate([time_freq, space_freq, space_freq]), 2)
    pair = jnp.arange(HD, dtype=jnp.int32) // 2
    where = jnp.where(
        pair < time_pairs,
        frame[:, None],
        jnp.where(pair < time_pairs + small_pairs, row_pos[:, None], col_pos[:, None]),
    )
    angles = where * freq
    sign = jnp.where(jnp.arange(HD) % 2 == 0, -1.0, 1.0).astype(jnp.float32)
    return jnp.cos(angles), jnp.sin(angles) * sign


def as_column(row):
    return jnp.broadcast_to(row, (BLK, BLK)).T


def as_row(column):
    return jnp.broadcast_to(column, (BLK, BLK)).T[0:1, :]


def inverse_norm(ssq_row):
    return as_column(lax.rsqrt(ssq_row * (1.0 / (H * HD)) + 1e-06))


def norm_rope(raw, inv, gain, cosine, sine):
    wide = raw.astype(jnp.float32) * inv * gain
    lane = lax.broadcasted_iota(jnp.int32, wide.shape, 1)
    partner = jnp.where(
        lane % 2 == 0, pltpu.roll(wide, HD - 1, 1), pltpu.roll(wide, 1, 1)
    )
    return (wide * cosine + partner * sine).astype(jnp.bfloat16)


def split3(row):
    hi = row.astype(jnp.bfloat16).astype(jnp.float32)
    rest = row - hi
    mid = rest.astype(jnp.bfloat16).astype(jnp.float32)
    return [hi, mid, rest - mid]


PER_STEP = 4
SLOTS = ((0, 0), (0, -1), (0, 1), (1, 0), (0, 2), (1, -1), (1, 1), (1, 2))
CHUNKS = (4, 3, 1)


def chip_move(dz, dx, dc):
    return [
        (z * 8 + x * 2 + c, (z + dz) % 2 * 8 + (x + dx) % 4 * 2 + (c + dc) % 2)
        for z in range(2)
        for x in range(4)
        for c in range(2)
    ]


def from_left(block):
    return lax.ppermute(block, "sy", chip_move(0, 1, 0))


def from_right(block):
    return lax.ppermute(block, "sy", chip_move(0, -1, 0))


def from_z(block):
    return lax.ppermute(block, "sy", chip_move(1, 0, 0))


def from_core(block):
    return lax.ppermute(block, "sy", chip_move(0, 0, 1))


ANYWHERE = pl.BlockSpec(memory_space=pltpu.HBM)
SMEM = pl.BlockSpec(memory_space=pltpu.SMEM)


def project_kernel(cuts, *refs):
    n = len(refs) - 7
    arrays, (own_w, other_w, own_ref, other_ref, ssq_ref, x_ref, sems) = refs[:n], refs[n:]

    @pl.when(pl.program_id(0) == 0)
    def _():
        copies, at = [], 0
        for i, (which, first, count) in enumerate(cuts):
            source = arrays[which].at[pl.ds(first, count)]
            copies.append(pltpu.make_async_copy(source, x_ref.at[pl.ds(at, count)], sems.at[i]))
            copies[-1].start()
            at += count
        for copy in copies:
            copy.wait()

    total = None
    for weight, out in ((own_w, own_ref), (other_w, other_ref)):
        made = jnp.dot(x_ref[...], weight[0], preferred_element_type=jnp.float32).astype(jnp.bfloat16)
        out[0] = made
        wide = made.astype(jnp.float32)
        part = jnp.sum(wide * wide, axis=-1, keepdims=True)
        total = part if total is None else total + part
    for i in range(x_ref.shape[0] // BLK):
        ssq_ref[0, i : i + 1, :] = as_row(total[i * BLK : (i + 1) * BLK])


def project(arrays, cuts, own_w, other_w):
    rows = sum(count for _, _, count in cuts)
    depth, wide = own_w.shape[1:]
    w_spec = pl.BlockSpec((1, depth, wide), lambda i: (i, 0, 0))
    o_spec = pl.BlockSpec((1, rows, wide), lambda i: (i, 0, 0))
    out = jax.ShapeDtypeStruct((3, rows, wide), jnp.bfloat16)
    return pl.pallas_call(
        functools.partial(project_kernel, cuts),
        grid=(3,),
        in_specs=[ANYWHERE] * len(arrays) + [w_spec, w_spec],
        out_specs=[o_spec, o_spec, pl.BlockSpec((1, rows // BLK, BLK), lambda i: (i, 0, 0))],
        out_shape=[out, out, jax.ShapeDtypeStruct((3, rows // BLK, BLK), jnp.float32)],
        scratch_shapes=[pltpu.VMEM((rows, depth), jnp.bfloat16), pltpu.SemaphoreType.DMA((len(cuts),))],
        compiler_params=pltpu.CompilerParams(
            dimension_semantics=("arbitrary",), vmem_limit_bytes=26 * 1024 * 1024
        ),
        cost_estimate=pl.CostEstimate(
            flops=12 * rows * depth * wide, bytes_accessed=12 * depth * wide, transcendentals=0
        ),
        name="project",
    )(*arrays, own_w, other_w)


def cut_kernel(*refs):
    n = len(refs) // 2
    for source, out in zip(refs[:n], refs[n:]):
        out[...] = source[...]


def cut(arrays, cuts):
    wide = arrays[0].shape[1]
    return pl.pallas_call(
        cut_kernel,
        grid=(1,),
        in_specs=[pl.BlockSpec((count, wide), lambda i, first=first: (first, 0)) for first, count in cuts],
        out_specs=[pl.BlockSpec((count, wide), lambda i: (0, 0)) for _, count in cuts],
        out_shape=[jax.ShapeDtypeStruct((count, wide), jnp.bfloat16) for _, count in cuts],
        compiler_params=pltpu.CompilerParams(vmem_limit_bytes=10 * 1024 * 1024),
        cost_estimate=pl.CostEstimate(flops=10**5, bytes_accessed=3 * 10**6, transcendentals=0),
        name="cut_rows",
    )(*arrays)


def sources(refs):
    at = 0
    for chunk, slots in enumerate(CHUNKS):
        for i in range(slots):
            for core in range(2):
                yield (at + i) * 2 + core, refs[chunk * 2 + core], pl.ds(i * BLK, BLK)
        at += slots


def halo_kernel(
    place_ref, fa, ga, fb, gb, fc, gc, ssq_ref, gk_ref, cos_lo, sin_lo, cos_hi, sin_hi,
    before_ref, after_ref, raw, sems,
):
    blocks = 2 * sum(CHUNKS)
    ends = ((lambda n: n >= blocks - ROUNDS, blocks - ROUNDS, 0), (lambda n: n < ROUNDS, 0, 1))

    def each(act):
        for at, ref, rows in sources((fa, ga, fb, gb, fc, gc)):
            n = place_ref[at]
            for inside, first, head in ends:

                @pl.when(inside(n))
                def _(n=n, first=first, head=head, ref=ref, rows=rows, at=at):
                    to = pl.ds(pl.multiple_of((n - first) * BLK, BLK), BLK)
                    cols = pl.ds(head * HD, HD)
                    out = (before_ref, after_ref)[head]
                    act(pltpu.make_async_copy(ref.at[0, rows, cols], raw.at[head, to], sems.at[at, 0]))
                    act(pltpu.make_async_copy(ref.at[2, rows, cols], out.at[to, pl.ds(HD, HD)], sems.at[at, 1]))

    each(lambda copy: copy.start())
    each(lambda copy: copy.wait())
    for head, out, first, cosine, sine in (
        (0, before_ref, blocks - ROUNDS, cos_hi, sin_hi),
        (1, after_ref, 0, cos_lo, sin_lo),
    ):
        for i in range(ROUNDS):
            rows = pl.ds(i * BLK, BLK)
            out[rows, 0:HD] = norm_rope(
                raw[head, rows, :], inverse_norm(ssq_ref[pl.ds(first + i, 1), :]),
                gk_ref[:, head * HD : (head + 1) * HD],
                cosine[rows, :], sine[rows, :],
            )


def halo(place, features, ssq_k, gk, cosine, sine):
    rows = cosine.shape[0]
    low = pl.BlockSpec((HALO, HD), lambda i: (0, 0))
    high = pl.BlockSpec((HALO, HD), lambda i: (rows // HALO - 1, 0))
    one = lambda a: pl.BlockSpec(a.shape, lambda i: (0, 0))
    out = jax.ShapeDtypeStruct((HALO, 2 * HD), jnp.bfloat16)
    return pl.pallas_call(
        halo_kernel,
        grid=(1,),
        in_specs=[SMEM] + [ANYWHERE] * 6 + [one(ssq_k), one(gk), low, low, high, high],
        out_specs=[pl.BlockSpec((HALO, 2 * HD), lambda i: (0, 0))] * 2,
        out_shape=[out, out],
        scratch_shapes=[
            pltpu.VMEM((2, HALO, HD), jnp.bfloat16),
            pltpu.SemaphoreType.DMA((2 * sum(CHUNKS), 2)),
        ],
        compiler_params=pltpu.CompilerParams(vmem_limit_bytes=16 * 1024 * 1024),
        cost_estimate=pl.CostEstimate(flops=10**7, bytes_accessed=3 * 10**6, transcendentals=0),
        name="halo_keys",
    )(place, *features, ssq_k, gk, cosine, sine, cosine, sine)


def attention_kernel(
    part, place_ref, fa, ga, fb, gb, fc, gc, before_ref, after_ref, sk_ref, sq_ref,
    gk_ref, gq_ref, cos_ref, sin_ref, *rest,
):
    out_ref, raw, kbuf, vbuf, sems = rest[-5:]
    step, head = pl.program_id(0), pl.program_id(1)
    blocks = 2 * sum(CHUNKS)
    columns = [slice(head * HD, (head + 1) * HD) for head in range(2)]
    own_first = (ROUNDS, 0)

    def guarded(condition, act):
        if condition is None:
            act()
        else:
            pl.when(condition)(act)

    @pl.when((step == 0) & (head == 0))
    def _():
        copies = []
        for at, ref, rows in sources((fa, ga, fb, gb, fc, gc)):
            n = place_ref[at]
            to = pl.ds(pl.multiple_of(n * BLK, BLK), BLK)
            needed = None if part == 0 else (n < ROUNDS) | (n >= blocks - ROUNDS)
            copies.append((n, needed, pltpu.make_async_copy(ref.at[:, rows], raw.at[:, to], sems.at[at])))
        for _, needed, copy in copies:
            guarded(needed, copy.start)
        if part == 1:
            for head, ref in enumerate((before_ref, after_ref)):
                to = pl.ds((0, blocks)[head] * BLK, HALO)
                kbuf[head, to, :] = ref[:, 0:HD]
                vbuf[head, :, to] = ref[:, HD:].T
        for n, needed, copy in copies:
            guarded(needed, copy.wait)

        for n in range(blocks):
            heads = [head for head in range(2) if part == 0 or (n < ROUNDS, n >= blocks - ROUNDS)[head]]
            rows = slice(n * BLK, (n + 1) * BLK)
            inv = inverse_norm(sk_ref[n : n + 1, :]) if heads else None
            for head in heads:
                to = slice((n + own_first[head]) * BLK, (n + own_first[head] + 1) * BLK)
                kbuf[head, to, :] = norm_rope(
                    raw[0, rows, columns[head]], inv, gk_ref[:, columns[head]], cos_ref[rows, :], sin_ref[rows, :]
                )
                vbuf[head, :, to] = raw[2, rows, columns[head]].T

    def attend(first, head):
        for j in range(PER_STEP):
            b = first + j
            rows = pl.ds(pl.multiple_of(b * BLK, BLK), BLK)
            window = pl.ds(pl.multiple_of(b * BLK, BLK), (ROUNDS + 1) * BLK)
            q = norm_rope(
                raw[1, rows, columns[head]], inverse_norm(sq_ref[pl.ds(b, 1), :]), gq_ref[:, columns[head]],
                cos_ref[rows, :], sin_ref[rows, :],
            )
            scores = lax.dot_general(
                kbuf[head, window, :], q, (((1,), (1,)), ((), ())), preferred_element_type=jnp.float32
            )
            top = jnp.max(scores, axis=0, keepdims=True)
            weight = jnp.exp2((scores - top) * (SCALE * LOG2E))
            total = jnp.sum(weight, axis=0, keepdims=True)
            mixed = jnp.dot(
                vbuf[head, :, window], weight.astype(jnp.bfloat16), preferred_element_type=jnp.float32
            )
            out_ref[j, 0, 0:BLK, :] = (mixed / total).T.astype(jnp.bfloat16)
            stats = split3(top * SCALE) + split3(total) + [jnp.zeros((EXTRA - 6, HD), jnp.float32)]
            out_ref[j, 0, BLK : BLK + EXTRA, :] = jnp.concatenate(stats, axis=0).astype(jnp.bfloat16)

    for which in range(2):
        first = (step + 1 - which) * PER_STEP if part == 0 else (0, blocks - ROUNDS)[which]
        pl.when(head == which)(functools.partial(attend, first, which))


def attention(part, place, features, before, after, sk, sq, gk, gq, cosine, sine, held=None):
    rows = cosine.shape[0]
    blocks = rows // BLK
    whole = lambda a: pl.BlockSpec(a.shape, lambda i, h, n=a.ndim: (0,) * n)
    steps = blocks // PER_STEP - 1 if part == 0 else 1
    which = (lambda i, h: (i + 1 - h, h, 0, 0)) if part == 0 else (lambda i, h: (h * (blocks // PER_STEP - 1), h, 0, 0))
    small = (before, after, sk, sq, gk, gq, cosine, sine)
    more = () if held is None else (held,)
    return pl.pallas_call(
        functools.partial(attention_kernel, part),
        grid=(steps, 2),
        in_specs=[SMEM] + [ANYWHERE] * 6 + [whole(a) for a in small] + [ANYWHERE] * len(more),
        out_specs=pl.BlockSpec((PER_STEP, 1, BLK + EXTRA, HD), which),
        out_shape=jax.ShapeDtypeStruct((blocks, 2, BLK + EXTRA, HD), jnp.bfloat16),
        scratch_shapes=[
            pltpu.VMEM((3, rows, 2 * HD), jnp.bfloat16),
            pltpu.VMEM((2, rows + HALO, HD), jnp.bfloat16),
            pltpu.VMEM((2, HD, rows + HALO), jnp.bfloat16),
            pltpu.SemaphoreType.DMA((blocks,)),
        ],
        input_output_aliases={15: 0} if more else {},
        compiler_params=pltpu.CompilerParams(
            dimension_semantics=("arbitrary", "arbitrary"), vmem_limit_bytes=24 * 1024 * 1024
        ),
        cost_estimate=pl.CostEstimate(
            flops=(1 + 2 * (1 - part)) * 5 * 10**8, bytes_accessed=10**7, transcendentals=10**6
        ),
        name=("window_attention", "window_attention_halo")[part],
    )(place, *features, *small, *more)


def along_sx(block, distance):
    n = lax.axis_size("sx")
    return lax.ppermute(block, "sx", [((i - distance) % n, i) for i in range(n)])


def unpack(arrived):
    attended = arrived[:, :, :BLK].transpose(2, 0, 1, 3).reshape(BLK, H * HD)
    stats = arrived[:, :, BLK : BLK + 6].astype(jnp.float32)
    best = (stats[:, :, 0] + stats[:, :, 1]) + stats[:, :, 2]
    total = (stats[:, :, 3] + stats[:, :, 4]) + stats[:, :, 5]
    return attended, best.reshape(H, BLK), total.reshape(H, BLK)


def body(tokens, mod_shift, mod_scale, w_query, w_key, w_value, query_gain, key_gain):
    group = lax.axis_index("sx")
    mine = lax.axis_index("sy")
    z, x, core = mine // 8, mine // 2 % 4, mine % 2
    chips = jnp.stack([(z + dz) % 2 * 4 + (x + dx) % 4 for dz, dx in SLOTS])
    place = jnp.stack([chips * 2 + core, chips * 2 + 1 - core], axis=1).reshape(-1).astype(jnp.int32)
    rows = BLK * lax.axis_size("sy")
    barrier = lax.optimization_barrier

    own = layer_norm(tokens, mod_shift, mod_scale)
    left, right, beside = from_left(own), from_right(own), from_z(own)
    key_w, query_w, value_w = barrier((w_key, w_query, w_value, own))[:3]
    one = barrier(jnp.bfloat16(1))
    sent_w = jnp.stack([key_w, query_w, value_w])
    own_w = sent_w * one
    cosine, sine = rope_tables(group * rows + jnp.arange(rows, dtype=jnp.int32))
    gq = lax.dynamic_slice(query_gain, (mine * 2 * HD,), (2 * HD,)).reshape(1, 2 * HD)
    gk = lax.dynamic_slice(key_gain, (mine * 2 * HD,), (2 * HD,)).reshape(1, 2 * HD)
    (left, right, beside), own_w, sent_w, (cosine, sine, gq, gk, place) = barrier(
        ((left, right, beside), own_w, sent_w, (cosine, sine, gq, gk, place))
    )

    far, z_right, z_left = from_left(left), from_right(beside), from_z(left)
    other_w = from_core(sent_w) * one
    near = project((own, left, right, beside), tuple((i, 0, BLK) for i in range(4)), own_w, other_w)
    near, far, z_right, z_left = barrier((near, far, z_right, z_left))

    part_left, part_right, part_z = cut((z_left, z_right, far), ((0, 48), (1, 48), (3, 32)))
    z_far = (from_left(part_left), from_right(part_right), from_z(part_z))
    middle = project((far, z_left, z_right), tuple((i, 0, BLK) for i in range(3)), own_w, other_w)
    z_far, middle = barrier((z_far, middle))
    last = project(z_far, tuple((i, 0, p.shape[0]) for i, p in enumerate(z_far)), own_w, other_w)

    features, parts = [], []
    for made, given, part in (near, middle, last):
        features += [made, from_core(given)]
        parts.append(part[:2])
    part = jnp.concatenate(parts, axis=1)
    here = chips[:, None] == jnp.arange(8)[None, :]
    part = jnp.sum(jnp.where(here[None, :, :, None], part[:, :, None, :], 0.0), axis=1)
    sent = jnp.broadcast_to(part.reshape(1, 16, BLK), (NSY, 16, BLK))
    seen = lax.all_to_all(sent, "sy", split_axis=0, concat_axis=0, tiled=True)
    ssq = jnp.sum(seen.reshape(8, 2, 2, 8, BLK), axis=0).transpose(1, 2, 0, 3).reshape(2, 16, BLK)
    before, after = halo(place, features, ssq[0], gk, cosine, sine)
    common = (ssq[0], ssq[1], gk, gq, cosine, sine)
    out = attention(0, place, features, before, after, *common)
    before, after = along_sx(before, 1), along_sx(after, -1)
    out = attention(1, place, features, before, after, *common, held=out)
    arrived = lax.all_to_all(out, "sy", split_axis=0, concat_axis=0, tiled=True)
    return unpack(arrived)


def solution(mesh):
    placed = (
        P(("sx", "sy"), None),
        P(),
        P(),
        P(None, "sy"),
        P(None, "sy"),
        P(None, "sy"),
        P(),
        P(),
    )
    return jax.shard_map(
        body,
        mesh=mesh,
        in_specs=placed,
        out_specs=(P(("sx", "sy"), None), P(None, ("sx", "sy")), P(None, ("sx", "sy"))),
        check_vma=False,
    )
```

```python
import functools

import jax
import jax.numpy as jnp
import numpy as np
from jax import lax
from jax.experimental import pallas as pl
from jax.experimental.pallas import tpu as pltpu
from jax.sharding import PartitionSpec as P

H = 32
HD = 128
ROUNDS = 4
GRID_W = 80
GRID_H = 45
BLK = 128
HALO = ROUNDS * BLK
EXTRA = 16
NSY = 16
SCALE = np.float32(1.0) / np.sqrt(np.float32(HD))
LOG2E = np.float32(1.4426950408889634)


def layer_norm_kernel(tokens_ref, shift_ref, scale_ref, out_ref):
    wide = tokens_ref[...].astype(jnp.float32)
    center = jnp.mean(wide, axis=-1, keepdims=True)
    apart = wide - center
    spread = jnp.mean(apart * apart, axis=-1, keepdims=True)
    scaled = apart * lax.rsqrt(spread + 1e-06)
    out_ref[...] = (scaled * (1.0 + scale_ref[...]) + shift_ref[...]).astype(jnp.bfloat16)


def layer_norm(values, mod_shift, mod_scale):
    rows, wide = values.shape
    block = pl.BlockSpec((64, wide), lambda i: (i, 0))
    vector = pl.BlockSpec((1, wide), lambda i: (0, 0))
    return pl.pallas_call(
        layer_norm_kernel,
        grid=(rows // 64,),
        in_specs=[block, vector, vector],
        out_specs=block,
        out_shape=jax.ShapeDtypeStruct((rows, wide), jnp.bfloat16),
        compiler_params=pltpu.CompilerParams(vmem_limit_bytes=60 * 1024 * 1024),
        cost_estimate=pl.CostEstimate(flops=10 * rows * wide, bytes_accessed=4 * rows * wide, transcendentals=rows),
        name="layer_norm",
    )(values, mod_shift.reshape(1, wide), mod_scale.reshape(1, wide))


def rope_tables(positions):
    small_pairs = HD // 6
    time_pairs = (HD - 4 * small_pairs) // 2
    frame = (positions // (GRID_H * GRID_W)).astype(jnp.float32)
    row_pos = (positions // GRID_W % GRID_H).astype(jnp.float32)
    col_pos = (positions % GRID_W).astype(jnp.float32)
    time_freq = 10000.0 ** (-jnp.arange(time_pairs, dtype=jnp.float32) / time_pairs)
    space_freq = 10000.0 ** (-jnp.arange(small_pairs, dtype=jnp.float32) / small_pairs)
    freq = jnp.repeat(jnp.concatenate([time_freq, space_freq, space_freq]), 2)
    pair = jnp.arange(HD, dtype=jnp.int32) // 2
    where = jnp.where(
        pair < time_pairs,
        frame[:, None],
        jnp.where(pair < time_pairs + small_pairs, row_pos[:, None], col_pos[:, None]),
    )
    angles = where * freq
    sign = jnp.where(jnp.arange(HD) % 2 == 0, -1.0, 1.0).astype(jnp.float32)
    return jnp.cos(angles), jnp.sin(angles) * sign


def as_column(row):
    return jnp.broadcast_to(row, (BLK, BLK)).T


def as_row(column):
    return jnp.broadcast_to(column, (BLK, BLK)).T[0:1, :]


def inverse_norm(ssq_row):
    return as_column(lax.rsqrt(ssq_row * (1.0 / (H * HD)) + 1e-06))


def norm_rope(raw, inv, gain, cosine, sine):
    wide = raw.astype(jnp.float32) * inv * gain
    lane = lax.broadcasted_iota(jnp.int32, wide.shape, 1)
    partner = jnp.where(
        lane % 2 == 0, pltpu.roll(wide, HD - 1, 1), pltpu.roll(wide, 1, 1)
    )
    return (wide * cosine + partner * sine).astype(jnp.bfloat16)


def split3(row):
    hi = row.astype(jnp.bfloat16).astype(jnp.float32)
    rest = row - hi
    mid = rest.astype(jnp.bfloat16).astype(jnp.float32)
    return [hi, mid, rest - mid]


PER_STEP = 4
SLOTS = ((0, 0), (0, -1), (0, 1), (1, 0), (0, 2), (1, -1), (1, 1), (1, 2))
CHUNKS = (4, 3, 1)


def chip_move(dz, dx, dc):
    return [
        (z * 8 + x * 2 + c, (z + dz) % 2 * 8 + (x + dx) % 4 * 2 + (c + dc) % 2)
        for z in range(2)
        for x in range(4)
        for c in range(2)
    ]


def from_left(block):
    return lax.ppermute(block, "sy", chip_move(0, 1, 0))


def from_right(block):
    return lax.ppermute(block, "sy", chip_move(0, -1, 0))


def from_z(block):
    return lax.ppermute(block, "sy", chip_move(1, 0, 0))


def from_core(block):
    return lax.ppermute(block, "sy", chip_move(0, 0, 1))


ANYWHERE = pl.BlockSpec(memory_space=pltpu.HBM)


def project_kernel(cuts, *refs):
    n = len(refs) - 7
    arrays, (own_w, other_w, own_ref, other_ref, ssq_ref, x_ref, sems) = refs[:n], refs[n:]

    @pl.when(pl.program_id(0) == 0)
    def _():
        copies, at = [], 0
        for i, (which, first, count) in enumerate(cuts):
            source = arrays[which].at[pl.ds(first, count)]
            copies.append(pltpu.make_async_copy(source, x_ref.at[pl.ds(at, count)], sems.at[i]))
            copies[-1].start()
            at += count
        for copy in copies:
            copy.wait()

    total = None
    for weight, out in ((own_w, own_ref), (other_w, other_ref)):
        made = jnp.dot(x_ref[...], weight[0], preferred_element_type=jnp.float32).astype(jnp.bfloat16)
        out[0] = made
        wide = made.astype(jnp.float32)
        part = jnp.sum(wide * wide, axis=-1, keepdims=True)
        total = part if total is None else total + part
    for i in range(x_ref.shape[0] // BLK):
        ssq_ref[0, i : i + 1, :] = as_row(total[i * BLK : (i + 1) * BLK])


def project(arrays, cuts, own_w, other_w):
    rows = sum(count for _, _, count in cuts)
    depth, wide = own_w.shape[1:]
    w_spec = pl.BlockSpec((1, depth, wide), lambda i: (i, 0, 0))
    o_spec = pl.BlockSpec((1, rows, wide), lambda i: (i, 0, 0))
    out = jax.ShapeDtypeStruct((3, rows, wide), jnp.bfloat16)
    return pl.pallas_call(
        functools.partial(project_kernel, cuts),
        grid=(3,),
        in_specs=[ANYWHERE] * len(arrays) + [w_spec, w_spec],
        out_specs=[o_spec, o_spec, pl.BlockSpec((1, rows // BLK, BLK), lambda i: (i, 0, 0))],
        out_shape=[out, out, jax.ShapeDtypeStruct((3, rows // BLK, BLK), jnp.float32)],
        scratch_shapes=[pltpu.VMEM((rows, depth), jnp.bfloat16), pltpu.SemaphoreType.DMA((len(cuts),))],
        compiler_params=pltpu.CompilerParams(
            dimension_semantics=("arbitrary",),
            vmem_limit_bytes=2 * rows * depth + 8 * depth * wide + 4 * 1024 * 1024,
        ),
        cost_estimate=pl.CostEstimate(
            flops=12 * rows * depth * wide, bytes_accessed=12 * depth * wide, transcendentals=0
        ),
        name="project",
    )(*arrays, own_w, other_w)


def cut_kernel(*refs):
    n = len(refs) // 2
    for source, out in zip(refs[:n], refs[n:]):
        out[...] = source[...]


def cut(arrays, cuts):
    wide = arrays[0].shape[1]
    return pl.pallas_call(
        cut_kernel,
        grid=(1,),
        in_specs=[pl.BlockSpec((count, wide), lambda i, first=first: (first, 0)) for first, count in cuts],
        out_specs=[pl.BlockSpec((count, wide), lambda i: (0, 0)) for _, count in cuts],
        out_shape=[jax.ShapeDtypeStruct((count, wide), jnp.bfloat16) for _, count in cuts],
        compiler_params=pltpu.CompilerParams(vmem_limit_bytes=10 * 1024 * 1024),
        cost_estimate=pl.CostEstimate(flops=10**5, bytes_accessed=3 * 10**6, transcendentals=0),
        name="cut_rows",
    )(*arrays)


def sources(refs):
    mine = lax.axis_index("sy")
    z, x, core = mine // 8, mine // 2 % 4, mine % 2
    at = 0
    for chunk, slots in enumerate(CHUNKS):
        for i in range(slots):
            dz, dx = SLOTS[at]
            chip = (z + dz) % 2 * 4 + (x + dx) % 4
            for other in range(2):
                n = chip * 2 + (core + other) % 2
                yield at * 2 + other, n, refs[chunk * 2 + other], pl.ds(i * BLK, BLK)
            at += 1


def halo_kernel(
    fa, ga, fb, gb, fc, gc, ssq_ref, gk_ref, cos_lo, sin_lo, cos_hi, sin_hi,
    before_ref, after_ref, raw, sems,
):
    blocks = 2 * sum(CHUNKS)
    ends = ((lambda n: n >= blocks - ROUNDS, blocks - ROUNDS, 0), (lambda n: n < ROUNDS, 0, 1))

    def each(act):
        for at, n, ref, rows in sources((fa, ga, fb, gb, fc, gc)):
            for inside, first, head in ends:

                @pl.when(inside(n))
                def _(n=n, first=first, head=head, ref=ref, rows=rows, at=at):
                    to = pl.ds(pl.multiple_of((n - first) * BLK, BLK), BLK)
                    cols = pl.ds(head * HD, HD)
                    out = (before_ref, after_ref)[head]
                    act(pltpu.make_async_copy(ref.at[0, rows, cols], raw.at[head, to], sems.at[at, 0]))
                    act(pltpu.make_async_copy(ref.at[2, rows, cols], out.at[to, pl.ds(HD, HD)], sems.at[at, 1]))

    each(lambda copy: copy.start())
    each(lambda copy: copy.wait())
    for head, out, first, cosine, sine in (
        (0, before_ref, blocks - ROUNDS, cos_hi, sin_hi),
        (1, after_ref, 0, cos_lo, sin_lo),
    ):
        for i in range(ROUNDS):
            rows = pl.ds(i * BLK, BLK)
            out[rows, 0:HD] = norm_rope(
                raw[head, rows, :], inverse_norm(ssq_ref[pl.ds(first + i, 1), :]),
                gk_ref[:, head * HD : (head + 1) * HD],
                cosine[rows, :], sine[rows, :],
            )


def halo(features, ssq_k, gk, cosine, sine):
    rows = cosine.shape[0]
    low = pl.BlockSpec((HALO, HD), lambda i: (0, 0))
    high = pl.BlockSpec((HALO, HD), lambda i: (rows // HALO - 1, 0))
    one = lambda a: pl.BlockSpec(a.shape, lambda i: (0, 0))
    out = jax.ShapeDtypeStruct((HALO, 2 * HD), jnp.bfloat16)
    return pl.pallas_call(
        halo_kernel,
        grid=(1,),
        in_specs=[ANYWHERE] * 6 + [one(ssq_k), one(gk), low, low, high, high],
        out_specs=[pl.BlockSpec((HALO, 2 * HD), lambda i: (0, 0))] * 2,
        out_shape=[out, out],
        scratch_shapes=[
            pltpu.VMEM((2, HALO, HD), jnp.bfloat16),
            pltpu.SemaphoreType.DMA((2 * sum(CHUNKS), 2)),
        ],
        compiler_params=pltpu.CompilerParams(vmem_limit_bytes=16 * 1024 * 1024),
        cost_estimate=pl.CostEstimate(flops=10**7, bytes_accessed=3 * 10**6, transcendentals=0),
        name="halo_keys",
    )(*features, ssq_k, gk, cosine, sine, cosine, sine)


def attention_kernel(
    part, fa, ga, fb, gb, fc, gc, sk_ref, sq_ref, gk_ref, gq_ref, cos_ref, sin_ref, *rest
):
    out_ref, raw, kbuf, vbuf, sems = rest[-5:]
    step, head = pl.program_id(0), pl.program_id(1)
    blocks = 2 * sum(CHUNKS)
    columns = [slice(head * HD, (head + 1) * HD) for head in range(2)]
    own_first = (ROUNDS, 0)

    def guarded(condition, act):
        if condition is None:
            act()
        else:
            pl.when(condition)(act)

    @pl.when((step == 0) & (head == 0))
    def _():
        copies = []
        for at, n, ref, rows in sources((fa, ga, fb, gb, fc, gc)):
            to = pl.ds(pl.multiple_of(n * BLK, BLK), BLK)
            needed = None if part == 0 else (n < ROUNDS) | (n >= blocks - ROUNDS)
            copies.append((n, needed, pltpu.make_async_copy(ref.at[:, rows], raw.at[:, to], sems.at[at])))
        for _, needed, copy in copies:
            guarded(needed, copy.start)
        if part == 1:
            for head, ref in enumerate(rest[:2]):
                to = pl.ds((0, blocks)[head] * BLK, HALO)
                kbuf[head, to, :] = ref[:, 0:HD]
                vbuf[head, :, to] = ref[:, HD:].T
        for n, needed, copy in copies:
            guarded(needed, copy.wait)

        for n in range(blocks):
            heads = [head for head in range(2) if part == 0 or (n < ROUNDS, n >= blocks - ROUNDS)[head]]
            rows = slice(n * BLK, (n + 1) * BLK)
            inv = inverse_norm(sk_ref[n : n + 1, :]) if heads else None
            for head in heads:
                to = slice((n + own_first[head]) * BLK, (n + own_first[head] + 1) * BLK)
                kbuf[head, to, :] = norm_rope(
                    raw[0, rows, columns[head]], inv, gk_ref[:, columns[head]], cos_ref[rows, :], sin_ref[rows, :]
                )
                vbuf[head, :, to] = raw[2, rows, columns[head]].T

    def attend(first, head):
        def score(j):
            b = first + j
            rows = pl.ds(pl.multiple_of(b * BLK, BLK), BLK)
            window = pl.ds(pl.multiple_of(b * BLK, BLK), (ROUNDS + 1) * BLK)
            q = norm_rope(
                raw[1, rows, columns[head]], inverse_norm(sq_ref[pl.ds(b, 1), :]), gq_ref[:, columns[head]],
                cos_ref[rows, :], sin_ref[rows, :],
            )
            return lax.dot_general(
                kbuf[head, window, :], q, (((1,), (1,)), ((), ())), preferred_element_type=jnp.float32
            )

        def finish(j, scores):
            window = pl.ds(pl.multiple_of((first + j) * BLK, BLK), (ROUNDS + 1) * BLK)
            top = jnp.max(scores, axis=0, keepdims=True)
            weight = jnp.exp2((scores - top) * (SCALE * LOG2E))
            total = jnp.sum(weight, axis=0, keepdims=True)
            mixed = jnp.dot(
                vbuf[head, :, window], weight.astype(jnp.bfloat16), preferred_element_type=jnp.float32
            )
            out_ref[j, 0, 0:BLK, :] = (mixed / total).T.astype(jnp.bfloat16)
            stats = split3(top * SCALE) + split3(total) + [jnp.zeros((EXTRA - 6, HD), jnp.float32)]
            out_ref[j, 0, BLK : BLK + EXTRA, :] = jnp.concatenate(stats, axis=0).astype(jnp.bfloat16)

        scores = [score(j) for j in range(PER_STEP)]
        for j in range(PER_STEP):
            finish(j, scores[j])
    for which in range(2):
        first = (step + 1 - which) * PER_STEP if part == 0 else (0, blocks - ROUNDS)[which]
        pl.when(head == which)(functools.partial(attend, first, which))


def attention(part, features, sk, sq, gk, gq, cosine, sine, before=None, after=None, held=None):
    rows = cosine.shape[0]
    blocks = rows // BLK
    whole = lambda a: pl.BlockSpec(a.shape, lambda i, h, n=a.ndim: (0,) * n)
    steps = blocks // PER_STEP - 1 if part == 0 else 1
    which = (lambda i, h: (i + 1 - h, h, 0, 0)) if part == 0 else (lambda i, h: (h * (blocks // PER_STEP - 1), h, 0, 0))
    small = (sk, sq, gk, gq, cosine, sine) + (() if held is None else (before, after))
    more = () if held is None else (held,)
    return pl.pallas_call(
        functools.partial(attention_kernel, part),
        grid=(steps, 2),
        in_specs=[ANYWHERE] * 6 + [whole(a) for a in small] + [ANYWHERE] * len(more),
        out_specs=pl.BlockSpec((PER_STEP, 1, BLK + EXTRA, HD), which),
        out_shape=jax.ShapeDtypeStruct((blocks, 2, BLK + EXTRA, HD), jnp.bfloat16),
        scratch_shapes=[
            pltpu.VMEM((3, rows, 2 * HD), jnp.bfloat16),
            pltpu.VMEM((2, rows + HALO, HD), jnp.bfloat16),
            pltpu.VMEM((2, HD, rows + HALO), jnp.bfloat16),
            pltpu.SemaphoreType.DMA((blocks,)),
        ],
        input_output_aliases={14: 0} if more else {},
        compiler_params=pltpu.CompilerParams(
            dimension_semantics=("arbitrary", "arbitrary"), vmem_limit_bytes=24 * 1024 * 1024
        ),
        cost_estimate=pl.CostEstimate(
            flops=(1 + 2 * (1 - part)) * 5 * 10**8, bytes_accessed=10**7, transcendentals=10**6
        ),
        name=("window_attention", "window_attention_halo")[part],
    )(*features, *small, *more)


def along_sx(block, distance):
    n = lax.axis_size("sx")
    return lax.ppermute(block, "sx", [((i - distance) % n, i) for i in range(n)])


def unpack_kernel(arrived_ref, attended_ref, best_ref, total_ref):
    classes, heads = arrived_ref.shape[:2]
    for c in range(classes):
        for h in range(heads):
            head = c * heads + h
            attended_ref[:, head * HD : (head + 1) * HD] = arrived_ref[c, h, 0:BLK, :]
            stats = arrived_ref[c, h, BLK : BLK + EXTRA, :].astype(jnp.float32)
            best_ref[head : head + 1, :] = (stats[0:1] + stats[1:2]) + stats[2:3]
            total_ref[head : head + 1, :] = (stats[3:4] + stats[4:5]) + stats[5:6]


def unpack(arrived):
    shapes = [
        jax.ShapeDtypeStruct((BLK, H * HD), jnp.bfloat16),
        jax.ShapeDtypeStruct((H, BLK), jnp.float32),
        jax.ShapeDtypeStruct((H, BLK), jnp.float32),
    ]
    return pl.pallas_call(
        unpack_kernel,
        grid=(1,),
        in_specs=[pl.BlockSpec(arrived.shape, lambda i: (0, 0, 0, 0))],
        out_specs=[pl.BlockSpec(a.shape, lambda i: (0, 0)) for a in shapes],
        out_shape=shapes,
        compiler_params=pltpu.CompilerParams(vmem_limit_bytes=16 * 1024 * 1024),
        name="unpack",
    )(arrived)


def body(tokens, mod_shift, mod_scale, w_query, w_key, w_value, query_gain, key_gain):
    group = lax.axis_index("sx")
    mine = lax.axis_index("sy")
    z, x = mine // 8, mine // 2 % 4
    chips = jnp.stack([(z + dz) % 2 * 4 + (x + dx) % 4 for dz, dx in SLOTS])
    here = (chips[:, None] == jnp.arange(8)[None, :]).astype(jnp.float32)
    rows = BLK * lax.axis_size("sy")
    barrier = lax.optimization_barrier

    own = layer_norm(tokens, mod_shift, mod_scale)
    left, right, beside = from_left(own), from_right(own), from_z(own)
    key_w, query_w, value_w = barrier((w_key, w_query, w_value, own))[:3]
    one = barrier(jnp.bfloat16(1))
    sent_w = jnp.stack([key_w, query_w, value_w])
    own_w = sent_w * one
    cosine, sine = rope_tables(group * rows + jnp.arange(rows, dtype=jnp.int32))
    gq = lax.dynamic_slice(query_gain, (mine * 2 * HD,), (2 * HD,)).reshape(1, 2 * HD)
    gk = lax.dynamic_slice(key_gain, (mine * 2 * HD,), (2 * HD,)).reshape(1, 2 * HD)
    (left, right, beside), own_w, sent_w, (cosine, sine, gq, gk, here) = barrier(
        ((left, right, beside), own_w, sent_w, (cosine, sine, gq, gk, here))
    )

    far, z_right, z_left = from_left(left), from_right(beside), from_z(left)
    other_w = from_core(sent_w) * one
    near = project((own, left, right, beside), tuple((i, 0, BLK) for i in range(4)), own_w, other_w)
    near, far, z_right, z_left = barrier((near, far, z_right, z_left))

    part_left, part_right, part_z = cut((z_left, z_right, far), ((0, 48), (1, 48), (3, 32)))
    z_far = (from_left(part_left), from_right(part_right), from_z(part_z))
    middle = project((far, z_left, z_right), tuple((i, 0, BLK) for i in range(3)), own_w, other_w)
    z_far, middle = barrier((z_far, middle))
    last = project(z_far, tuple((i, 0, p.shape[0]) for i, p in enumerate(z_far)), own_w, other_w)

    features, parts = [], []
    for made, given, part in (near, middle, last):
        features += [made, from_core(given)]
        parts.append(part[:2])
    part = jnp.concatenate(parts, axis=1)
    part = jnp.sum(here[None, :, :, None] * part[:, :, None, :], axis=1)
    sent = jnp.broadcast_to(part.reshape(1, 16, BLK), (NSY, 16, BLK))
    seen = lax.all_to_all(sent, "sy", split_axis=0, concat_axis=0, tiled=True)
    ssq = jnp.sum(seen.reshape(8, 2, 2, 8, BLK), axis=0).transpose(1, 2, 0, 3).reshape(2, 16, BLK)
    before, after = halo(features, ssq[0], gk, cosine, sine)
    common = (ssq[0], ssq[1], gk, gq, cosine, sine)
    out = attention(0, features, *common)
    before, after = along_sx(before, 1), along_sx(after, -1)
    out = attention(1, features, *common, before=before, after=after, held=out)
    arrived = lax.all_to_all(out, "sy", split_axis=0, concat_axis=0, tiled=True)
    return unpack(arrived)


def solution(mesh):
    placed = (
        P(("sx", "sy"), None),
        P(),
        P(),
        P(None, "sy"),
        P(None, "sy"),
        P(None, "sy"),
        P(),
        P(),
    )
    return jax.shard_map(
        body,
        mesh=mesh,
        in_specs=placed,
        out_specs=(P(("sx", "sy"), None), P(None, ("sx", "sy")), P(None, ("sx", "sy"))),
        check_vma=False,
    )
```

```python
import functools

import jax
import jax.numpy as jnp
import numpy as np
from jax import lax
from jax.experimental import pallas as pl
from jax.experimental.pallas import tpu as pltpu
from jax.sharding import PartitionSpec as P

H = 32
HD = 128
ROUNDS = 4
GRID_W = 80
GRID_H = 45
BLK = 128
HALO = ROUNDS * BLK
EXTRA = 8
NSY = 16
SCALE = np.float32(1.0) / np.sqrt(np.float32(HD))
LOG2E = np.float32(1.4426950408889634)


def layer_norm_kernel(tokens_ref, shift_ref, scale_ref, out_ref):
    wide = tokens_ref[...].astype(jnp.float32)
    center = jnp.mean(wide, axis=-1, keepdims=True)
    apart = wide - center
    spread = jnp.mean(apart * apart, axis=-1, keepdims=True)
    scaled = apart * lax.rsqrt(spread + 1e-06)
    out_ref[...] = (scaled * (1.0 + scale_ref[...]) + shift_ref[...]).astype(jnp.bfloat16)


def layer_norm(values, mod_shift, mod_scale):
    rows, wide = values.shape
    block = pl.BlockSpec((64, wide), lambda i: (i, 0))
    vector = pl.BlockSpec((1, wide), lambda i: (0, 0))
    return pl.pallas_call(
        layer_norm_kernel,
        grid=(rows // 64,),
        in_specs=[block, vector, vector],
        out_specs=block,
        out_shape=jax.ShapeDtypeStruct((rows, wide), jnp.bfloat16),
        compiler_params=pltpu.CompilerParams(vmem_limit_bytes=60 * 1024 * 1024),
        cost_estimate=pl.CostEstimate(flops=10 * rows * wide, bytes_accessed=4 * rows * wide, transcendentals=rows),
        name="layer_norm",
    )(values, mod_shift.reshape(1, wide), mod_scale.reshape(1, wide))


def rope_tables(positions):
    small_pairs = HD // 6
    time_pairs = (HD - 4 * small_pairs) // 2
    frame = (positions // (GRID_H * GRID_W)).astype(jnp.float32)
    row_pos = (positions // GRID_W % GRID_H).astype(jnp.float32)
    col_pos = (positions % GRID_W).astype(jnp.float32)
    time_freq = 10000.0 ** (-jnp.arange(time_pairs, dtype=jnp.float32) / time_pairs)
    space_freq = 10000.0 ** (-jnp.arange(small_pairs, dtype=jnp.float32) / small_pairs)
    freq = jnp.repeat(jnp.concatenate([time_freq, space_freq, space_freq]), 2)
    pair = jnp.arange(HD, dtype=jnp.int32) // 2
    where = jnp.where(
        pair < time_pairs,
        frame[:, None],
        jnp.where(pair < time_pairs + small_pairs, row_pos[:, None], col_pos[:, None]),
    )
    angles = where * freq
    sign = jnp.where(jnp.arange(HD) % 2 == 0, -1.0, 1.0).astype(jnp.float32)
    return jnp.cos(angles), jnp.sin(angles) * sign


def as_column(row):
    return jnp.broadcast_to(row, (BLK, BLK)).T


def as_row(column):
    return jnp.broadcast_to(column, (BLK, BLK)).T[0:1, :]


def inverse_norm(ssq_row):
    return as_column(lax.rsqrt(ssq_row * (1.0 / (H * HD)) + 1e-06))


def norm_rope(raw, inv, gain, cosine, sine):
    wide = raw.astype(jnp.float32) * inv * gain
    lane = lax.broadcasted_iota(jnp.int32, wide.shape, 1)
    partner = jnp.where(
        lane % 2 == 0, pltpu.roll(wide, HD - 1, 1), pltpu.roll(wide, 1, 1)
    )
    return (wide * cosine + partner * sine).astype(jnp.bfloat16)


def split3(row):
    hi = row.astype(jnp.bfloat16).astype(jnp.float32)
    rest = row - hi
    mid = rest.astype(jnp.bfloat16).astype(jnp.float32)
    return [hi, mid, rest - mid]


PER_STEP = 4
SLOTS = ((0, 0), (0, -1), (0, 1), (1, 0), (0, 2), (1, -1), (1, 1), (1, 2))
CHUNKS = (4, 3, 1)


def chip_move(dz, dx, dc):
    return [
        (z * 8 + x * 2 + c, (z + dz) % 2 * 8 + (x + dx) % 4 * 2 + (c + dc) % 2)
        for z in range(2)
        for x in range(4)
        for c in range(2)
    ]


def from_left(block):
    return lax.ppermute(block, "sy", chip_move(0, 1, 0))


def from_right(block):
    return lax.ppermute(block, "sy", chip_move(0, -1, 0))


def from_z(block):
    return lax.ppermute(block, "sy", chip_move(1, 0, 0))


def from_core(block):
    return lax.ppermute(block, "sy", chip_move(0, 0, 1))


ANYWHERE = pl.BlockSpec(memory_space=pltpu.HBM)


def project_kernel(cuts, *refs):
    n = len(refs) - 7
    arrays, (own_w, other_w, own_ref, other_ref, ssq_ref, x_ref, sems) = refs[:n], refs[n:]

    @pl.when(pl.program_id(0) == 0)
    def _():
        copies, at = [], 0
        for i, (which, first, count) in enumerate(cuts):
            source = arrays[which].at[pl.ds(first, count)]
            copies.append(pltpu.make_async_copy(source, x_ref.at[pl.ds(at, count)], sems.at[i]))
            copies[-1].start()
            at += count
        for copy in copies:
            copy.wait()

    total = None
    for weight, out in ((own_w, own_ref), (other_w, other_ref)):
        made = jnp.dot(x_ref[...], weight[0], preferred_element_type=jnp.float32).astype(jnp.bfloat16)
        out[0] = made
        wide = made.astype(jnp.float32)
        part = jnp.sum(wide * wide, axis=-1, keepdims=True)
        total = part if total is None else total + part
    for i in range(x_ref.shape[0] // BLK):
        ssq_ref[0, i : i + 1, :] = as_row(total[i * BLK : (i + 1) * BLK])


def project(arrays, cuts, own_w, other_w):
    rows = sum(count for _, _, count in cuts)
    depth, wide = own_w.shape[1:]
    w_spec = pl.BlockSpec((1, depth, wide), lambda i: (i, 0, 0))
    o_spec = pl.BlockSpec((1, rows, wide), lambda i: (i, 0, 0))
    out = jax.ShapeDtypeStruct((3, rows, wide), jnp.bfloat16)
    return pl.pallas_call(
        functools.partial(project_kernel, cuts),
        grid=(3,),
        in_specs=[ANYWHERE] * len(arrays) + [w_spec, w_spec],
        out_specs=[o_spec, o_spec, pl.BlockSpec((1, rows // BLK, BLK), lambda i: (i, 0, 0))],
        out_shape=[out, out, jax.ShapeDtypeStruct((3, rows // BLK, BLK), jnp.float32)],
        scratch_shapes=[pltpu.VMEM((rows, depth), jnp.bfloat16), pltpu.SemaphoreType.DMA((len(cuts),))],
        compiler_params=pltpu.CompilerParams(
            dimension_semantics=("arbitrary",),
            vmem_limit_bytes=2 * rows * depth + 8 * depth * wide + 4 * 1024 * 1024,
        ),
        cost_estimate=pl.CostEstimate(
            flops=12 * rows * depth * wide, bytes_accessed=12 * depth * wide, transcendentals=0
        ),
        name="project",
    )(*arrays, own_w, other_w)


def cut_kernel(*refs):
    n = len(refs) // 2
    for source, out in zip(refs[:n], refs[n:]):
        out[...] = source[...]


def cut(arrays, cuts):
    wide = arrays[0].shape[1]
    return pl.pallas_call(
        cut_kernel,
        grid=(1,),
        in_specs=[pl.BlockSpec((count, wide), lambda i, first=first: (first, 0)) for first, count in cuts],
        out_specs=[pl.BlockSpec((count, wide), lambda i: (0, 0)) for _, count in cuts],
        out_shape=[jax.ShapeDtypeStruct((count, wide), jnp.bfloat16) for _, count in cuts],
        compiler_params=pltpu.CompilerParams(vmem_limit_bytes=10 * 1024 * 1024),
        cost_estimate=pl.CostEstimate(flops=10**5, bytes_accessed=3 * 10**6, transcendentals=0),
        name="cut_rows",
    )(*arrays)


def sources(refs):
    mine = lax.axis_index("sy")
    z, x, core = mine // 8, mine // 2 % 4, mine % 2
    at = 0
    for chunk, slots in enumerate(CHUNKS):
        for i in range(slots):
            dz, dx = SLOTS[at]
            chip = (z + dz) % 2 * 4 + (x + dx) % 4
            for other in range(2):
                n = chip * 2 + (core + other) % 2
                yield at * 2 + other, n, refs[chunk * 2 + other], pl.ds(i * BLK, BLK)
            at += 1


def payload_kernel(*refs):
    parts, out_ref, held = refs[:-2], refs[-2], refs[-1]
    mine = lax.axis_index("sy")
    z, x = mine // 8, mine // 2 % 4
    at = 0
    for part, slots in zip(parts, CHUNKS):
        for i in range(slots):
            dz, dx = SLOTS[at]
            chip = (z + dz) % 2 * 4 + (x + dx) % 4
            for kind in range(2):
                held[pl.ds(kind * 8 + chip, 1), :] = part[kind, i : i + 1, :]
            at += 1
    for i in range(out_ref.shape[0]):
        out_ref[i] = held[...]


def payload(parts):
    return pl.pallas_call(
        payload_kernel,
        grid=(1,),
        in_specs=[pl.BlockSpec(p.shape, lambda i: (0, 0, 0)) for p in parts],
        out_specs=pl.BlockSpec((NSY, 16, BLK), lambda i: (0, 0, 0)),
        out_shape=jax.ShapeDtypeStruct((NSY, 16, BLK), jnp.float32),
        scratch_shapes=[pltpu.VMEM((16, BLK), jnp.float32)],
        compiler_params=pltpu.CompilerParams(vmem_limit_bytes=4 * 1024 * 1024),
        name="square_sums",
    )(*parts)


def halo_kernel(
    fa, ga, fb, gb, fc, gc, ssq_ref, gk_ref, cos_lo, sin_lo, cos_hi, sin_hi,
    before_ref, after_ref, raw, sems,
):
    blocks = 2 * sum(CHUNKS)
    ends = ((lambda n: n >= blocks - ROUNDS, blocks - ROUNDS, 0), (lambda n: n < ROUNDS, 0, 1))

    def each(act):
        for at, n, ref, rows in sources((fa, ga, fb, gb, fc, gc)):
            for inside, first, head in ends:

                @pl.when(inside(n))
                def _(n=n, first=first, head=head, ref=ref, rows=rows, at=at):
                    to = pl.ds(pl.multiple_of((n - first) * BLK, BLK), BLK)
                    cols = pl.ds(head * HD, HD)
                    out = (before_ref, after_ref)[head]
                    act(pltpu.make_async_copy(ref.at[0, rows, cols], raw.at[head, to], sems.at[at, 0]))
                    act(pltpu.make_async_copy(ref.at[2, rows, cols], out.at[to, pl.ds(HD, HD)], sems.at[at, 1]))

    each(lambda copy: copy.start())
    each(lambda copy: copy.wait())
    for head, out, first, cosine, sine in (
        (0, before_ref, blocks - ROUNDS, cos_hi, sin_hi),
        (1, after_ref, 0, cos_lo, sin_lo),
    ):
        for i in range(ROUNDS):
            rows = pl.ds(i * BLK, BLK)
            out[rows, 0:HD] = norm_rope(
                raw[head, rows, :], inverse_norm(ssq_ref[pl.ds(first + i, 1), :]),
                gk_ref[:, head * HD : (head + 1) * HD],
                cosine[rows, :], sine[rows, :],
            )


def halo(features, ssq_k, gk, cosine, sine):
    rows = cosine.shape[0]
    low = pl.BlockSpec((HALO, HD), lambda i: (0, 0))
    high = pl.BlockSpec((HALO, HD), lambda i: (rows // HALO - 1, 0))
    one = lambda a: pl.BlockSpec(a.shape, lambda i: (0, 0))
    out = jax.ShapeDtypeStruct((HALO, 2 * HD), jnp.bfloat16)
    return pl.pallas_call(
        halo_kernel,
        grid=(1,),
        in_specs=[ANYWHERE] * 6 + [one(ssq_k), one(gk), low, low, high, high],
        out_specs=[pl.BlockSpec((HALO, 2 * HD), lambda i: (0, 0))] * 2,
        out_shape=[out, out],
        scratch_shapes=[
            pltpu.VMEM((2, HALO, HD), jnp.bfloat16),
            pltpu.SemaphoreType.DMA((2 * sum(CHUNKS), 2)),
        ],
        compiler_params=pltpu.CompilerParams(vmem_limit_bytes=16 * 1024 * 1024),
        cost_estimate=pl.CostEstimate(flops=10**9, bytes_accessed=10**4, transcendentals=0),
        name="halo_keys",
    )(*features, ssq_k, gk, cosine, sine, cosine, sine)


def attention_kernel(
    part, fa, ga, fb, gb, fc, gc, sk_ref, sq_ref, gk_ref, gq_ref, cos_ref, sin_ref, *rest
):
    out_ref, raw, kbuf, vbuf, sems = rest[-5:]
    step, head = pl.program_id(0), pl.program_id(1)
    blocks = 2 * sum(CHUNKS)
    columns = [slice(head * HD, (head + 1) * HD) for head in range(2)]
    own_first = (ROUNDS, 0)

    def guarded(condition, act):
        if condition is None:
            act()
        else:
            pl.when(condition)(act)

    @pl.when((step == 0) & (head == 0))
    def _():
        copies = []
        for at, n, ref, rows in sources((fa, ga, fb, gb, fc, gc)):
            to = pl.ds(pl.multiple_of(n * BLK, BLK), BLK)
            needed = None if part == 0 else (n < ROUNDS) | (n >= blocks - ROUNDS)
            copies.append((n, needed, pltpu.make_async_copy(ref.at[:, rows], raw.at[:, to], sems.at[at])))
        for _, needed, copy in copies:
            guarded(needed, copy.start)
        if part == 1:
            for head, ref in enumerate(rest[:2]):
                to = pl.ds((0, blocks)[head] * BLK, HALO)
                kbuf[head, to, :] = ref[:, 0:HD]
                vbuf[head, :, to] = ref[:, HD:].T
        for n, needed, copy in copies:
            guarded(needed, copy.wait)

        for n in range(blocks):
            heads = [head for head in range(2) if part == 0 or (n < ROUNDS, n >= blocks - ROUNDS)[head]]
            rows = slice(n * BLK, (n + 1) * BLK)
            inv = inverse_norm(sk_ref[n : n + 1, :]) if heads else None
            for head in heads:
                to = slice((n + own_first[head]) * BLK, (n + own_first[head] + 1) * BLK)
                kbuf[head, to, :] = norm_rope(
                    raw[0, rows, columns[head]], inv, gk_ref[:, columns[head]], cos_ref[rows, :], sin_ref[rows, :]
                )
                vbuf[head, :, to] = raw[2, rows, columns[head]].T

    def attend(first, head):
        def score(j):
            b = first + j
            rows = pl.ds(pl.multiple_of(b * BLK, BLK), BLK)
            window = pl.ds(pl.multiple_of(b * BLK, BLK), (ROUNDS + 1) * BLK)
            q = norm_rope(
                raw[1, rows, columns[head]], inverse_norm(sq_ref[pl.ds(b, 1), :]), gq_ref[:, columns[head]],
                cos_ref[rows, :], sin_ref[rows, :],
            )
            return lax.dot_general(
                kbuf[head, window, :], q, (((1,), (1,)), ((), ())), preferred_element_type=jnp.float32
            )

        def finish(j, scores):
            window = pl.ds(pl.multiple_of((first + j) * BLK, BLK), (ROUNDS + 1) * BLK)
            top = jnp.max(scores, axis=0, keepdims=True)
            weight = jnp.exp2((scores - top) * (SCALE * LOG2E))
            total = jnp.sum(weight, axis=0, keepdims=True)
            mixed = jnp.dot(
                vbuf[head, :, window], weight.astype(jnp.bfloat16), preferred_element_type=jnp.float32
            )
            out_ref[j, 0, 0:BLK, :] = (mixed / total).T.astype(jnp.bfloat16)
            stats = split3(top * SCALE) + split3(total) + [jnp.zeros((EXTRA - 6, HD), jnp.float32)]
            out_ref[j, 0, BLK : BLK + EXTRA, :] = jnp.concatenate(stats, axis=0).astype(jnp.bfloat16)

        scores = [score(j) for j in range(PER_STEP)]
        for j in range(PER_STEP):
            finish(j, scores[j])
    for which in range(2):
        first = (step + 1 - which) * PER_STEP if part == 0 else (0, blocks - ROUNDS)[which]
        pl.when(head == which)(functools.partial(attend, first, which))


def attention(part, features, sk, sq, gk, gq, cosine, sine, before=None, after=None, held=None):
    rows = cosine.shape[0]
    blocks = rows // BLK
    whole = lambda a: pl.BlockSpec(a.shape, lambda i, h, n=a.ndim: (0,) * n)
    steps = blocks // PER_STEP - 1 if part == 0 else 1
    which = (lambda i, h: (i + 1 - h, h, 0, 0)) if part == 0 else (lambda i, h: (h * (blocks // PER_STEP - 1), h, 0, 0))
    small = (sk, sq, gk, gq, cosine, sine) + (() if held is None else (before, after))
    more = () if held is None else (held,)
    return pl.pallas_call(
        functools.partial(attention_kernel, part),
        grid=(steps, 2),
        in_specs=[ANYWHERE] * 6 + [whole(a) for a in small] + [ANYWHERE] * len(more),
        out_specs=pl.BlockSpec((PER_STEP, 1, BLK + EXTRA, HD), which),
        out_shape=jax.ShapeDtypeStruct((blocks, 2, BLK + EXTRA, HD), jnp.bfloat16),
        scratch_shapes=[
            pltpu.VMEM((3, rows, 2 * HD), jnp.bfloat16),
            pltpu.VMEM((2, rows + HALO, HD), jnp.bfloat16),
            pltpu.VMEM((2, HD, rows + HALO), jnp.bfloat16),
            pltpu.SemaphoreType.DMA((blocks,)),
        ],
        input_output_aliases={14: 0} if more else {},
        compiler_params=pltpu.CompilerParams(
            dimension_semantics=("arbitrary", "arbitrary"), vmem_limit_bytes=24 * 1024 * 1024
        ),
        cost_estimate=pl.CostEstimate(
            flops=(1 + 2 * (1 - part)) * 10**9, bytes_accessed=10**4, transcendentals=10**6
        ),
        name=("window_attention", "window_attention_halo")[part],
    )(*features, *small, *more)


def along_sx(block, distance):
    n = lax.axis_size("sx")
    return lax.ppermute(block, "sx", [((i - distance) % n, i) for i in range(n)])


def unpack_kernel(arrived_ref, attended_ref, best_ref, total_ref):
    classes, heads = arrived_ref.shape[:2]
    for c in range(classes):
        for h in range(heads):
            head = c * heads + h
            attended_ref[:, head * HD : (head + 1) * HD] = arrived_ref[c, h, 0:BLK, :]
            stats = arrived_ref[c, h, BLK : BLK + EXTRA, :].astype(jnp.float32)
            best_ref[head : head + 1, :] = (stats[0:1] + stats[1:2]) + stats[2:3]
            total_ref[head : head + 1, :] = (stats[3:4] + stats[4:5]) + stats[5:6]


def unpack(arrived):
    shapes = [
        jax.ShapeDtypeStruct((BLK, H * HD), jnp.bfloat16),
        jax.ShapeDtypeStruct((H, BLK), jnp.float32),
        jax.ShapeDtypeStruct((H, BLK), jnp.float32),
    ]
    return pl.pallas_call(
        unpack_kernel,
        grid=(1,),
        in_specs=[pl.BlockSpec(arrived.shape, lambda i: (0, 0, 0, 0))],
        out_specs=[pl.BlockSpec(a.shape, lambda i: (0, 0)) for a in shapes],
        out_shape=shapes,
        compiler_params=pltpu.CompilerParams(vmem_limit_bytes=16 * 1024 * 1024),
        name="unpack",
    )(arrived)


def body(tokens, mod_shift, mod_scale, w_query, w_key, w_value, query_gain, key_gain):
    group = lax.axis_index("sx")
    mine = lax.axis_index("sy")
    rows = BLK * lax.axis_size("sy")
    barrier = lax.optimization_barrier

    own = layer_norm(tokens, mod_shift, mod_scale)
    left, right, beside = from_left(own), from_right(own), from_z(own)
    key_w, query_w, value_w = barrier((w_key, w_query, w_value, own))[:3]
    one = barrier(jnp.bfloat16(1))
    sent_w = jnp.stack([key_w, query_w, value_w])
    own_w = sent_w * one
    cosine, sine = rope_tables(group * rows + jnp.arange(rows, dtype=jnp.int32))
    gq = lax.dynamic_slice(query_gain, (mine * 2 * HD,), (2 * HD,)).reshape(1, 2 * HD)
    gk = lax.dynamic_slice(key_gain, (mine * 2 * HD,), (2 * HD,)).reshape(1, 2 * HD)
    (left, right, beside), own_w, sent_w, (cosine, sine, gq, gk) = barrier(
        ((left, right, beside), own_w, sent_w, (cosine, sine, gq, gk))
    )

    far, z_right, z_left = from_left(left), from_right(beside), from_z(left)
    other_w = from_core(sent_w) * one
    near = project((own, left, right, beside), tuple((i, 0, BLK) for i in range(4)), own_w, other_w)
    near, far, z_right, z_left = barrier((near, far, z_right, z_left))

    part_left, part_right, part_z = cut((z_left, z_right, far), ((0, 48), (1, 48), (3, 32)))
    z_far = (from_left(part_left), from_right(part_right), from_z(part_z))
    middle = project((far, z_left, z_right), tuple((i, 0, BLK) for i in range(3)), own_w, other_w)
    z_far, middle = barrier((z_far, middle))
    last = project(z_far, tuple((i, 0, p.shape[0]) for i, p in enumerate(z_far)), own_w, other_w)

    features, parts = [], []
    for made, given, part in (near, middle, last):
        features += [made, from_core(given)]
        parts.append(part)
    sent = payload(parts)
    seen = lax.all_to_all(sent, "sy", split_axis=0, concat_axis=0, tiled=True)
    ssq = jnp.sum(seen.reshape(8, 2, 2, 8, BLK), axis=0).transpose(1, 2, 0, 3).reshape(2, 16, BLK)
    before, after = halo(features, ssq[0], gk, cosine, sine)
    common = (ssq[0], ssq[1], gk, gq, cosine, sine)
    out = attention(0, features, *common)
    before, after = along_sx(before, 1), along_sx(after, -1)
    out = attention(1, features, *common, before=before, after=after, held=out)
    arrived = lax.all_to_all(out, "sy", split_axis=0, concat_axis=0, tiled=True)
    return unpack(arrived)


def solution(mesh):
    placed = (
        P(("sx", "sy"), None),
        P(),
        P(),
        P(None, "sy"),
        P(None, "sy"),
        P(None, "sy"),
        P(),
        P(),
    )
    return jax.shard_map(
        body,
        mesh=mesh,
        in_specs=placed,
        out_specs=(P(("sx", "sy"), None), P(None, ("sx", "sy")), P(None, ("sx", "sy"))),
        check_vma=False,
    )
```

```python
import functools

import jax
import jax.numpy as jnp
import numpy as np
from jax import lax
from jax.experimental import pallas as pl
from jax.experimental.pallas import tpu as pltpu
from jax.sharding import PartitionSpec as P

H = 32
HD = 128
ROUNDS = 4
GRID_W = 80
GRID_H = 45
BLK = 128
HALO = ROUNDS * BLK
EXTRA = 8
NSY = 16
SCALE = np.float32(1.0) / np.sqrt(np.float32(HD))
LOG2E = np.float32(1.4426950408889634)


def layer_norm_kernel(tokens_ref, shift_ref, scale_ref, out_ref):
    wide = tokens_ref[...].astype(jnp.float32)
    center = jnp.mean(wide, axis=-1, keepdims=True)
    apart = wide - center
    spread = jnp.mean(apart * apart, axis=-1, keepdims=True)
    scaled = apart * lax.rsqrt(spread + 1e-06)
    out_ref[...] = (scaled * (1.0 + scale_ref[...]) + shift_ref[...]).astype(jnp.bfloat16)


def layer_norm(values, mod_shift, mod_scale):
    rows, wide = values.shape
    block = pl.BlockSpec((64, wide), lambda i: (i, 0))
    vector = pl.BlockSpec((1, wide), lambda i: (0, 0))
    return pl.pallas_call(
        layer_norm_kernel,
        grid=(rows // 64,),
        in_specs=[block, vector, vector],
        out_specs=block,
        out_shape=jax.ShapeDtypeStruct((rows, wide), jnp.bfloat16),
        compiler_params=pltpu.CompilerParams(vmem_limit_bytes=60 * 1024 * 1024),
        cost_estimate=pl.CostEstimate(flops=10 * rows * wide, bytes_accessed=4 * rows * wide, transcendentals=rows),
        name="layer_norm",
    )(values, mod_shift.reshape(1, wide), mod_scale.reshape(1, wide))


def rope_tables(positions):
    small_pairs = HD // 6
    time_pairs = (HD - 4 * small_pairs) // 2
    frame = (positions // (GRID_H * GRID_W)).astype(jnp.float32)
    row_pos = (positions // GRID_W % GRID_H).astype(jnp.float32)
    col_pos = (positions % GRID_W).astype(jnp.float32)
    time_freq = 10000.0 ** (-jnp.arange(time_pairs, dtype=jnp.float32) / time_pairs)
    space_freq = 10000.0 ** (-jnp.arange(small_pairs, dtype=jnp.float32) / small_pairs)
    freq = jnp.repeat(jnp.concatenate([time_freq, space_freq, space_freq]), 2)
    pair = jnp.arange(HD, dtype=jnp.int32) // 2
    where = jnp.where(
        pair < time_pairs,
        frame[:, None],
        jnp.where(pair < time_pairs + small_pairs, row_pos[:, None], col_pos[:, None]),
    )
    angles = where * freq
    sign = jnp.where(jnp.arange(HD) % 2 == 0, -1.0, 1.0).astype(jnp.float32)
    return jnp.cos(angles), jnp.sin(angles) * sign


def as_column(row):
    return jnp.broadcast_to(row, (BLK, BLK)).T


def as_row(column):
    return jnp.broadcast_to(column, (BLK, BLK)).T[0:1, :]


def inverse_norm(ssq_row):
    return as_column(lax.rsqrt(ssq_row * (1.0 / (H * HD)) + 1e-06))


def norm_rope(raw, inv, gain, cosine, sine):
    wide = raw.astype(jnp.float32) * inv * gain
    lane = lax.broadcasted_iota(jnp.int32, wide.shape, 1)
    partner = jnp.where(
        lane % 2 == 0, pltpu.roll(wide, HD - 1, 1), pltpu.roll(wide, 1, 1)
    )
    return (wide * cosine + partner * sine).astype(jnp.bfloat16)


def split3(row):
    hi = row.astype(jnp.bfloat16).astype(jnp.float32)
    rest = row - hi
    mid = rest.astype(jnp.bfloat16).astype(jnp.float32)
    return [hi, mid, rest - mid]


PER_STEP = 4
SLOTS = ((0, 0), (0, -1), (0, 1), (1, 0), (0, 2), (1, -1), (1, 1), (1, 2))
CHUNKS = (4, 3, 1)


def chip_move(dz, dx, dc):
    return [
        (z * 8 + x * 2 + c, (z + dz) % 2 * 8 + (x + dx) % 4 * 2 + (c + dc) % 2)
        for z in range(2)
        for x in range(4)
        for c in range(2)
    ]


def from_left(block):
    return lax.ppermute(block, "sy", chip_move(0, 1, 0))


def from_right(block):
    return lax.ppermute(block, "sy", chip_move(0, -1, 0))


def from_z(block):
    return lax.ppermute(block, "sy", chip_move(1, 0, 0))


def from_core(block):
    return lax.ppermute(block, "sy", chip_move(0, 0, 1))


ANYWHERE = pl.BlockSpec(memory_space=pltpu.HBM)


def project_kernel(cuts, *refs):
    n = len(refs) - 7
    arrays, (own_w, other_w, own_ref, other_ref, ssq_ref, x_ref, sems) = refs[:n], refs[n:]

    @pl.when(pl.program_id(0) == 0)
    def _():
        copies, at = [], 0
        for i, (which, first, count) in enumerate(cuts):
            source = arrays[which].at[pl.ds(first, count)]
            copies.append(pltpu.make_async_copy(source, x_ref.at[pl.ds(at, count)], sems.at[i]))
            copies[-1].start()
            at += count
        for copy in copies:
            copy.wait()

    total = None
    for weight, out in ((own_w, own_ref), (other_w, other_ref)):
        made = jnp.dot(x_ref[...], weight[0], preferred_element_type=jnp.float32).astype(jnp.bfloat16)
        out[0] = made
        wide = made.astype(jnp.float32)
        part = jnp.sum(wide * wide, axis=-1, keepdims=True)
        total = part if total is None else total + part
    for i in range(x_ref.shape[0] // BLK):
        ssq_ref[0, i : i + 1, :] = as_row(total[i * BLK : (i + 1) * BLK])


def project(arrays, cuts, own_w, other_w):
    rows = sum(count for _, _, count in cuts)
    depth, wide = own_w.shape[1:]
    w_spec = pl.BlockSpec((1, depth, wide), lambda i: (i, 0, 0))
    o_spec = pl.BlockSpec((1, rows, wide), lambda i: (i, 0, 0))
    out = jax.ShapeDtypeStruct((3, rows, wide), jnp.bfloat16)
    return pl.pallas_call(
        functools.partial(project_kernel, cuts),
        grid=(3,),
        in_specs=[ANYWHERE] * len(arrays) + [w_spec, w_spec],
        out_specs=[o_spec, o_spec, pl.BlockSpec((1, rows // BLK, BLK), lambda i: (i, 0, 0))],
        out_shape=[out, out, jax.ShapeDtypeStruct((3, rows // BLK, BLK), jnp.float32)],
        scratch_shapes=[pltpu.VMEM((rows, depth), jnp.bfloat16), pltpu.SemaphoreType.DMA((len(cuts),))],
        compiler_params=pltpu.CompilerParams(
            dimension_semantics=("arbitrary",),
            vmem_limit_bytes=2 * rows * depth + 8 * depth * wide + 4 * 1024 * 1024,
        ),
        cost_estimate=pl.CostEstimate(
            flops=12 * rows * depth * wide, bytes_accessed=12 * depth * wide, transcendentals=0
        ),
        name="project",
    )(*arrays, own_w, other_w)


def cut_kernel(*refs):
    n = len(refs) // 2
    for source, out in zip(refs[:n], refs[n:]):
        out[...] = source[...]


def cut(arrays, cuts):
    wide = arrays[0].shape[1]
    return pl.pallas_call(
        cut_kernel,
        grid=(1,),
        in_specs=[pl.BlockSpec((count, wide), lambda i, first=first: (first, 0)) for first, count in cuts],
        out_specs=[pl.BlockSpec((count, wide), lambda i: (0, 0)) for _, count in cuts],
        out_shape=[jax.ShapeDtypeStruct((count, wide), jnp.bfloat16) for _, count in cuts],
        compiler_params=pltpu.CompilerParams(vmem_limit_bytes=10 * 1024 * 1024),
        cost_estimate=pl.CostEstimate(flops=10**5, bytes_accessed=3 * 10**6, transcendentals=0),
        name="cut_rows",
    )(*arrays)


def sources(refs):
    mine = lax.axis_index("sy")
    z, x, core = mine // 8, mine // 2 % 4, mine % 2
    at = 0
    for chunk, slots in enumerate(CHUNKS):
        for i in range(slots):
            dz, dx = SLOTS[at]
            chip = (z + dz) % 2 * 4 + (x + dx) % 4
            for other in range(2):
                n = chip * 2 + (core + other) % 2
                yield at * 2 + other, n, refs[chunk * 2 + other], pl.ds(i * BLK, BLK)
            at += 1


def payload_kernel(*refs):
    parts, out_ref, held = refs[:-2], refs[-2], refs[-1]
    mine = lax.axis_index("sy")
    z, x = mine // 8, mine // 2 % 4
    at = 0
    for part, slots in zip(parts, CHUNKS):
        for i in range(slots):
            dz, dx = SLOTS[at]
            chip = (z + dz) % 2 * 4 + (x + dx) % 4
            for kind in range(2):
                held[pl.ds(kind * 8 + chip, 1), :] = part[kind, i : i + 1, :]
            at += 1
    for i in range(out_ref.shape[0]):
        out_ref[i] = held[...]


def payload(parts):
    return pl.pallas_call(
        payload_kernel,
        grid=(1,),
        in_specs=[pl.BlockSpec(p.shape, lambda i: (0, 0, 0)) for p in parts],
        out_specs=pl.BlockSpec((NSY, 16, BLK), lambda i: (0, 0, 0)),
        out_shape=jax.ShapeDtypeStruct((NSY, 16, BLK), jnp.float32),
        scratch_shapes=[pltpu.VMEM((16, BLK), jnp.float32)],
        compiler_params=pltpu.CompilerParams(vmem_limit_bytes=4 * 1024 * 1024),
        name="square_sums",
    )(*parts)


def halo_kernel(
    fa, ga, fb, gb, fc, gc, ssq_ref, gk_ref, cos_lo, sin_lo, cos_hi, sin_hi,
    before_ref, after_ref, raw, sems,
):
    blocks = 2 * sum(CHUNKS)
    ends = ((lambda n: n >= blocks - ROUNDS, blocks - ROUNDS, 0), (lambda n: n < ROUNDS, 0, 1))

    def each(act):
        for at, n, ref, rows in sources((fa, ga, fb, gb, fc, gc)):
            for inside, first, head in ends:

                @pl.when(inside(n))
                def _(n=n, first=first, head=head, ref=ref, rows=rows, at=at):
                    to = pl.ds(pl.multiple_of((n - first) * BLK, BLK), BLK)
                    cols = pl.ds(head * HD, HD)
                    out = (before_ref, after_ref)[head]
                    act(pltpu.make_async_copy(ref.at[0, rows, cols], raw.at[head, to], sems.at[at, 0]))
                    act(pltpu.make_async_copy(ref.at[2, rows, cols], out.at[to, pl.ds(HD, HD)], sems.at[at, 1]))

    each(lambda copy: copy.start())
    each(lambda copy: copy.wait())
    for head, out, first, cosine, sine in (
        (0, before_ref, blocks - ROUNDS, cos_hi, sin_hi),
        (1, after_ref, 0, cos_lo, sin_lo),
    ):
        for i in range(ROUNDS):
            rows = pl.ds(i * BLK, BLK)
            out[rows, 0:HD] = norm_rope(
                raw[head, rows, :], inverse_norm(ssq_ref[pl.ds(first + i, 1), :]),
                gk_ref[:, head * HD : (head + 1) * HD],
                cosine[rows, :], sine[rows, :],
            )


def halo(features, ssq_k, gk, cosine, sine):
    rows = cosine.shape[0]
    low = pl.BlockSpec((HALO, HD), lambda i: (0, 0))
    high = pl.BlockSpec((HALO, HD), lambda i: (rows // HALO - 1, 0))
    one = lambda a: pl.BlockSpec(a.shape, lambda i: (0, 0))
    out = jax.ShapeDtypeStruct((HALO, 2 * HD), jnp.bfloat16)
    return pl.pallas_call(
        halo_kernel,
        grid=(1,),
        in_specs=[ANYWHERE] * 6 + [one(ssq_k), one(gk), low, low, high, high],
        out_specs=[pl.BlockSpec((HALO, 2 * HD), lambda i: (0, 0))] * 2,
        out_shape=[out, out],
        scratch_shapes=[
            pltpu.VMEM((2, HALO, HD), jnp.bfloat16),
            pltpu.SemaphoreType.DMA((2 * sum(CHUNKS), 2)),
        ],
        compiler_params=pltpu.CompilerParams(vmem_limit_bytes=16 * 1024 * 1024),
        cost_estimate=pl.CostEstimate(flops=10**9, bytes_accessed=10**4, transcendentals=0),
        name="halo_keys",
    )(*features, ssq_k, gk, cosine, sine, cosine, sine)


def attention_kernel(
    part, fa, ga, fb, gb, fc, gc, sk_ref, sq_ref, gk_ref, gq_ref, cos_ref, sin_ref, *rest
):
    out_ref, raw, kbuf, vbuf, sems = rest[-5:]
    step, head = pl.program_id(0), pl.program_id(1)
    blocks = 2 * sum(CHUNKS)
    columns = [slice(head * HD, (head + 1) * HD) for head in range(2)]
    own_first = (ROUNDS, 0)

    def guarded(condition, act):
        if condition is None:
            act()
        else:
            pl.when(condition)(act)

    @pl.when((step == 0) & (head == 0))
    def _():
        copies = []
        for at, n, ref, rows in sources((fa, ga, fb, gb, fc, gc)):
            to = pl.ds(pl.multiple_of(n * BLK, BLK), BLK)
            needed = None if part == 0 else (n < ROUNDS) | (n >= blocks - ROUNDS)
            copies.append((n, needed, pltpu.make_async_copy(ref.at[:, rows], raw.at[:, to], sems.at[at])))
        for _, needed, copy in copies:
            guarded(needed, copy.start)
        if part == 1:
            for head, ref in enumerate(rest[:2]):
                to = pl.ds((0, blocks)[head] * BLK, HALO)
                kbuf[head, to, :] = ref[:, 0:HD]
                vbuf[head, :, to] = ref[:, HD:].T
        for n, needed, copy in copies:
            guarded(needed, copy.wait)

        for n in range(blocks):
            heads = [head for head in range(2) if part == 0 or (n < ROUNDS, n >= blocks - ROUNDS)[head]]
            rows = slice(n * BLK, (n + 1) * BLK)
            inv = inverse_norm(sk_ref[n : n + 1, :]) if heads else None
            for head in heads:
                to = slice((n + own_first[head]) * BLK, (n + own_first[head] + 1) * BLK)
                kbuf[head, to, :] = norm_rope(
                    raw[0, rows, columns[head]], inv, gk_ref[:, columns[head]], cos_ref[rows, :], sin_ref[rows, :]
                )
                vbuf[head, :, to] = raw[2, rows, columns[head]].T

    def attend(first, head):
        def score(j):
            b = first + j
            rows = pl.ds(pl.multiple_of(b * BLK, BLK), BLK)
            window = pl.ds(pl.multiple_of(b * BLK, BLK), (ROUNDS + 1) * BLK)
            q = norm_rope(
                raw[1, rows, columns[head]], inverse_norm(sq_ref[pl.ds(b, 1), :]), gq_ref[:, columns[head]],
                cos_ref[rows, :], sin_ref[rows, :],
            )
            return lax.dot_general(
                kbuf[head, window, :], q, (((1,), (1,)), ((), ())), preferred_element_type=jnp.float32
            )

        def finish(j, scores):
            window = pl.ds(pl.multiple_of((first + j) * BLK, BLK), (ROUNDS + 1) * BLK)
            top = jnp.max(scores, axis=0, keepdims=True)
            weight = jnp.exp2((scores - top) * (SCALE * LOG2E))
            total = jnp.sum(weight, axis=0, keepdims=True)
            mixed = jnp.dot(
                vbuf[head, :, window], weight.astype(jnp.bfloat16), preferred_element_type=jnp.float32
            )
            out_ref[j, 0, 0:BLK, :] = (mixed * (1.0 / total)).T.astype(jnp.bfloat16)
            stats = split3(top * SCALE) + split3(total) + [jnp.zeros((EXTRA - 6, HD), jnp.float32)]
            out_ref[j, 0, BLK : BLK + EXTRA, :] = jnp.concatenate(stats, axis=0).astype(jnp.bfloat16)

        scores = [score(j) for j in range(PER_STEP)]
        for j in range(PER_STEP):
            finish(j, scores[j])
    for which in range(2):
        first = (step + 1 - which) * PER_STEP if part == 0 else (0, blocks - ROUNDS)[which]
        pl.when(head == which)(functools.partial(attend, first, which))


def attention(part, features, sk, sq, gk, gq, cosine, sine, before=None, after=None, held=None):
    rows = cosine.shape[0]
    blocks = rows // BLK
    whole = lambda a: pl.BlockSpec(a.shape, lambda i, h, n=a.ndim: (0,) * n)
    steps = blocks // PER_STEP - 1 if part == 0 else 1
    which = (lambda i, h: (i + 1 - h, h, 0, 0)) if part == 0 else (lambda i, h: (h * (blocks // PER_STEP - 1), h, 0, 0))
    small = (sk, sq, gk, gq, cosine, sine) + (() if held is None else (before, after))
    more = () if held is None else (held,)
    return pl.pallas_call(
        functools.partial(attention_kernel, part),
        grid=(steps, 2),
        in_specs=[ANYWHERE] * 6 + [whole(a) for a in small] + [ANYWHERE] * len(more),
        out_specs=pl.BlockSpec((PER_STEP, 1, BLK + EXTRA, HD), which),
        out_shape=jax.ShapeDtypeStruct((blocks, 2, BLK + EXTRA, HD), jnp.bfloat16),
        scratch_shapes=[
            pltpu.VMEM((3, rows, 2 * HD), jnp.bfloat16),
            pltpu.VMEM((2, rows + HALO, HD), jnp.bfloat16),
            pltpu.VMEM((2, HD, rows + HALO), jnp.bfloat16),
            pltpu.SemaphoreType.DMA((blocks,)),
        ],
        input_output_aliases={14: 0} if more else {},
        compiler_params=pltpu.CompilerParams(
            dimension_semantics=("arbitrary", "arbitrary"), vmem_limit_bytes=24 * 1024 * 1024
        ),
        cost_estimate=pl.CostEstimate(
            flops=(1 + 2 * (1 - part)) * 10**9, bytes_accessed=10**4, transcendentals=10**6
        ),
        name=("window_attention", "window_attention_halo")[part],
    )(*features, *small, *more)


def along_sx(block, distance):
    n = lax.axis_size("sx")
    return lax.ppermute(block, "sx", [((i - distance) % n, i) for i in range(n)])


def unpack_kernel(arrived_ref, attended_ref, best_ref, total_ref):
    classes, heads = arrived_ref.shape[:2]
    for c in range(classes):
        for h in range(heads):
            head = c * heads + h
            attended_ref[:, head * HD : (head + 1) * HD] = arrived_ref[c, h, 0:BLK, :]
            stats = arrived_ref[c, h, BLK : BLK + EXTRA, :].astype(jnp.float32)
            best_ref[head : head + 1, :] = (stats[0:1] + stats[1:2]) + stats[2:3]
            total_ref[head : head + 1, :] = (stats[3:4] + stats[4:5]) + stats[5:6]


def unpack(arrived):
    shapes = [
        jax.ShapeDtypeStruct((BLK, H * HD), jnp.bfloat16),
        jax.ShapeDtypeStruct((H, BLK), jnp.float32),
        jax.ShapeDtypeStruct((H, BLK), jnp.float32),
    ]
    return pl.pallas_call(
        unpack_kernel,
        grid=(1,),
        in_specs=[pl.BlockSpec(arrived.shape, lambda i: (0, 0, 0, 0))],
        out_specs=[pl.BlockSpec(a.shape, lambda i: (0, 0)) for a in shapes],
        out_shape=shapes,
        compiler_params=pltpu.CompilerParams(vmem_limit_bytes=16 * 1024 * 1024),
        name="unpack",
    )(arrived)


def body(tokens, mod_shift, mod_scale, w_query, w_key, w_value, query_gain, key_gain):
    group = lax.axis_index("sx")
    mine = lax.axis_index("sy")
    rows = BLK * lax.axis_size("sy")
    barrier = lax.optimization_barrier

    own = layer_norm(tokens, mod_shift, mod_scale)
    left, right, beside = from_left(own), from_right(own), from_z(own)
    key_w, query_w, value_w = barrier((w_key, w_query, w_value, own))[:3]
    one = barrier(jnp.bfloat16(1))
    sent_w = jnp.stack([key_w, query_w, value_w])
    own_w = sent_w * one
    cosine, sine = rope_tables(group * rows + jnp.arange(rows, dtype=jnp.int32))
    gq = lax.dynamic_slice(query_gain, (mine * 2 * HD,), (2 * HD,)).reshape(1, 2 * HD)
    gk = lax.dynamic_slice(key_gain, (mine * 2 * HD,), (2 * HD,)).reshape(1, 2 * HD)
    (left, right, beside), own_w, sent_w, (cosine, sine, gq, gk) = barrier(
        ((left, right, beside), own_w, sent_w, (cosine, sine, gq, gk))
    )

    far, z_right, z_left = from_left(left), from_right(beside), from_z(left)
    other_w = from_core(sent_w) * one
    near = project((own, left, right, beside), tuple((i, 0, BLK) for i in range(4)), own_w, other_w)
    near, far, z_right, z_left = barrier((near, far, z_right, z_left))

    part_left, part_right, part_z = cut((z_left, z_right, far), ((0, 48), (1, 48), (3, 32)))
    z_far = (from_left(part_left), from_right(part_right), from_z(part_z))
    middle = project((far, z_left, z_right), tuple((i, 0, BLK) for i in range(3)), own_w, other_w)
    z_far, middle = barrier((z_far, middle))
    last = project(z_far, tuple((i, 0, p.shape[0]) for i, p in enumerate(z_far)), own_w, other_w)

    features, parts = [], []
    for made, given, part in (near, middle, last):
        features += [made, from_core(given)]
        parts.append(part)
    sent = payload(parts)
    seen = lax.all_to_all(sent, "sy", split_axis=0, concat_axis=0, tiled=True)
    ssq = jnp.sum(seen.reshape(8, 2, 2, 8, BLK), axis=0).transpose(1, 2, 0, 3).reshape(2, 16, BLK)
    before, after = halo(features, ssq[0], gk, cosine, sine)
    common = (ssq[0], ssq[1], gk, gq, cosine, sine)
    out = attention(0, features, *common)
    before, after = along_sx(before, 1), along_sx(after, -1)
    out = attention(1, features, *common, before=before, after=after, held=out)
    arrived = lax.all_to_all(out, "sy", split_axis=0, concat_axis=0, tiled=True)
    return unpack(arrived)


def solution(mesh):
    placed = (
        P(("sx", "sy"), None),
        P(),
        P(),
        P(None, "sy"),
        P(None, "sy"),
        P(None, "sy"),
        P(),
        P(),
    )
    return jax.shard_map(
        body,
        mesh=mesh,
        in_specs=placed,
        out_specs=(P(("sx", "sy"), None), P(None, ("sx", "sy")), P(None, ("sx", "sy"))),
        check_vma=False,
    )
```

```python
import functools

import jax
import jax.numpy as jnp
import numpy as np
from jax import lax
from jax.experimental import pallas as pl
from jax.experimental.pallas import tpu as pltpu
from jax.sharding import PartitionSpec as P

H = 32
HD = 128
ROUNDS = 4
GRID_W = 80
GRID_H = 45
BLK = 128
HALO = ROUNDS * BLK
EXTRA = 8
NSY = 16
SCALE = np.float32(1.0) / np.sqrt(np.float32(HD))
LOG2E = np.float32(1.4426950408889634)


def layer_norm_kernel(tokens_ref, shift_ref, scale_ref, out_ref):
    wide = tokens_ref[...].astype(jnp.float32)
    center = jnp.mean(wide, axis=-1, keepdims=True)
    apart = wide - center
    spread = jnp.mean(apart * apart, axis=-1, keepdims=True)
    scaled = apart * lax.rsqrt(spread + 1e-06)
    out_ref[...] = (scaled * (1.0 + scale_ref[...]) + shift_ref[...]).astype(jnp.bfloat16)


def layer_norm(values, mod_shift, mod_scale):
    rows, wide = values.shape
    block = pl.BlockSpec((64, wide), lambda i: (i, 0))
    vector = pl.BlockSpec((1, wide), lambda i: (0, 0))
    return pl.pallas_call(
        layer_norm_kernel,
        grid=(rows // 64,),
        in_specs=[block, vector, vector],
        out_specs=block,
        out_shape=jax.ShapeDtypeStruct((rows, wide), jnp.bfloat16),
        compiler_params=pltpu.CompilerParams(vmem_limit_bytes=60 * 1024 * 1024),
        cost_estimate=pl.CostEstimate(flops=10 * rows * wide, bytes_accessed=4 * rows * wide, transcendentals=rows),
        name="layer_norm",
    )(values, mod_shift.reshape(1, wide), mod_scale.reshape(1, wide))


def rope_tables(positions):
    small_pairs = HD // 6
    time_pairs = (HD - 4 * small_pairs) // 2
    frame = (positions // (GRID_H * GRID_W)).astype(jnp.float32)
    row_pos = (positions // GRID_W % GRID_H).astype(jnp.float32)
    col_pos = (positions % GRID_W).astype(jnp.float32)
    time_freq = 10000.0 ** (-jnp.arange(time_pairs, dtype=jnp.float32) / time_pairs)
    space_freq = 10000.0 ** (-jnp.arange(small_pairs, dtype=jnp.float32) / small_pairs)
    freq = jnp.repeat(jnp.concatenate([time_freq, space_freq, space_freq]), 2)
    pair = jnp.arange(HD, dtype=jnp.int32) // 2
    where = jnp.where(
        pair < time_pairs,
        frame[:, None],
        jnp.where(pair < time_pairs + small_pairs, row_pos[:, None], col_pos[:, None]),
    )
    angles = where * freq
    sign = jnp.where(jnp.arange(HD) % 2 == 0, -1.0, 1.0).astype(jnp.float32)
    return jnp.cos(angles), jnp.sin(angles) * sign


def as_column(row):
    return jnp.broadcast_to(row, (BLK, BLK)).T


def as_row(column):
    return jnp.broadcast_to(column, (BLK, BLK)).T[0:1, :]


def inverse_norm(ssq_row):
    return as_column(lax.rsqrt(ssq_row * (1.0 / (H * HD)) + 1e-06))


def norm_rope(raw, inv, gain, cosine, sine):
    wide = raw.astype(jnp.float32) * inv * gain
    lane = lax.broadcasted_iota(jnp.int32, wide.shape, 1)
    partner = jnp.where(
        lane % 2 == 0, pltpu.roll(wide, HD - 1, 1), pltpu.roll(wide, 1, 1)
    )
    return (wide * cosine + partner * sine).astype(jnp.bfloat16)


def split3(row):
    hi = row.astype(jnp.bfloat16).astype(jnp.float32)
    rest = row - hi
    mid = rest.astype(jnp.bfloat16).astype(jnp.float32)
    return [hi, mid, rest - mid]


PER_STEP = 4
SLOTS = ((0, 0), (0, -1), (0, 1), (1, 0), (0, 2), (1, -1), (1, 1), (1, 2))
CHUNKS = (4, 3, 1)


def chip_move(dz, dx, dc):
    return [
        (z * 8 + x * 2 + c, (z + dz) % 2 * 8 + (x + dx) % 4 * 2 + (c + dc) % 2)
        for z in range(2)
        for x in range(4)
        for c in range(2)
    ]


def from_left(block):
    return lax.ppermute(block, "sy", chip_move(0, 1, 0))


def from_right(block):
    return lax.ppermute(block, "sy", chip_move(0, -1, 0))


def from_z(block):
    return lax.ppermute(block, "sy", chip_move(1, 0, 0))


def from_core(block):
    return lax.ppermute(block, "sy", chip_move(0, 0, 1))


ANYWHERE = pl.BlockSpec(memory_space=pltpu.HBM)


def project_kernel(cuts, *refs):
    n = len(refs) - 7
    arrays, (own_w, other_w, own_ref, other_ref, ssq_ref, x_ref, sems) = refs[:n], refs[n:]

    @pl.when(pl.program_id(0) == 0)
    def _():
        copies, at = [], 0
        for i, (which, first, count) in enumerate(cuts):
            source = arrays[which].at[pl.ds(first, count)]
            copies.append(pltpu.make_async_copy(source, x_ref.at[pl.ds(at, count)], sems.at[i]))
            copies[-1].start()
            at += count
        for copy in copies:
            copy.wait()

    total = None
    for weight, out in ((own_w, own_ref), (other_w, other_ref)):
        made = jnp.dot(x_ref[...], weight[pl.program_id(0)], preferred_element_type=jnp.float32).astype(jnp.bfloat16)
        out[0] = made
        wide = made.astype(jnp.float32)
        part = jnp.sum(wide * wide, axis=-1, keepdims=True)
        total = part if total is None else total + part
    for i in range(x_ref.shape[0] // BLK):
        ssq_ref[0, i : i + 1, :] = as_row(total[i * BLK : (i + 1) * BLK])


def project(arrays, cuts, own_w, other_w):
    rows = sum(count for _, _, count in cuts)
    depth, wide = own_w.shape[1:]
    w_spec = pl.BlockSpec(memory_space=pltpu.VMEM)
    o_spec = pl.BlockSpec((1, rows, wide), lambda i: (i, 0, 0))
    out = jax.ShapeDtypeStruct((3, rows, wide), jnp.bfloat16)
    return pl.pallas_call(
        functools.partial(project_kernel, cuts),
        grid=(3,),
        in_specs=[ANYWHERE] * len(arrays) + [w_spec, w_spec],
        out_specs=[o_spec, o_spec, pl.BlockSpec((1, rows // BLK, BLK), lambda i: (i, 0, 0))],
        out_shape=[out, out, jax.ShapeDtypeStruct((3, rows // BLK, BLK), jnp.float32)],
        scratch_shapes=[pltpu.VMEM((rows, depth), jnp.bfloat16), pltpu.SemaphoreType.DMA((len(cuts),))],
        compiler_params=pltpu.CompilerParams(
            dimension_semantics=("arbitrary",),
            vmem_limit_bytes=2 * rows * depth + 6 * 1024 * 1024,
        ),
        cost_estimate=pl.CostEstimate(
            flops=12 * rows * depth * wide, bytes_accessed=12 * depth * wide, transcendentals=0
        ),
        name="project",
    )(*arrays, own_w, other_w)


def cut_kernel(*refs):
    n = len(refs) // 2
    for source, out in zip(refs[:n], refs[n:]):
        out[...] = source[...]


def cut(arrays, cuts):
    wide = arrays[0].shape[1]
    return pl.pallas_call(
        cut_kernel,
        grid=(1,),
        in_specs=[pl.BlockSpec((count, wide), lambda i, first=first: (first, 0)) for first, count in cuts],
        out_specs=[pl.BlockSpec((count, wide), lambda i: (0, 0)) for _, count in cuts],
        out_shape=[jax.ShapeDtypeStruct((count, wide), jnp.bfloat16) for _, count in cuts],
        compiler_params=pltpu.CompilerParams(vmem_limit_bytes=10 * 1024 * 1024),
        cost_estimate=pl.CostEstimate(flops=10**5, bytes_accessed=3 * 10**6, transcendentals=0),
        name="cut_rows",
    )(*arrays)


def sources(refs):
    mine = lax.axis_index("sy")
    z, x, core = mine // 8, mine // 2 % 4, mine % 2
    at = 0
    for chunk, slots in enumerate(CHUNKS):
        for i in range(slots):
            dz, dx = SLOTS[at]
            chip = (z + dz) % 2 * 4 + (x + dx) % 4
            for other in range(2):
                n = chip * 2 + (core + other) % 2
                yield at * 2 + other, n, refs[chunk * 2 + other], pl.ds(i * BLK, BLK)
            at += 1


def payload_kernel(*refs):
    parts, out_ref, held = refs[:-2], refs[-2], refs[-1]
    mine = lax.axis_index("sy")
    z, x = mine // 8, mine // 2 % 4
    at = 0
    for part, slots in zip(parts, CHUNKS):
        for i in range(slots):
            dz, dx = SLOTS[at]
            chip = (z + dz) % 2 * 4 + (x + dx) % 4
            for kind in range(2):
                held[pl.ds(kind * 8 + chip, 1), :] = part[kind, i : i + 1, :]
            at += 1
    for i in range(out_ref.shape[0]):
        out_ref[i] = held[...]


def payload(parts):
    return pl.pallas_call(
        payload_kernel,
        grid=(1,),
        in_specs=[pl.BlockSpec(p.shape, lambda i: (0, 0, 0)) for p in parts],
        out_specs=pl.BlockSpec((NSY, 16, BLK), lambda i: (0, 0, 0)),
        out_shape=jax.ShapeDtypeStruct((NSY, 16, BLK), jnp.float32),
        scratch_shapes=[pltpu.VMEM((16, BLK), jnp.float32)],
        compiler_params=pltpu.CompilerParams(vmem_limit_bytes=4 * 1024 * 1024),
        name="square_sums",
    )(*parts)


def halo_kernel(
    fa, ga, fb, gb, fc, gc, ssq_ref, gk_ref, cos_lo, sin_lo, cos_hi, sin_hi,
    before_ref, after_ref, raw, sems,
):
    blocks = 2 * sum(CHUNKS)
    ends = ((lambda n: n >= blocks - ROUNDS, blocks - ROUNDS, 0), (lambda n: n < ROUNDS, 0, 1))

    def each(act):
        for at, n, ref, rows in sources((fa, ga, fb, gb, fc, gc)):
            for inside, first, head in ends:

                @pl.when(inside(n))
                def _(n=n, first=first, head=head, ref=ref, rows=rows, at=at):
                    to = pl.ds(pl.multiple_of((n - first) * BLK, BLK), BLK)
                    cols = pl.ds(head * HD, HD)
                    out = (before_ref, after_ref)[head]
                    act(pltpu.make_async_copy(ref.at[0, rows, cols], raw.at[head, to], sems.at[at, 0]))
                    act(pltpu.make_async_copy(ref.at[2, rows, cols], out.at[to, pl.ds(HD, HD)], sems.at[at, 1]))

    each(lambda copy: copy.start())
    each(lambda copy: copy.wait())
    for head, out, first, cosine, sine in (
        (0, before_ref, blocks - ROUNDS, cos_hi, sin_hi),
        (1, after_ref, 0, cos_lo, sin_lo),
    ):
        for i in range(ROUNDS):
            rows = pl.ds(i * BLK, BLK)
            out[rows, 0:HD] = norm_rope(
                raw[head, rows, :], inverse_norm(ssq_ref[pl.ds(first + i, 1), :]),
                gk_ref[:, head * HD : (head + 1) * HD],
                cosine[rows, :], sine[rows, :],
            )


def halo(features, ssq_k, gk, cosine, sine):
    rows = cosine.shape[0]
    low = pl.BlockSpec((HALO, HD), lambda i: (0, 0))
    high = pl.BlockSpec((HALO, HD), lambda i: (rows // HALO - 1, 0))
    one = lambda a: pl.BlockSpec(a.shape, lambda i: (0, 0))
    out = jax.ShapeDtypeStruct((HALO, 2 * HD), jnp.bfloat16)
    return pl.pallas_call(
        halo_kernel,
        grid=(1,),
        in_specs=[ANYWHERE] * 6 + [one(ssq_k), one(gk), low, low, high, high],
        out_specs=[pl.BlockSpec((HALO, 2 * HD), lambda i: (0, 0))] * 2,
        out_shape=[out, out],
        scratch_shapes=[
            pltpu.VMEM((2, HALO, HD), jnp.bfloat16),
            pltpu.SemaphoreType.DMA((2 * sum(CHUNKS), 2)),
        ],
        compiler_params=pltpu.CompilerParams(vmem_limit_bytes=16 * 1024 * 1024),
        cost_estimate=pl.CostEstimate(flops=10**9, bytes_accessed=10**4, transcendentals=0),
        name="halo_keys",
    )(*features, ssq_k, gk, cosine, sine, cosine, sine)


def attention_kernel(
    part, fa, ga, fb, gb, fc, gc, sk_ref, sq_ref, gk_ref, gq_ref, cos_ref, sin_ref, *rest
):
    out_ref, raw, kbuf, vbuf, sems = rest[-5:]
    step, head = pl.program_id(0), pl.program_id(1)
    blocks = 2 * sum(CHUNKS)
    columns = [slice(head * HD, (head + 1) * HD) for head in range(2)]
    own_first = (ROUNDS, 0)

    def guarded(condition, act):
        if condition is None:
            act()
        else:
            pl.when(condition)(act)

    @pl.when((step == 0) & (head == 0))
    def _():
        copies = []
        for at, n, ref, rows in sources((fa, ga, fb, gb, fc, gc)):
            to = pl.ds(pl.multiple_of(n * BLK, BLK), BLK)
            needed = None if part == 0 else (n < ROUNDS) | (n >= blocks - ROUNDS)
            copies.append((n, needed, pltpu.make_async_copy(ref.at[:, rows], raw.at[:, to], sems.at[at])))
        for _, needed, copy in copies:
            guarded(needed, copy.start)
        if part == 1:
            for head, ref in enumerate(rest[:2]):
                to = pl.ds((0, blocks)[head] * BLK, HALO)
                kbuf[head, to, :] = ref[:, 0:HD]
                vbuf[head, :, to] = ref[:, HD:].T
        for n, needed, copy in copies:
            guarded(needed, copy.wait)

        for n in range(blocks):
            heads = [head for head in range(2) if part == 0 or (n < ROUNDS, n >= blocks - ROUNDS)[head]]
            rows = slice(n * BLK, (n + 1) * BLK)
            inv = inverse_norm(sk_ref[n : n + 1, :]) if heads else None
            for head in heads:
                to = slice((n + own_first[head]) * BLK, (n + own_first[head] + 1) * BLK)
                kbuf[head, to, :] = norm_rope(
                    raw[0, rows, columns[head]], inv, gk_ref[:, columns[head]], cos_ref[rows, :], sin_ref[rows, :]
                )
                vbuf[head, :, to] = raw[2, rows, columns[head]].T

    def attend(first, head):
        def score(j):
            b = first + j
            rows = pl.ds(pl.multiple_of(b * BLK, BLK), BLK)
            window = pl.ds(pl.multiple_of(b * BLK, BLK), (ROUNDS + 1) * BLK)
            q = norm_rope(
                raw[1, rows, columns[head]], inverse_norm(sq_ref[pl.ds(b, 1), :]), gq_ref[:, columns[head]],
                cos_ref[rows, :], sin_ref[rows, :],
            )
            return lax.dot_general(
                kbuf[head, window, :], q, (((1,), (1,)), ((), ())), preferred_element_type=jnp.float32
            )

        def finish(j, scores):
            window = pl.ds(pl.multiple_of((first + j) * BLK, BLK), (ROUNDS + 1) * BLK)
            top = jnp.max(scores, axis=0, keepdims=True)
            weight = jnp.exp2((scores - top) * (SCALE * LOG2E))
            total = jnp.sum(weight, axis=0, keepdims=True)
            mixed = jnp.dot(
                vbuf[head, :, window], weight.astype(jnp.bfloat16), preferred_element_type=jnp.float32
            )
            out_ref[j, 0, 0:BLK, :] = (mixed / total).T.astype(jnp.bfloat16)
            stats = split3(top * SCALE) + split3(total) + [jnp.zeros((EXTRA - 6, HD), jnp.float32)]
            out_ref[j, 0, BLK : BLK + EXTRA, :] = jnp.concatenate(stats, axis=0).astype(jnp.bfloat16)

        scores = [score(j) for j in range(PER_STEP)]
        for j in range(PER_STEP):
            finish(j, scores[j])
    for which in range(2):
        first = (step + 1 - which) * PER_STEP if part == 0 else (0, blocks - ROUNDS)[which]
        pl.when(head == which)(functools.partial(attend, first, which))


def attention(part, features, sk, sq, gk, gq, cosine, sine, before=None, after=None, held=None):
    rows = cosine.shape[0]
    blocks = rows // BLK
    whole = lambda a: pl.BlockSpec(a.shape, lambda i, h, n=a.ndim: (0,) * n)
    steps = blocks // PER_STEP - 1 if part == 0 else 1
    which = (lambda i, h: (i + 1 - h, h, 0, 0)) if part == 0 else (lambda i, h: (h * (blocks // PER_STEP - 1), h, 0, 0))
    small = (sk, sq, gk, gq, cosine, sine) + (() if held is None else (before, after))
    more = () if held is None else (held,)
    return pl.pallas_call(
        functools.partial(attention_kernel, part),
        grid=(steps, 2),
        in_specs=[ANYWHERE] * 6 + [whole(a) for a in small] + [ANYWHERE] * len(more),
        out_specs=pl.BlockSpec((PER_STEP, 1, BLK + EXTRA, HD), which),
        out_shape=jax.ShapeDtypeStruct((blocks, 2, BLK + EXTRA, HD), jnp.bfloat16),
        scratch_shapes=[
            pltpu.VMEM((3, rows, 2 * HD), jnp.bfloat16),
            pltpu.VMEM((2, rows + HALO, HD), jnp.bfloat16),
            pltpu.VMEM((2, HD, rows + HALO), jnp.bfloat16),
            pltpu.SemaphoreType.DMA((blocks,)),
        ],
        input_output_aliases={14: 0} if more else {},
        compiler_params=pltpu.CompilerParams(
            dimension_semantics=("arbitrary", "arbitrary"), vmem_limit_bytes=24 * 1024 * 1024
        ),
        cost_estimate=pl.CostEstimate(
            flops=(1 + 2 * (1 - part)) * 10**9, bytes_accessed=10**4, transcendentals=10**6
        ),
        name=("window_attention", "window_attention_halo")[part],
    )(*features, *small, *more)


def along_sx(block, distance):
    n = lax.axis_size("sx")
    return lax.ppermute(block, "sx", [((i - distance) % n, i) for i in range(n)])


def unpack_kernel(arrived_ref, attended_ref, best_ref, total_ref):
    classes, heads = arrived_ref.shape[:2]
    for c in range(classes):
        for h in range(heads):
            head = c * heads + h
            attended_ref[:, head * HD : (head + 1) * HD] = arrived_ref[c, h, 0:BLK, :]
            stats = arrived_ref[c, h, BLK : BLK + EXTRA, :].astype(jnp.float32)
            best_ref[head : head + 1, :] = (stats[0:1] + stats[1:2]) + stats[2:3]
            total_ref[head : head + 1, :] = (stats[3:4] + stats[4:5]) + stats[5:6]


def unpack(arrived):
    shapes = [
        jax.ShapeDtypeStruct((BLK, H * HD), jnp.bfloat16),
        jax.ShapeDtypeStruct((H, BLK), jnp.float32),
        jax.ShapeDtypeStruct((H, BLK), jnp.float32),
    ]
    return pl.pallas_call(
        unpack_kernel,
        grid=(1,),
        in_specs=[pl.BlockSpec(arrived.shape, lambda i: (0, 0, 0, 0))],
        out_specs=[pl.BlockSpec(a.shape, lambda i: (0, 0)) for a in shapes],
        out_shape=shapes,
        compiler_params=pltpu.CompilerParams(vmem_limit_bytes=16 * 1024 * 1024),
        name="unpack",
    )(arrived)


def body(tokens, mod_shift, mod_scale, w_query, w_key, w_value, query_gain, key_gain):
    group = lax.axis_index("sx")
    mine = lax.axis_index("sy")
    rows = BLK * lax.axis_size("sy")
    barrier = lax.optimization_barrier

    own = layer_norm(tokens, mod_shift, mod_scale)
    left, right, beside = from_left(own), from_right(own), from_z(own)
    key_w, query_w, value_w = barrier((w_key, w_query, w_value, own))[:3]
    one = barrier(jnp.bfloat16(1))
    sent_w = jnp.stack([key_w, query_w, value_w])
    own_w = sent_w * one
    cosine, sine = rope_tables(group * rows + jnp.arange(rows, dtype=jnp.int32))
    gq = lax.dynamic_slice(query_gain, (mine * 2 * HD,), (2 * HD,)).reshape(1, 2 * HD)
    gk = lax.dynamic_slice(key_gain, (mine * 2 * HD,), (2 * HD,)).reshape(1, 2 * HD)
    (left, right, beside), own_w, sent_w, (cosine, sine, gq, gk) = barrier(
        ((left, right, beside), own_w, sent_w, (cosine, sine, gq, gk))
    )

    far, z_right, z_left = from_left(left), from_right(beside), from_z(left)
    other_w = from_core(sent_w) * one
    near = project((own, left, right, beside), tuple((i, 0, BLK) for i in range(4)), own_w, other_w)
    near, far, z_right, z_left = barrier((near, far, z_right, z_left))

    part_left, part_right, part_z = cut((z_left, z_right, far), ((0, 48), (1, 48), (3, 32)))
    z_far = (from_left(part_left), from_right(part_right), from_z(part_z))
    middle = project((far, z_left, z_right), tuple((i, 0, BLK) for i in range(3)), own_w, other_w)
    z_far, middle = barrier((z_far, middle))
    last = project(z_far, tuple((i, 0, p.shape[0]) for i, p in enumerate(z_far)), own_w, other_w)

    features, parts = [], []
    for made, given, part in (near, middle, last):
        features += [made, from_core(given)]
        parts.append(part)
    sent = payload(parts)
    seen = lax.all_to_all(sent, "sy", split_axis=0, concat_axis=0, tiled=True)
    ssq = jnp.sum(seen.reshape(8, 2, 2, 8, BLK), axis=0).transpose(1, 2, 0, 3).reshape(2, 16, BLK)
    before, after = halo(features, ssq[0], gk, cosine, sine)
    common = (ssq[0], ssq[1], gk, gq, cosine, sine)
    out = attention(0, features, *common)
    before, after = along_sx(before, 1), along_sx(after, -1)
    out = attention(1, features, *common, before=before, after=after, held=out)
    arrived = lax.all_to_all(out, "sy", split_axis=0, concat_axis=0, tiled=True)
    return unpack(arrived)


def solution(mesh):
    placed = (
        P(("sx", "sy"), None),
        P(),
        P(),
        P(None, "sy"),
        P(None, "sy"),
        P(None, "sy"),
        P(),
        P(),
    )
    return jax.shard_map(
        body,
        mesh=mesh,
        in_specs=placed,
        out_specs=(P(("sx", "sy"), None), P(None, ("sx", "sy")), P(None, ("sx", "sy"))),
        check_vma=False,
    )
```
